32 devices in a mesh: dp: 8 (over z, x), mp: 4 (over y, core).
Axes of the slice: x: 2, y: 2, z: 4, core: 2. Of those that a mesh axis runs over, the one named last changes fastest.
Arguments:
- inputs: bfloat16 [8192, 768], P(('dp', 'mp')), may hold values from -6 to 6
- query_key_value: bfloat16 [768, 3, 768], P('dp', None, 'mp'), may hold values from -0.21875 to 0.21875
- output_weight: bfloat16 [768, 768], P('mp', 'dp'), may hold values from -3.5 to 3.5
- expert_input: bfloat16 [8, 2, 768, 2048], P(None, None, 'dp', 'mp'), may hold values from -0.21875 to 0.21875
- expert_output: bfloat16 [8, 2048, 768], P(None, 'mp', 'dp'), may hold values from -0.25 to 0.25
- first_gain: bfloat16 [768], replicated, may hold values from 0.5 to 1.5
- second_gain: bfloat16 [768], replicated, may hold values from 0.5 to 1.5
- router_weight: bfloat16 [768, 12], replicated, may hold values from -0.21875 to 0.21875
- logit_carry: float32 [12, 12], replicated, may hold values from -1.75 to 1.75
- constant_mix: bfloat16 [768, 4], replicated, may hold values from -0.21875 to 0.21875
- constant_values: bfloat16 [2, 768], replicated, may hold values from -6 to 6
- previous_logits: float32 [8192, 12], P('dp'), may hold values from -6 to 6
- routes: int32 [8192, 2], P('dp'), may hold values from 0 to 11, all different within a row; in each aligned block of 1024 rows (0 to 1023, 1024 to 2047, ...) at most 256 rows name the same one
- cotangent: bfloat16 [8192, 768], P(('dp', 'mp')), may hold values from -6 to 6
Outputs:
- output: bfloat16 [8192, 768], P(('dp', 'mp'))
- input_grad: float32 [8192, 768], P(('dp', 'mp'))
- logits_grad: float32 [8192, 12], P(('dp', 'mp'))
- query_key_value_grad: float32 [768, 3, 768], P('dp', None, 'mp')
- output_weight_grad: float32 [768, 768], P('mp', 'dp')
- expert_input_grad: float32 [8, 2, 768, 2048], P(None, None, 'dp', 'mp')
- expert_output_grad: float32 [8, 2048, 768], P(None, 'mp', 'dp')
- first_gain_grad: float32 [768], replicated
- second_gain_grad: float32 [768], replicated
- router_grad: float32 [768, 12], replicated
- logit_carry_grad: float32 [12, 12], replicated
- constant_mix_grad: float32 [768, 4], replicated
- constant_values_grad: float32 [2, 768], replicated
The draws below stay inside these ranges and needn't reach their ends.
Inputs may be any that keep to these rules, and one draw needn't show every extreme that they name: `routes`: each row names two different experts. Among the tokens of one index of dp no expert is named by more than 256 rows, a bound that some block reaches.
All inputs are finite; a program needn't handle non-finite values.
Results may differ from the reference program's by a relative error of at most 0.015.
Values may be sent and summed in bfloat16 or wider, within the bound.
A program may use at most 256 MiB of HBM per device.

```python
import math
import jax
import jax.numpy as jnp
import numpy as np
from jax import lax

D = 768
HEADS = 12
HD = 64
FF = 2048
NFFN = 8
NEXP = 12
SEQ = 1024
SEQ_GRP = 1
GROUP = 1024
CAP = 256
TOKENS = 8192
N_DP = 8


def levels(rng, dims, split, smallest, top_value):
    level, own = 1.0, jax.random.fold_in(rng, 6)
    for dim, parts in split:
        steps = jnp.exp(jax.random.uniform(jax.random.fold_in(own, dim), (parts,), jnp.float32, smallest / len(split), top_value / len(split)))
        level = level * jnp.repeat(steps, dims[dim] // parts).reshape([-1 if axis == dim else 1 for axis in range(len(dims))])
    return level


def routed_block(stream_key, own, number, rows, number_of, top, reach, slope):
    ranking = jax.random.permutation(stream_key, number_of)
    packed, ordinary = load_shares(number_of, rows * top, reach, slope, True), load_shares(number_of, rows * top, reach, slope, False)
    places = jnp.arange(number_of)

    def named(lengths, turn):
        used = int((lengths > 0).sum())
        fixed = max(1, used // 4)
        shifted = fixed + (places - fixed + turn * (used - fixed)) % max(1, number_of - fixed)
        return jnp.zeros((number_of,), jnp.int32).at[ranking[jnp.where(places < fixed, places, shifted)]].set(jnp.asarray(lengths, jnp.int32))

    lengths = jnp.where(number % 4 == 0, named(packed, number // 4), named(ordinary, number - number // 4 - 1))
    mixed = jax.random.permutation(jax.random.fold_in(own, 3), number_of)
    giver, sink = mixed[0:number_of // 2 * 2:2], mixed[1:number_of // 2 * 2:2]
    margin = jnp.minimum(lengths[giver] - 1, reach - lengths[sink]) // 2
    margin = jnp.where((giver == ranking[0]) | (sink == ranking[0]) | (lengths[sink] == 0), 0, jnp.maximum(margin, 0))
    shifted = jax.random.randint(jax.random.fold_in(own, 4), (number_of // 2,), 0, 1 << 20) % (margin + 1)
    lengths = lengths.at[giver].add(-shifted).at[sink].add(shifted)
    labels = jnp.searchsorted(jnp.cumsum(lengths), jnp.arange(rows * top), side="right").astype(jnp.int32)
    grid = labels.reshape(top, rows).T
    grid = grid[jax.random.permutation(jax.random.fold_in(own, 1), rows)]
    turn = jax.random.randint(jax.random.fold_in(own, 2), (rows, 1), 0, top)
    return jnp.take_along_axis(grid, (jnp.arange(top)[None, :] + turn) % top, axis=1)


def load_shares(amount, total, limit, skew, full):
    portions = [(1 << 20) // math.isqrt(grade ** skew) + 1 for grade in range(1, amount + 1)]
    largest = limit if full else min(limit, max(-(-total // amount), total * portions[0] // sum(portions)))
    least = 1 if total - largest >= amount - 1 else 0
    counts, surplus = [largest] + [least] * (amount - 1), total - largest - least * (amount - 1)
    while surplus > 0:
        candidates = [i for i in range(1, amount) if counts[i] < largest] or [i for i in range(1, amount) if counts[i] < limit]
        mass, left = sum([portions[i] for i in candidates]), surplus
        for i in candidates:
            extra = min(limit - counts[i], max(1, left * portions[i] // mass), surplus)
            counts[i] = counts[i] + extra
            surplus = surplus - extra
    return np.array(counts)


def centred(stream_key, shape, width, bound, split=(), held_as=jnp.bfloat16):
    level = levels(stream_key, shape, split, -0.22, 0.18) if split else 1.0
    result = jax.random.normal(stream_key, shape, jnp.float32) * width * level
    return jnp.minimum(jnp.maximum(result, -bound), bound).astype(held_as)


def setup_inputs(seed: int = 0) -> dict:
    streams_of = jax.random.split(jax.random.key(seed), 15)
    inputs = centred(streams_of[0], (TOKENS, D), 1.0, 6.0, ((0, 32),))
    query_key_value = centred(streams_of[1], (D, 3, D), D ** -0.5, 0.21875, ((0, 8), (2, 4)))
    output_weight = centred(streams_of[2], (D, D), (max(1, 4 * D // SEQ)) ** -0.5, 3.5, ((0, 4), (1, 8)))
    expert_input = centred(streams_of[3], (NFFN, 2, D, FF), D ** -0.5, 0.21875, ((2, 8), (3, 4)))
    expert_output = centred(streams_of[4], (NFFN, FF, D), (FF // 4) ** -0.5, 0.25, ((1, 4), (2, 8)))
    first_gain = jnp.clip(1.0 + 0.1 * jax.random.normal(streams_of[5], (D,), jnp.float32), 0.5, 1.5).astype(jnp.bfloat16)
    second_gain = jnp.clip(1.0 + 0.1 * jax.random.normal(streams_of[6], (D,), jnp.float32), 0.5, 1.5).astype(jnp.bfloat16)
    router_weight = centred(streams_of[7], (D, NEXP), D ** -0.5, 0.21875)
    logit_carry = centred(streams_of[8], (NEXP, NEXP), NEXP ** -0.5, 1.75, (), jnp.float32)
    constant_mix = centred(streams_of[9], (D, 4), D ** -0.5, 0.21875)
    constant_values = centred(streams_of[10], (2, D), 1.0, 6.0)
    previous_logits = centred(streams_of[11], (TOKENS, NEXP), 1.0, 6.0, ((0, 8),), jnp.float32)
    routes_keys = jax.random.split(jax.random.fold_in(streams_of[12], 1), TOKENS // GROUP)
    routes_turns = jax.random.permutation(jax.random.fold_in(streams_of[12], 3), TOKENS // GROUP)
    routes = jax.vmap(lambda own, number: routed_block(jax.random.fold_in(streams_of[12], 2), own, number, GROUP, NEXP, 2, CAP, 2))(routes_keys, routes_turns).reshape((TOKENS, 2))
    cotangent = centred(streams_of[13], (TOKENS, D), 1.0, 6.0, ((0, 32),))
    return dict(inputs=inputs, query_key_value=query_key_value, output_weight=output_weight, expert_input=expert_input, expert_output=expert_output, first_gain=first_gain, second_gain=second_gain, router_weight=router_weight, logit_carry=logit_carry, constant_mix=constant_mix, constant_values=constant_values, previous_logits=previous_logits, routes=routes, cotangent=cotangent)


@jax.custom_vjp
def low(v):
    return lax.optimization_barrier(v.astype(jnp.bfloat16)).astype(jnp.float32)

@jax.custom_vjp
def low_back(v):
    return v

def low_keep(v):
    return (low(v), None)

def low_pass(kept, grad):
    return (grad,)

def back_keep(v):
    return (v, None)

def back_low(kept, grad):
    return (low(grad),)
low.defvjp(low_keep, low_pass)
low_back.defvjp(back_keep, back_low)
epsilon = 1e-06
rope_base = 10000.0
highest = lax.Precision.HIGHEST

def rms_norm(values, gain):
    norm_scale = lax.rsqrt(lax.optimization_barrier(jnp.mean(values * values, axis=-1, keepdims=True)) + epsilon)
    return values * norm_scale * gain

def rope_tables(length, period, half):
    positions = (jnp.arange(length, dtype=jnp.int32) % period).astype(jnp.float32)
    frequency = rope_base ** (-jnp.arange(half, dtype=jnp.float32) / half)
    angles = positions[:, None] * frequency[None, :]
    return (jnp.cos(angles), jnp.sin(angles))

def rotate(values, cosine, sine_table):
    half = values.shape[-1] // 2
    front_half = values[..., :half]
    back_half = values[..., half:]
    cosine = cosine[:, None, :]
    sine_table = sine_table[:, None, :]
    return jnp.concatenate([front_half * cosine - back_half * sine_table, back_half * cosine + front_half * sine_table], axis=-1)

def dispatch_tables(route_rows, experts, capacity):
    row_count = route_rows.shape[0]
    flat_routes = route_rows.reshape(-1)
    onehot = (flat_routes[:, None] == jnp.arange(experts, dtype=jnp.int32)[None, :]).astype(jnp.int32)
    before = jnp.cumsum(onehot, axis=0) - onehot
    position = lax.optimization_barrier(jnp.sum(before * onehot, axis=1))
    target = jnp.where(flat_routes < experts, flat_routes * capacity + position, experts * capacity)
    assigned = jnp.full((experts * capacity + 1,), 2 * row_count, jnp.int32).at[target].set(jnp.arange(2 * row_count, dtype=jnp.int32))[:-1]
    tokens_of = jnp.minimum(assigned // 2, row_count - 1)
    return (assigned, tokens_of)

def group_forward(params, group_piece):
    attention_in, attention_out, expert_in, expert_out, gain_one, gain_two, router, carry_matrix, mixing, constants = params
    tokens, previous, route_rows = group_piece
    group_rows = tokens.shape[0]
    normed_one = low(rms_norm(tokens, gain_one))
    joint_proj = low_back(jnp.einsum('td,dkf->tkf', normed_one, attention_in, precision=highest))
    cosine, sine_table = rope_tables(SEQ, SEQ, HD // 2)
    queries = low(rotate(joint_proj[:, 0].reshape(SEQ_GRP, SEQ, HEADS, HD), cosine, sine_table))
    keys_turned = low(rotate(joint_proj[:, 1].reshape(SEQ_GRP, SEQ, HEADS, HD), cosine, sine_table))
    values_heads = low(joint_proj[:, 2].reshape(SEQ_GRP, SEQ, HEADS, HD))
    scores = low_back(jnp.einsum('bqhd,bkhd->bhqk', queries, keys_turned, precision=highest) * HD ** (-0.5))
    causal = jnp.arange(SEQ, dtype=jnp.int32)[:, None] >= jnp.arange(SEQ, dtype=jnp.int32)[None, :]
    scores = jnp.where(causal, scores, -jnp.inf)
    attention_weights = jax.nn.softmax(scores, axis=-1)
    mixed = jnp.einsum('bhqk,bkhd->bqhd', low(attention_weights), values_heads, precision=highest).reshape(group_rows, D)
    mixed = low(low_back(mixed))
    attended = low_back(jnp.dot(mixed, attention_out, precision=highest))
    hidden = tokens + attended
    normed_two = low(rms_norm(hidden, gain_two))
    logits = jnp.dot(normed_two, router, precision=highest) + jnp.dot(previous, carry_matrix, precision=highest)
    chosen = jnp.take_along_axis(logits, route_rows, axis=1)
    gates = jax.nn.softmax(chosen, axis=-1)
    assigned, tokens_of = dispatch_tables(route_rows, NFFN, CAP)
    gate_table = jnp.concatenate([gates.reshape(-1), jnp.zeros((1,), jnp.float32)])[assigned].reshape(NFFN, CAP)
    rows_in = normed_two[tokens_of].reshape(NFFN, CAP, D)
    gate_up = low_back(jnp.einsum('ecd,ekdf->ekcf', rows_in, expert_in, precision=highest))
    hidden_units = low(jax.nn.silu(gate_up[:, 0]) * gate_up[:, 1])
    expert_rows = low_back(jnp.einsum('ecf,efd->ecd', hidden_units, expert_out, precision=highest))
    weighted = (expert_rows * gate_table[:, :, None]).reshape(NFFN * CAP, D)
    routed = jnp.zeros((group_rows, D), jnp.float32).at[tokens_of].add(weighted)
    mix_logits = jnp.dot(normed_two, mixing, precision=highest).reshape(group_rows, 2, 2)
    alphas = jax.nn.softmax(mix_logits, axis=-1)
    constant_rows = [alphas[:, 0, 0:1] * normed_two + alphas[:, 0, 1:2] * constants[0][None, :], alphas[:, 1, 0:1] * normed_two + alphas[:, 1, 1:2] * constants[1][None, :]]
    local_rows = jnp.zeros_like(hidden)
    for route_slot in range(2):
        chosen_expert = route_rows[:, route_slot:route_slot + 1]
        expert_value = jnp.where(chosen_expert == NFFN + 1, normed_two, 0.0)
        expert_value = expert_value + jnp.where(chosen_expert == NFFN + 2, constant_rows[0], 0.0) + jnp.where(chosen_expert == NFFN + 3, constant_rows[1], 0.0)
        local_rows = local_rows + gates[:, route_slot:route_slot + 1] * expert_value
    return hidden + (routed + local_rows)

def reference(inputs, query_key_value, output_weight, expert_input, expert_output, first_gain, second_gain, router_weight, logit_carry, constant_mix, constant_values, previous_logits, routes, cotangent):
    weights = tuple((weight.astype(jnp.float32) for weight in (query_key_value, output_weight, expert_input, expert_output, first_gain, second_gain, router_weight, logit_carry, constant_mix, constant_values)))

    def forward(tokens, params, previous):
        pieces = (tokens.reshape(N_DP, GROUP, D), previous.reshape(N_DP, GROUP, NEXP), routes.reshape(N_DP, GROUP, 2))

        def one_group(group_piece):
            return group_forward(params, group_piece)
        return lax.map(jax.checkpoint(one_group), pieces).reshape(TOKENS, D)
    output, pullback = jax.vjp(forward, inputs.astype(jnp.float32), weights, previous_logits.astype(jnp.float32))
    input_grad, weight_grads, logits_grad = pullback(cotangent.astype(jnp.float32))
    return (output.astype(jnp.bfloat16), input_grad, logits_grad, weight_grads[0], weight_grads[1], weight_grads[2], weight_grads[3], weight_grads[4], weight_grads[5], weight_grads[6], weight_grads[7], weight_grads[8], weight_grads[9])
```

```python
import jax
import jax.numpy as jnp
from jax import lax
from jax.sharding import PartitionSpec as P

HD = 64
NFFN = 8
NEXP = 12
SEQ = 1024
CAP = 256


epsilon = 1e-06
rope_base = 10000.0
highest = lax.Precision.HIGHEST


def rope_tables(length, period, half):
    positions = (jnp.arange(length, dtype=jnp.int32) % period).astype(jnp.float32)
    frequency = rope_base ** (-jnp.arange(half, dtype=jnp.float32) / half)
    angles = positions[:, None] * frequency[None, :]
    return (jnp.cos(angles), jnp.sin(angles))


def rotate(values, cosine, sine_table):
    half = values.shape[-1] // 2
    front_half = values[..., :half]
    back_half = values[..., half:]
    cosine = cosine[:, None, :]
    sine_table = sine_table[:, None, :]
    return jnp.concatenate(
        [
            front_half * cosine - back_half * sine_table,
            back_half * cosine + front_half * sine_table,
        ],
        axis=-1,
    )


def rotate_back(grads, cosine, sine_table):
    half = grads.shape[-1] // 2
    front_half = grads[..., :half]
    back_half = grads[..., half:]
    cosine = cosine[:, None, :]
    sine_table = sine_table[:, None, :]
    return jnp.concatenate(
        [
            front_half * cosine + back_half * sine_table,
            back_half * cosine - front_half * sine_table,
        ],
        axis=-1,
    )


def dispatch_tables(route_rows, experts, capacity):
    row_count = route_rows.shape[0]
    flat_routes = route_rows.reshape(-1)
    onehot = (flat_routes[:, None] == jnp.arange(experts, dtype=jnp.int32)[None, :]).astype(
        jnp.int32
    )
    before = jnp.cumsum(onehot, axis=0) - onehot
    position = jnp.sum(before * onehot, axis=1)
    target = jnp.where(flat_routes < experts, flat_routes * capacity + position, experts * capacity)
    assigned = (
        jnp.full((experts * capacity + 1,), 2 * row_count, jnp.int32)
        .at[target]
        .set(jnp.arange(2 * row_count, dtype=jnp.int32))[:-1]
    )
    tokens_of = jnp.minimum(assigned // 2, row_count - 1)
    return (assigned, tokens_of)


def norm_back(values, norm_scale, gain, grads):
    scaled = values * norm_scale
    gain_grad = jnp.sum(grads * scaled, axis=0)
    weighted_grad = grads * gain
    values_grad = norm_scale * (
        weighted_grad - scaled * jnp.mean(weighted_grad * scaled, axis=-1, keepdims=True)
    )
    return (gain_grad, values_grad)


def local_values(chosen_expert, normed_rows, constant_rows):
    expert_value = jnp.where(chosen_expert == NFFN + 1, normed_rows, 0.0)
    return (
        expert_value
        + jnp.where(chosen_expert == NFFN + 2, constant_rows[0], 0.0)
        + jnp.where(chosen_expert == NFFN + 3, constant_rows[1], 0.0)
    )


def clusters():
    groups = lax.axis_size("dp") // NFFN
    near = [[group * NFFN + expert for expert in range(NFFN)] for group in range(groups)]
    far = [[group * NFFN + expert for group in range(groups)] for expert in range(NFFN)]
    return groups, near, far


def swap(blocks):
    _, near, _ = clusters()
    return lax.all_to_all(blocks, "dp", 0, 0, axis_index_groups=near, tiled=True)


def exchange(shard, dim):
    groups, near, far = clusters()
    own = lax.all_to_all(shard, "dp", 0, dim, axis_index_groups=near, tiled=True)
    if groups > 1:
        own = lax.all_gather(own, "dp", axis=dim, axis_index_groups=far, tiled=True)
    return own


def exchange_back(grads, dim):
    groups, near, far = clusters()
    if groups > 1:
        grads = lax.psum_scatter(
            grads, "dp", scatter_dimension=dim, axis_index_groups=far, tiled=True
        )
    grads = grads.astype(jnp.bfloat16)
    return lax.all_to_all(grads, "dp", dim, 0, axis_index_groups=near, tiled=True).astype(
        jnp.float32
    )


def per_device(
    inputs,
    query_key_value,
    output_weight,
    expert_input,
    expert_output,
    first_gain,
    second_gain,
    router_weight,
    logit_carry,
    constant_mix,
    constant_values,
    previous_logits,
    routes,
    cotangent,
):
    shard_rows = inputs.shape[0]
    model_width = inputs.shape[1]
    group_rows = shard_rows * lax.axis_size("mp")
    offset = lax.axis_index("mp") * shard_rows
    heads_here = query_key_value.shape[2] // HD
    score_scale = HD ** (-0.5)
    block_rows = min(512, SEQ)
    blocks_per_seq = SEQ // block_rows
    block_count = group_rows // block_rows
    sequences = group_rows // SEQ
    gain_one = first_gain.astype(jnp.float32)
    gain_two = second_gain.astype(jnp.float32)
    tokens = inputs.astype(jnp.float32)
    scale_one = lax.rsqrt(jnp.mean(tokens * tokens, axis=-1, keepdims=True) + epsilon)
    normed_one = (tokens * scale_one * gain_one).astype(jnp.bfloat16)
    rows_one = lax.all_gather(normed_one, "mp", axis=0, tiled=True)
    attention_in, attention_out = (
        lax.all_gather(query_key_value, "dp", axis=0, tiled=True),
        lax.all_gather(output_weight, "dp", axis=1, tiled=True),
    )
    joint_proj = jnp.einsum(
        "td,dkf->tkf", rows_one, attention_in, preferred_element_type=jnp.float32
    )
    cosine, sine_table = rope_tables(group_rows, SEQ, HD // 2)
    queries = rotate(
        joint_proj[:, 0].reshape(group_rows, heads_here, HD), cosine, sine_table
    ).astype(jnp.bfloat16)
    keys_turned = rotate(
        joint_proj[:, 1].reshape(group_rows, heads_here, HD), cosine, sine_table
    ).astype(jnp.bfloat16)
    values_heads = joint_proj[:, 2].reshape(group_rows, heads_here, HD).astype(jnp.bfloat16)
    query_blocks = queries.reshape(block_count, block_rows, heads_here, HD)
    key_seqs = keys_turned.reshape(sequences, SEQ, heads_here, HD)
    value_seqs = values_heads.reshape(sequences, SEQ, heads_here, HD)
    key_positions = jnp.arange(SEQ, dtype=jnp.int32)

    def block_scores(block_index):
        seq_index = block_index // blocks_per_seq
        query_rows = query_blocks[block_index]
        key_rows = key_seqs[seq_index]
        raw_scores = (
            jnp.einsum("qhd,khd->hqk", query_rows, key_rows, preferred_element_type=jnp.float32)
            * score_scale
        )
        query_positions = block_index % blocks_per_seq * block_rows + jnp.arange(
            block_rows, dtype=jnp.int32
        )
        causal = query_positions[:, None] >= key_positions[None, :]
        return (
            jnp.where(causal[None], raw_scores, -jnp.inf),
            query_rows,
            key_rows,
            value_seqs[seq_index],
        )

    def attend_block(block_index):
        scores, query_rows, key_rows, value_rows = block_scores(block_index)
        row_peak = jnp.max(scores, axis=-1, keepdims=True)
        exponent = jnp.exp(scores - row_peak)
        row_total = jnp.sum(exponent, axis=-1, keepdims=True)
        attention_weights = (exponent / row_total).astype(jnp.bfloat16)
        mixed_rows = jnp.einsum(
            "hqk,khd->qhd", attention_weights, value_rows, preferred_element_type=jnp.float32
        )
        return (mixed_rows, (row_peak + jnp.log(row_total))[..., 0])

    mixed_blocks, log_totals = lax.map(attend_block, jnp.arange(block_count, dtype=jnp.int32))
    mixed = mixed_blocks.reshape(group_rows, heads_here * HD).astype(jnp.bfloat16)
    attention_part = jnp.dot(mixed, attention_out, preferred_element_type=jnp.float32)
    attended = lax.psum_scatter(attention_part, "mp", scatter_dimension=0, tiled=True)
    hidden = tokens + attended
    scale_two = lax.rsqrt(jnp.mean(hidden * hidden, axis=-1, keepdims=True) + epsilon)
    normed_two = (hidden * scale_two * gain_two).astype(jnp.bfloat16)
    rows_two = lax.all_gather(normed_two, "mp", axis=0, tiled=True)
    logits = jnp.dot(rows_two, router_weight, preferred_element_type=jnp.float32) + jnp.dot(
        previous_logits, logit_carry, precision=highest
    )
    chosen = jnp.take_along_axis(logits, routes, axis=1)
    gates = jax.nn.softmax(chosen, axis=-1)
    assigned, tokens_of = dispatch_tables(routes, NFFN, CAP)
    gate_table = jnp.concatenate([gates.reshape(-1), jnp.zeros((1,), jnp.float32)])[
        assigned
    ].reshape(NFFN, CAP)
    expert_in_rows = exchange(expert_input, 2)[0]
    expert_out_rows = exchange(expert_output, 2)[0]
    rows_in = swap(rows_two[tokens_of].reshape(NFFN, CAP, model_width))
    rows_in = rows_in.reshape(NFFN * CAP, model_width)
    gate_up = jnp.einsum("cd,kdf->kcf", rows_in, expert_in_rows, preferred_element_type=jnp.float32)
    gate_pre = gate_up[0]
    up_pre = gate_up[1]
    hidden_units = (jax.nn.silu(gate_pre) * up_pre).astype(jnp.bfloat16)
    expert_rows = jnp.einsum(
        "cf,fd->cd", hidden_units, expert_out_rows, preferred_element_type=jnp.float32
    )
    expert_rows = swap(expert_rows.astype(jnp.bfloat16).reshape(NFFN, CAP, model_width))
    expert_rows = expert_rows.astype(jnp.float32)
    weighted = (expert_rows * gate_table[:, :, None]).reshape(NFFN * CAP, model_width)
    routed = jnp.zeros((group_rows, model_width), jnp.float32).at[tokens_of].add(weighted)
    routed_own = lax.psum_scatter(
        routed.astype(jnp.bfloat16), "mp", scatter_dimension=0, tiled=True
    ).astype(jnp.float32)
    routes_own = lax.dynamic_slice_in_dim(routes, offset, shard_rows, 0)
    gates_own = lax.dynamic_slice_in_dim(gates, offset, shard_rows, 0)
    previous_own = lax.dynamic_slice_in_dim(previous_logits, offset, shard_rows, 0)
    normed_float = normed_two.astype(jnp.float32)
    mixing = constant_mix.astype(jnp.float32)
    constants = constant_values.astype(jnp.float32)
    mix_logits = jnp.dot(normed_two, constant_mix, preferred_element_type=jnp.float32).reshape(
        shard_rows, 2, 2
    )
    alphas = jax.nn.softmax(mix_logits, axis=-1)
    constant_rows = [
        alphas[:, 0, 0:1] * normed_float + alphas[:, 0, 1:2] * constants[0][None, :],
        alphas[:, 1, 0:1] * normed_float + alphas[:, 1, 1:2] * constants[1][None, :],
    ]
    first_value = local_values(routes_own[:, 0:1], normed_float, constant_rows)
    second_value = local_values(routes_own[:, 1:2], normed_float, constant_rows)
    local_rows = gates_own[:, 0:1] * first_value + gates_own[:, 1:2] * second_value
    output = (hidden + (routed_own + local_rows)).astype(jnp.bfloat16)
    grad_out = cotangent.astype(jnp.float32)
    grad_rows_all = lax.all_gather(cotangent, "mp", axis=0, tiled=True)
    slot_grads = grad_rows_all[tokens_of].reshape(NFFN, CAP, model_width).astype(jnp.float32)
    expert_grad = (slot_grads * gate_table[:, :, None]).astype(jnp.bfloat16)
    gate_slot = jnp.sum(slot_grads * expert_rows, axis=-1)
    out_grad = swap(expert_grad).reshape(NFFN * CAP, model_width)
    output_side_grad = jnp.einsum(
        "cf,cd->fd", hidden_units, out_grad, preferred_element_type=jnp.float32
    )
    units_grad = jnp.einsum(
        "cd,fd->cf", out_grad, expert_out_rows, preferred_element_type=jnp.float32
    )
    sigmoid_gate = jax.nn.sigmoid(gate_pre)
    gate_pre_grad = units_grad * up_pre * sigmoid_gate * (1.0 + gate_pre * (1.0 - sigmoid_gate))
    up_pre_grad = units_grad * gate_pre * sigmoid_gate
    pre_grads = jnp.stack([gate_pre_grad, up_pre_grad], axis=0).astype(jnp.bfloat16)
    input_side_grad = jnp.einsum(
        "cd,kcf->kdf", rows_in, pre_grads, preferred_element_type=jnp.float32
    )
    rows_grad = jnp.einsum(
        "kcf,kdf->cd", pre_grads, expert_in_rows, preferred_element_type=jnp.float32
    )
    rows_grad = swap(rows_grad.astype(jnp.bfloat16).reshape(NFFN, CAP, model_width))
    rows_grad = rows_grad.astype(jnp.float32)
    normed_part = (
        jnp.zeros((group_rows, model_width), jnp.float32)
        .at[tokens_of]
        .add(rows_grad.reshape(NFFN * CAP, model_width))
    )
    gate_part = (
        jnp.zeros((2 * group_rows + 1,), jnp.float32)
        .at[assigned]
        .add(gate_slot.reshape(-1))[:-1]
        .reshape(group_rows, 2)
    )
    normed_grad_moe, gate_grad_ffn = (
        lax.psum_scatter(normed_part, "mp", scatter_dimension=0, tiled=True),
        lax.psum_scatter(gate_part, "mp", scatter_dimension=0, tiled=True),
    )
    local_gate_grad = jnp.stack(
        [jnp.sum(grad_out * first_value, axis=-1), jnp.sum(grad_out * second_value, axis=-1)],
        axis=1,
    )
    gate_grad = gate_grad_ffn + local_gate_grad
    copy_weight = gates_own[:, 0:1] * (routes_own[:, 0:1] == NFFN + 1) + gates_own[:, 1:2] * (
        routes_own[:, 1:2] == NFFN + 1
    )
    normed_grad = normed_grad_moe + copy_weight * grad_out
    mix_grads = []
    values_grads = []
    for constant_index in range(2):
        expert_number = NFFN + 2 + constant_index
        route_weight = gates_own[:, 0:1] * (routes_own[:, 0:1] == expert_number) + gates_own[
            :, 1:2
        ] * (routes_own[:, 1:2] == expert_number)
        const_grad = route_weight * grad_out
        normed_grad = normed_grad + alphas[:, constant_index, 0:1] * const_grad
        alpha_grad = jnp.stack(
            [
                jnp.sum(const_grad * normed_float, axis=-1),
                jnp.sum(const_grad * constants[constant_index][None, :], axis=-1),
            ],
            axis=1,
        )
        values_grads.append(jnp.sum(alphas[:, constant_index, 1:2] * const_grad, axis=0))
        alpha_pair = alphas[:, constant_index]
        mix_grads.append(
            alpha_pair * (alpha_grad - jnp.sum(alpha_pair * alpha_grad, axis=-1, keepdims=True))
        )
    mix_grad = jnp.concatenate(mix_grads, axis=1)
    constant_mix_grad = jnp.einsum("td,tc->dc", normed_float, mix_grad, precision=highest)
    normed_grad = normed_grad + jnp.einsum("tc,dc->td", mix_grad, mixing, precision=highest)
    constant_values_grad = jnp.stack(values_grads, axis=0)
    chosen_grad = gates_own * (gate_grad - jnp.sum(gates_own * gate_grad, axis=-1, keepdims=True))
    expert_ids = jnp.arange(NEXP, dtype=jnp.int32)[None, :]
    logit_grad = chosen_grad[:, 0:1] * (routes_own[:, 0:1] == expert_ids) + chosen_grad[:, 1:2] * (
        routes_own[:, 1:2] == expert_ids
    )
    router_grad = jnp.einsum("td,te->de", normed_float, logit_grad, precision=highest)
    logit_carry_grad = jnp.einsum("tf,te->fe", previous_own, logit_grad, precision=highest)
    logits_grad = jnp.einsum("te,fe->tf", logit_grad, logit_carry, precision=highest)
    normed_grad = normed_grad + jnp.einsum(
        "te,de->td", logit_grad, router_weight.astype(jnp.float32), precision=highest
    )
    second_gain_grad, hidden_norm_grad = norm_back(hidden, scale_two, gain_two, normed_grad)
    hidden_grad = grad_out + hidden_norm_grad
    attended_grad = lax.all_gather(hidden_grad.astype(jnp.bfloat16), "mp", axis=0, tiled=True)
    output_weight_grad = jnp.einsum(
        "tf,td->fd", mixed, attended_grad, preferred_element_type=jnp.float32
    )
    mixed_grad = jnp.einsum(
        "td,fd->tf", attended_grad, attention_out, preferred_element_type=jnp.float32
    ).astype(jnp.bfloat16)
    mixed_grad_blocks = mixed_grad.reshape(block_count, block_rows, heads_here, HD)

    def attend_back(block_index):
        scores, query_rows, key_rows, value_rows = block_scores(block_index)
        out_grad_rows = mixed_grad_blocks[block_index]
        attention_weights = jnp.exp(scores - log_totals[block_index][:, :, None])
        weights_grad = jnp.einsum(
            "qhd,khd->hqk", out_grad_rows, value_rows, preferred_element_type=jnp.float32
        )
        inner_sum = jnp.sum(attention_weights * weights_grad, axis=-1, keepdims=True)
        score_grad = (attention_weights * (weights_grad - inner_sum)).astype(jnp.bfloat16)
        query_grad = (
            jnp.einsum("hqk,khd->qhd", score_grad, key_rows, preferred_element_type=jnp.float32)
            * score_scale
        )
        key_grad = (
            jnp.einsum("hqk,qhd->khd", score_grad, query_rows, preferred_element_type=jnp.float32)
            * score_scale
        )
        value_grad = jnp.einsum(
            "hqk,qhd->khd",
            attention_weights.astype(jnp.bfloat16),
            out_grad_rows,
            preferred_element_type=jnp.float32,
        )
        return (query_grad, key_grad, value_grad)

    query_grads, key_grads, value_grads = lax.map(
        attend_back, jnp.arange(block_count, dtype=jnp.int32)
    )
    query_grads = query_grads.reshape(group_rows, heads_here, HD)
    key_grads = (
        key_grads.reshape(sequences, blocks_per_seq, SEQ, heads_here, HD)
        .sum(axis=1)
        .reshape(group_rows, heads_here, HD)
    )
    value_grads = (
        value_grads.reshape(sequences, blocks_per_seq, SEQ, heads_here, HD)
        .sum(axis=1)
        .reshape(group_rows, heads_here, HD)
    )
    query_raw_grad = rotate_back(query_grads, cosine, sine_table).reshape(
        group_rows, heads_here * HD
    )
    key_raw_grad = rotate_back(key_grads, cosine, sine_table).reshape(group_rows, heads_here * HD)
    joint_grad = jnp.stack(
        [query_raw_grad, key_raw_grad, value_grads.reshape(group_rows, heads_here * HD)], axis=1
    ).astype(jnp.bfloat16)
    attention_in_grad = jnp.einsum(
        "td,tkf->dkf", rows_one, joint_grad, preferred_element_type=jnp.float32
    )
    normed_one_part = jnp.einsum(
        "tkf,dkf->td", joint_grad, attention_in, preferred_element_type=jnp.float32
    )
    normed_one_grad = lax.psum_scatter(
        normed_one_part.astype(jnp.bfloat16), "mp", scatter_dimension=0, tiled=True
    ).astype(jnp.float32)
    first_gain_grad, input_norm_grad = norm_back(tokens, scale_one, gain_one, normed_one_grad)
    input_grad = hidden_grad + input_norm_grad
    attention_in_own, attention_out_own = (
        lax.psum_scatter(attention_in_grad, "dp", scatter_dimension=0, tiled=True),
        lax.psum_scatter(output_weight_grad, "dp", scatter_dimension=1, tiled=True),
    )
    expert_in_grad = exchange_back(input_side_grad[None], 2)
    expert_out_grad = exchange_back(output_side_grad[None], 2)
    small_sums = lax.psum(
        (
            first_gain_grad,
            second_gain_grad,
            router_grad,
            logit_carry_grad,
            constant_mix_grad,
            constant_values_grad,
        ),
        ("dp", "mp"),
    )
    return (
        output,
        input_grad,
        logits_grad,
        attention_in_own,
        attention_out_own,
        expert_in_grad,
        expert_out_grad,
        small_sums[0],
        small_sums[1],
        small_sums[2],
        small_sums[3],
        small_sums[4],
        small_sums[5],
    )


def solution(mesh):
    in_specs = (
        P(("dp", "mp"), None),
        P("dp", None, "mp"),
        P("mp", "dp"),
        P(None, None, "dp", "mp"),
        P(None, "mp", "dp"),
        P(),
        P(),
        P(),
        P(),
        P(),
        P(),
        P("dp", None),
        P("dp", None),
        P(("dp", "mp"), None),
    )
    out_specs = (
        P(("dp", "mp"), None),
        P(("dp", "mp"), None),
        P(("dp", "mp"), None),
        P("dp", None, "mp"),
        P("mp", "dp"),
        P(None, None, "dp", "mp"),
        P(None, "mp", "dp"),
        P(),
        P(),
        P(),
        P(),
        P(),
        P(),
    )
    return jax.shard_map(
        per_device, mesh=mesh, in_specs=in_specs, out_specs=out_specs, check_vma=False
    )
```

```python
import functools
import numpy as np
import jax
import jax.numpy as jnp
from jax import lax
from jax.sharding import PartitionSpec as P
from jax.experimental import pallas as pl
from jax.experimental.pallas import tpu as pltpu

HD = 64
NFFN = 8
NEXP = 12
SEQ = 1024
CAP = 256
MP = 4
QUARTER = CAP // MP

epsilon = 1e-06
rope_base = 10000.0
highest = lax.Precision.HIGHEST
f32 = jnp.float32
bf16 = jnp.bfloat16
MESH = pl.DeviceIdType.MESH
VM = pl.BlockSpec(memory_space=pltpu.VMEM)
HB = pl.BlockSpec(memory_space=pl.ANY)
NT = (((1,), (1,)), ((), ()))
TN = (((0,), (0,)), ((), ()))


def flip(index, distance):
    out = index
    bit = 1
    while bit <= distance:
        if distance & bit:
            out = out + bit - 2 * bit * ((index // bit) % 2)
        bit *= 2
    return out


def dotf(a, b, dims=None):
    if dims is None:
        return jnp.dot(a, b, preferred_element_type=f32)
    return lax.dot_general(a, b, dims, preferred_element_type=f32)


def remote(src, dst, send, recv, **where):
    return pltpu.make_async_remote_copy(
        src_ref=src, dst_ref=dst, send_sem=send, recv_sem=recv, device_id=where, device_id_type=MESH
    )


def greet(mp_me, near, base):
    barrier = pltpu.get_barrier_semaphore()
    for k in range(1, MP):
        pl.semaphore_signal(barrier, inc=1, device_id={"mp": flip(mp_me, k)}, device_id_type=MESH)
    for k in range(1, NFFN):
        pl.semaphore_signal(
            barrier, inc=1, device_id={"dp": base + flip(near, k)}, device_id_type=MESH
        )
    pl.semaphore_wait(barrier, MP - 1 + NFFN - 1)


def rope_constants():
    half = HD // 2
    positions = np.arange(SEQ, dtype=np.float32)
    frequency = (rope_base ** (-np.arange(half, dtype=np.float32) / half)).astype(np.float32)
    angles = (positions[:, None] * frequency[None, :]).astype(np.float32)
    cosine, sine = np.cos(angles), np.sin(angles)
    return (
        np.concatenate([cosine, cosine], axis=1),
        np.concatenate([-sine, sine], axis=1),
    )


def swap_halves(x):
    half = HD // 2
    return jnp.concatenate([x[:, half:], x[:, :half]], axis=1)


class Gather:
    def __init__(self, ref, mp_me, send, recv):
        self.me, self.core, self.chip = mp_me, flip(mp_me, 1), flip(mp_me, 2)
        own = ref.at[mp_me]
        far = ref.at[self.chip]
        self.to_chip = remote(own, own, send.at[0], recv.at[0], mp=self.chip)
        self.to_core = remote(own, own, send.at[1], recv.at[1], mp=self.core)
        self.relay = remote(far, far, send.at[2], recv.at[2], mp=self.core)

    def start(self):
        self.to_chip.start()
        self.to_core.start()

    def forward(self):
        self.to_chip.wait_recv()
        self.relay.start()

    def finish(self):
        self.to_core.wait_recv()
        self.relay.wait_recv()
        self.to_chip.wait_send()
        self.to_core.wait_send()
        self.relay.wait_send()


def attention_kernel(
    inside,
    x_ref, gain1_ref, gain2_ref, cos_ref, sin_ref, wshard_ref, win_shard, wout_shard,
    rows1_ref, w_ref, q_ref, k_ref, v_ref, mixed_ref, lse_ref, hidden_ref, rows2_ref, *rest,
):
    if inside:
        win_ref, wout_ref, *rest = rest
    (part_ref, core_in, chip_out, chip_in, core_out,
     sends, recvs, wsend, wrecv, esend, erecv, local) = rest
    mp_me = lax.axis_index("mp")
    dp_me = lax.axis_index("dp")
    near = lax.rem(dp_me, NFFN)
    base = dp_me - near
    core, chip = flip(mp_me, 1), flip(mp_me, 2)
    rows = x_ref.shape[0]
    depth = w_ref.shape[1]
    greet(mp_me, near, base)

    tokens = x_ref[...].astype(f32)
    scale = lax.rsqrt(jnp.mean(tokens * tokens, axis=-1, keepdims=True) + epsilon)
    rows1_ref[mp_me] = (tokens * scale * gain1_ref[...]).astype(bf16)
    gather1 = Gather(rows1_ref, mp_me, sends.at[pl.ds(0, 3)], recvs.at[pl.ds(0, 3)])
    gather1.start()

    if inside:
        w_ref[near] = wshard_ref[...]
        own = w_ref.at[near]
        along = [
            remote(own, own, wsend.at[k], wrecv.at[k], dp=base + flip(near, k)) for k in (2, 4, 6)
        ]
        for copy in along:
            copy.start()
        mate = base + flip(near, 1)
        across = [remote(own, own, wsend.at[0], wrecv.at[0], dp=mate)]
        across[0].start()
        for k, copy in zip((2, 4, 6), along):
            copy.wait_recv()
            block = w_ref.at[flip(near, k)]
            onward = remote(block, block, wsend.at[k + 1], wrecv.at[k + 1], dp=mate)
            onward.start()
            across.append(onward)
        gather1.forward()
        for copy in across:
            copy.wait_recv()
        for copy in along + across:
            copy.wait_send()
        experts = []
        din = win_shard.shape[2]
        place = pl.ds(pl.multiple_of(near * din, din), din)
        for k in (6, 4, 7, 5, 2, 3, 1):
            peer = flip(near, k)
            for i, (src, dst) in enumerate(
                [(win_shard.at[peer], win_ref.at[:, place]), (wout_shard.at[peer], wout_ref.at[place])]
            ):
                experts.append(
                    remote(src, dst, esend.at[i, k], erecv.at[i, k], dp=base + peer)
                )
        for copy in experts:
            copy.start()
        mine = [
            pltpu.make_async_copy(win_shard.at[near], win_ref.at[:, place], local.at[0]),
            pltpu.make_async_copy(wout_shard.at[near], wout_ref.at[place], local.at[1]),
        ]
        for copy in mine:
            copy.start()
    else:
        w_ref[...] = wshard_ref[...]
        gather1.forward()
    gather1.finish()

    width = x_ref.shape[1]
    w_all = w_ref[...].reshape(width, w_ref.shape[2])
    heads = q_ref.shape[0]
    cols = heads * HD

    def project(i, carry):
        at = pl.ds(pl.multiple_of(i * rows, rows), rows)
        joint = dotf(rows1_ref[i], w_all[:, : 3 * cols])
        cosine, sine = cos_ref[at], sin_ref[at]
        for h in range(heads):
            query = joint[:, h * HD : (h + 1) * HD]
            key = joint[:, cols + h * HD : cols + (h + 1) * HD]
            q_ref[h, at] = (query * cosine + swap_halves(query) * sine).astype(bf16)
            k_ref[h, at] = (key * cosine + swap_halves(key) * sine).astype(bf16)
            v_ref[h, at] = joint[:, 2 * cols + h * HD : 2 * cols + (h + 1) * HD].astype(bf16)
        return carry

    lax.fori_loop(0, MP, project, 0)
    out_weight = w_all[:, 3 * cols :]

    to_core = [
        remote(core_out.at[j], core_in.at[j], sends.at[3 + j], recvs.at[3 + j], mp=core)
        for j in range(2)
    ]
    to_chip = remote(chip_out, chip_in, sends.at[5], recvs.at[5], mp=chip)

    def attend(step, carry):
        block = flip(mp_me, 3)
        block = jnp.where(step == 1, core, jnp.where(step == 2, chip, jnp.where(step == 3, mp_me, block)))
        at = pl.ds(pl.multiple_of(block * rows, rows), rows)
        row_ids = block * rows + lax.broadcasted_iota(jnp.int32, (rows, SEQ), 0)
        seen = row_ids >= lax.broadcasted_iota(jnp.int32, (rows, SEQ), 1)
        for h in range(heads):
            scores = dotf(q_ref[h, at], k_ref[h], NT) * HD**-0.5
            scores = jnp.where(seen, scores, -jnp.inf)
            peak = jnp.max(scores, axis=-1, keepdims=True)
            exponent = jnp.exp(scores - peak)
            total = jnp.sum(exponent, axis=-1, keepdims=True)
            probs = (exponent * (1.0 / total)).astype(bf16)
            mixed_ref[at, h * HD : (h + 1) * HD] = dotf(probs, v_ref[h]).astype(bf16)
            lse_ref[at, h : h + 1] = peak + jnp.log(total)
        part = dotf(mixed_ref[at], out_weight, NT)

        @pl.when(step == 0)
        def _():
            core_out[0] = part.astype(bf16)
            to_core[0].start()

        @pl.when(step == 1)
        def _():
            core_out[1] = part.astype(bf16)
            to_core[1].start()

        @pl.when(step == 2)
        def _():
            to_core[0].wait_recv()
            chip_out[...] = (part + core_in[0].astype(f32)).astype(bf16)
            to_chip.start()

        @pl.when(step == 3)
        def _():
            part_ref[...] = part

        return carry

    lax.fori_loop(0, MP, attend, 0)
    to_core[1].wait_recv()
    partial = part_ref[...] + core_in[1].astype(f32)
    to_chip.wait_recv()
    hidden = x_ref[...].astype(f32) + (partial + chip_in[...].astype(f32))
    hidden_ref[...] = hidden
    scale2 = lax.rsqrt(jnp.mean(hidden * hidden, axis=-1, keepdims=True) + epsilon)
    rows2_ref[mp_me] = (hidden * scale2 * gain2_ref[...]).astype(bf16)
    gather2 = Gather(rows2_ref, mp_me, sends.at[pl.ds(6, 3)], recvs.at[pl.ds(6, 3)])
    gather2.start()
    for copy in to_core + [to_chip]:
        copy.wait_send()
    gather2.forward()
    gather2.finish()
    if inside:
        for copy in experts:
            copy.wait_recv()
        for copy in experts:
            copy.wait_send()
        for copy in mine:
            copy.wait()


def attention(x, gain1, gain2, wshard, win, wout, groups):
    rows, width = x.shape
    cos, sin = rope_constants()
    inside = groups == 1
    cols = wshard.shape[-1]
    depth = width // NFFN
    hidden_cols = win.shape[-1]
    heads = cols // 4 // HD
    sd = jax.ShapeDtypeStruct
    outs = [
        sd((MP, rows, width), bf16),
        sd((NFFN, depth, cols), bf16),
        sd((heads, SEQ, HD), bf16),
        sd((heads, SEQ, HD), bf16),
        sd((heads, SEQ, HD), bf16),
        sd((SEQ, heads * HD), bf16),
        sd((SEQ, 128), f32),
        sd((rows, width), f32),
        sd((MP, rows, width), bf16),
    ]
    specs = [VM] * len(outs)
    if inside:
        outs += [sd((2, width, hidden_cols), bf16), sd((width, hidden_cols), bf16)]
        specs += [HB, HB]
    else:
        wshard = wshard.reshape(NFFN, depth, cols)
    dma = pltpu.SemaphoreType.DMA
    return pl.pallas_call(
        functools.partial(attention_kernel, inside),
        out_shape=outs,
        in_specs=[VM] * 6 + [HB, HB],
        out_specs=specs,
        scratch_shapes=[
            pltpu.VMEM((rows, width), f32),
            pltpu.VMEM((2, rows, width), bf16),
            pltpu.VMEM((rows, width), bf16),
            pltpu.VMEM((rows, width), bf16),
            pltpu.VMEM((2, rows, width), bf16),
            dma((9,)), dma((9,)),
            dma((8,)), dma((8,)),
            dma((2, 8)), dma((2, 8)),
            dma((2,)),
        ],
        compiler_params=pltpu.CompilerParams(
            collective_id=0, has_side_effects=True, vmem_limit_bytes=56 * 2**20
        ),
        name="attention_forward",
    )(x, gain1, gain2, jnp.asarray(cos), jnp.asarray(sin), wshard, win, wout)


def rotate_back(grads, cosine, sine_table):
    half = grads.shape[-1] // 2
    front_half = grads[..., :half]
    back_half = grads[..., half:]
    cosine = cosine[:, None, :]
    sine_table = sine_table[:, None, :]
    return jnp.concatenate(
        [
            front_half * cosine + back_half * sine_table,
            back_half * cosine - front_half * sine_table,
        ],
        axis=-1,
    )


def dispatch_tables(route_rows, experts, capacity):
    row_count = route_rows.shape[0]
    flat_routes = route_rows.reshape(-1)
    onehot = (flat_routes[:, None] == jnp.arange(experts, dtype=jnp.int32)[None, :]).astype(
        jnp.int32
    )
    before = jnp.cumsum(onehot, axis=0) - onehot
    position = jnp.sum(before * onehot, axis=1)
    target = jnp.where(flat_routes < experts, flat_routes * capacity + position, experts * capacity)
    assigned = (
        jnp.full((experts * capacity + 1,), 2 * row_count, jnp.int32)
        .at[target]
        .set(jnp.arange(2 * row_count, dtype=jnp.int32))[:-1]
    )
    tokens_of = jnp.minimum(assigned // 2, row_count - 1)
    return (assigned, tokens_of)


def norm_back(values, norm_scale, gain, grads):
    scaled = values * norm_scale
    gain_grad = jnp.sum(grads * scaled, axis=0)
    weighted_grad = grads * gain
    values_grad = norm_scale * (
        weighted_grad - scaled * jnp.mean(weighted_grad * scaled, axis=-1, keepdims=True)
    )
    return (gain_grad, values_grad)


def local_values(chosen_expert, normed_rows, constant_rows):
    expert_value = jnp.where(chosen_expert == NFFN + 1, normed_rows, 0.0)
    return (
        expert_value
        + jnp.where(chosen_expert == NFFN + 2, constant_rows[0], 0.0)
        + jnp.where(chosen_expert == NFFN + 3, constant_rows[1], 0.0)
    )


def clusters():
    groups = lax.axis_size("dp") // NFFN
    near = [[group * NFFN + expert for expert in range(NFFN)] for group in range(groups)]
    far = [[group * NFFN + expert for group in range(groups)] for expert in range(NFFN)]
    return groups, near, far


def swap(blocks):
    _, near, _ = clusters()
    return lax.all_to_all(blocks, "dp", 0, 0, axis_index_groups=near, tiled=True)


def exchange(shard, dim):
    groups, near, far = clusters()
    own = lax.all_to_all(shard, "dp", 0, dim, axis_index_groups=near, tiled=True)
    if groups > 1:
        own = lax.all_gather(own, "dp", axis=dim, axis_index_groups=far, tiled=True)
    return own


def exchange_back(grads, dim):
    groups, near, far = clusters()
    if groups > 1:
        grads = lax.psum_scatter(
            grads, "dp", scatter_dimension=dim, axis_index_groups=far, tiled=True
        )
    grads = grads.astype(jnp.bfloat16)
    return lax.all_to_all(grads, "dp", dim, 0, axis_index_groups=near, tiled=True).astype(
        jnp.float32
    )


def per_device(
    inputs,
    query_key_value,
    output_weight,
    expert_input,
    expert_output,
    first_gain,
    second_gain,
    router_weight,
    logit_carry,
    constant_mix,
    constant_values,
    previous_logits,
    routes,
    cotangent,
):
    shard_rows = inputs.shape[0]
    model_width = inputs.shape[1]
    group_rows = shard_rows * lax.axis_size("mp")
    offset = lax.axis_index("mp") * shard_rows
    heads_here = query_key_value.shape[2] // HD
    score_scale = HD ** (-0.5)
    block_rows = min(512, SEQ)
    blocks_per_seq = SEQ // block_rows
    block_count = group_rows // block_rows
    sequences = group_rows // SEQ
    gain_one = first_gain.astype(jnp.float32)
    gain_two = second_gain.astype(jnp.float32)
    tokens = inputs.astype(jnp.float32)
    scale_one = lax.rsqrt(jnp.mean(tokens * tokens, axis=-1, keepdims=True) + epsilon)
    cos, sin = rope_constants()
    cosine, sine_table = jnp.asarray(cos[:, : HD // 2]), jnp.asarray(sin[:, HD // 2 :])
    groups, _, _ = clusters()
    shard = jnp.concatenate(
        [query_key_value.reshape(query_key_value.shape[0], -1), output_weight.T], axis=1
    )
    expert_output_t = expert_output.transpose(0, 2, 1)
    if groups > 1:
        shard = lax.all_gather(shard, "dp", axis=0, tiled=True)
        expert_in_rows = exchange(expert_input, 2)[0]
        expert_out_t = exchange(expert_output_t, 1)[0]
    got = attention(
        inputs, gain_one[None], gain_two[None], shard, expert_input, expert_output_t, groups
    )
    if groups == 1:
        expert_in_rows, expert_out_t = got[9:]
    rows_one = got[0].reshape(group_rows, model_width)
    weights_all = got[1].reshape(model_width, -1)
    attention_in = weights_all[:, : 3 * heads_here * HD].reshape(model_width, 3, heads_here * HD)
    attention_out = weights_all[:, 3 * heads_here * HD :].T
    query_blocks, key_seqs, value_seqs = (
        part.transpose(1, 0, 2).reshape(-1, rows, heads_here, HD)
        for part, rows in zip(got[2:5], (block_rows, SEQ, SEQ))
    )
    mixed = got[5]
    log_totals = got[6][:, :heads_here].reshape(block_count, block_rows, heads_here)
    log_totals = log_totals.transpose(0, 2, 1)
    hidden = got[7]
    scale_two = lax.rsqrt(jnp.mean(hidden * hidden, axis=-1, keepdims=True) + epsilon)
    rows_two = got[8].reshape(group_rows, model_width)
    normed_two = lax.dynamic_slice_in_dim(rows_two, offset, shard_rows, 0)
    key_positions = jnp.arange(SEQ, dtype=jnp.int32)

    def block_scores(block_index):
        seq_index = block_index // blocks_per_seq
        query_rows = query_blocks[block_index]
        key_rows = key_seqs[seq_index]
        raw_scores = (
            jnp.einsum("qhd,khd->hqk", query_rows, key_rows, preferred_element_type=jnp.float32)
            * score_scale
        )
        query_positions = block_index % blocks_per_seq * block_rows + jnp.arange(
            block_rows, dtype=jnp.int32
        )
        causal = query_positions[:, None] >= key_positions[None, :]
        return (
            jnp.where(causal[None], raw_scores, -jnp.inf),
            query_rows,
            key_rows,
            value_seqs[seq_index],
        )

    logits = jnp.dot(rows_two, router_weight, preferred_element_type=jnp.float32) + jnp.dot(
        previous_logits, logit_carry, precision=highest
    )
    chosen = jnp.take_along_axis(logits, routes, axis=1)
    gates = jax.nn.softmax(chosen, axis=-1)
    assigned, tokens_of = dispatch_tables(routes, NFFN, CAP)
    gate_table = jnp.concatenate([gates.reshape(-1), jnp.zeros((1,), jnp.float32)])[
        assigned
    ].reshape(NFFN, CAP)
    rows_in = swap(rows_two[tokens_of].reshape(NFFN, CAP, model_width))
    rows_in = rows_in.reshape(NFFN * CAP, model_width)
    gate_up = jnp.einsum("cd,kdf->kcf", rows_in, expert_in_rows, preferred_element_type=jnp.float32)
    gate_pre = gate_up[0]
    up_pre = gate_up[1]
    hidden_units = (jax.nn.silu(gate_pre) * up_pre).astype(jnp.bfloat16)
    expert_rows = jnp.einsum(
        "cf,df->cd", hidden_units, expert_out_t, preferred_element_type=jnp.float32
    )
    expert_rows = swap(expert_rows.astype(jnp.bfloat16).reshape(NFFN, CAP, model_width))
    expert_rows = expert_rows.astype(jnp.float32)
    weighted = (expert_rows * gate_table[:, :, None]).reshape(NFFN * CAP, model_width)
    routed = jnp.zeros((group_rows, model_width), jnp.float32).at[tokens_of].add(weighted)
    routed_own = lax.psum_scatter(
        routed.astype(jnp.bfloat16), "mp", scatter_dimension=0, tiled=True
    ).astype(jnp.float32)
    routes_own = lax.dynamic_slice_in_dim(routes, offset, shard_rows, 0)
    gates_own = lax.dynamic_slice_in_dim(gates, offset, shard_rows, 0)
    previous_own = lax.dynamic_slice_in_dim(previous_logits, offset, shard_rows, 0)
    normed_float = normed_two.astype(jnp.float32)
    mixing = constant_mix.astype(jnp.float32)
    constants = constant_values.astype(jnp.float32)
    mix_logits = jnp.dot(normed_two, constant_mix, preferred_element_type=jnp.float32).reshape(
        shard_rows, 2, 2
    )
    alphas = jax.nn.softmax(mix_logits, axis=-1)
    constant_rows = [
        alphas[:, 0, 0:1] * normed_float + alphas[:, 0, 1:2] * constants[0][None, :],
        alphas[:, 1, 0:1] * normed_float + alphas[:, 1, 1:2] * constants[1][None, :],
    ]
    first_value = local_values(routes_own[:, 0:1], normed_float, constant_rows)
    second_value = local_values(routes_own[:, 1:2], normed_float, constant_rows)
    local_rows = gates_own[:, 0:1] * first_value + gates_own[:, 1:2] * second_value
    output = (hidden + (routed_own + local_rows)).astype(jnp.bfloat16)
    grad_out = cotangent.astype(jnp.float32)
    grad_rows_all = lax.all_gather(cotangent, "mp", axis=0, tiled=True)
    slot_grads = grad_rows_all[tokens_of].reshape(NFFN, CAP, model_width).astype(jnp.float32)
    expert_grad = (slot_grads * gate_table[:, :, None]).astype(jnp.bfloat16)
    gate_slot = jnp.sum(slot_grads * expert_rows, axis=-1)
    out_grad = swap(expert_grad).reshape(NFFN * CAP, model_width)
    output_side_grad = jnp.einsum(
        "cf,cd->fd", hidden_units, out_grad, preferred_element_type=jnp.float32
    )
    units_grad = jnp.einsum(
        "cd,df->cf", out_grad, expert_out_t, preferred_element_type=jnp.float32
    )
    sigmoid_gate = jax.nn.sigmoid(gate_pre)
    gate_pre_grad = units_grad * up_pre * sigmoid_gate * (1.0 + gate_pre * (1.0 - sigmoid_gate))
    up_pre_grad = units_grad * gate_pre * sigmoid_gate
    pre_grads = jnp.stack([gate_pre_grad, up_pre_grad], axis=0).astype(jnp.bfloat16)
    input_side_grad = jnp.einsum(
        "cd,kcf->kdf", rows_in, pre_grads, preferred_element_type=jnp.float32
    )
    rows_grad = jnp.einsum(
        "kcf,kdf->cd", pre_grads, expert_in_rows, preferred_element_type=jnp.float32
    )
    rows_grad = swap(rows_grad.astype(jnp.bfloat16).reshape(NFFN, CAP, model_width))
    rows_grad = rows_grad.astype(jnp.float32)
    normed_part = (
        jnp.zeros((group_rows, model_width), jnp.float32)
        .at[tokens_of]
        .add(rows_grad.reshape(NFFN * CAP, model_width))
    )
    gate_part = (
        jnp.zeros((2 * group_rows + 1,), jnp.float32)
        .at[assigned]
        .add(gate_slot.reshape(-1))[:-1]
        .reshape(group_rows, 2)
    )
    normed_grad_moe, gate_grad_ffn = (
        lax.psum_scatter(normed_part, "mp", scatter_dimension=0, tiled=True),
        lax.psum_scatter(gate_part, "mp", scatter_dimension=0, tiled=True),
    )
    local_gate_grad = jnp.stack(
        [jnp.sum(grad_out * first_value, axis=-1), jnp.sum(grad_out * second_value, axis=-1)],
        axis=1,
    )
    gate_grad = gate_grad_ffn + local_gate_grad
    copy_weight = gates_own[:, 0:1] * (routes_own[:, 0:1] == NFFN + 1) + gates_own[:, 1:2] * (
        routes_own[:, 1:2] == NFFN + 1
    )
    normed_grad = normed_grad_moe + copy_weight * grad_out
    mix_grads = []
    values_grads = []
    for constant_index in range(2):
        expert_number = NFFN + 2 + constant_index
        route_weight = gates_own[:, 0:1] * (routes_own[:, 0:1] == expert_number) + gates_own[
            :, 1:2
        ] * (routes_own[:, 1:2] == expert_number)
        const_grad = route_weight * grad_out
        normed_grad = normed_grad + alphas[:, constant_index, 0:1] * const_grad
        alpha_grad = jnp.stack(
            [
                jnp.sum(const_grad * normed_float, axis=-1),
                jnp.sum(const_grad * constants[constant_index][None, :], axis=-1),
            ],
            axis=1,
        )
        values_grads.append(jnp.sum(alphas[:, constant_index, 1:2] * const_grad, axis=0))
        alpha_pair = alphas[:, constant_index]
        mix_grads.append(
            alpha_pair * (alpha_grad - jnp.sum(alpha_pair * alpha_grad, axis=-1, keepdims=True))
        )
    mix_grad = jnp.concatenate(mix_grads, axis=1)
    constant_mix_grad = jnp.einsum("td,tc->dc", normed_float, mix_grad, precision=highest)
    normed_grad = normed_grad + jnp.einsum("tc,dc->td", mix_grad, mixing, precision=highest)
    constant_values_grad = jnp.stack(values_grads, axis=0)
    chosen_grad = gates_own * (gate_grad - jnp.sum(gates_own * gate_grad, axis=-1, keepdims=True))
    expert_ids = jnp.arange(NEXP, dtype=jnp.int32)[None, :]
    logit_grad = chosen_grad[:, 0:1] * (routes_own[:, 0:1] == expert_ids) + chosen_grad[:, 1:2] * (
        routes_own[:, 1:2] == expert_ids
    )
    router_grad = jnp.einsum("td,te->de", normed_float, logit_grad, precision=highest)
    logit_carry_grad = jnp.einsum("tf,te->fe", previous_own, logit_grad, precision=highest)
    logits_grad = jnp.einsum("te,fe->tf", logit_grad, logit_carry, precision=highest)
    normed_grad = normed_grad + jnp.einsum(
        "te,de->td", logit_grad, router_weight.astype(jnp.float32), precision=highest
    )
    second_gain_grad, hidden_norm_grad = norm_back(hidden, scale_two, gain_two, normed_grad)
    hidden_grad = grad_out + hidden_norm_grad
    attended_grad = lax.all_gather(hidden_grad.astype(jnp.bfloat16), "mp", axis=0, tiled=True)
    output_weight_grad = jnp.einsum(
        "tf,td->fd", mixed, attended_grad, preferred_element_type=jnp.float32
    )
    mixed_grad = jnp.einsum(
        "td,fd->tf", attended_grad, attention_out, preferred_element_type=jnp.float32
    ).astype(jnp.bfloat16)
    mixed_grad_blocks = mixed_grad.reshape(block_count, block_rows, heads_here, HD)

    def attend_back(block_index):
        scores, query_rows, key_rows, value_rows = block_scores(block_index)
        out_grad_rows = mixed_grad_blocks[block_index]
        attention_weights = jnp.exp(scores - log_totals[block_index][:, :, None])
        weights_grad = jnp.einsum(
            "qhd,khd->hqk", out_grad_rows, value_rows, preferred_element_type=jnp.float32
        )
        inner_sum = jnp.sum(attention_weights * weights_grad, axis=-1, keepdims=True)
        score_grad = (attention_weights * (weights_grad - inner_sum)).astype(jnp.bfloat16)
        query_grad = (
            jnp.einsum("hqk,khd->qhd", score_grad, key_rows, preferred_element_type=jnp.float32)
            * score_scale
        )
        key_grad = (
            jnp.einsum("hqk,qhd->khd", score_grad, query_rows, preferred_element_type=jnp.float32)
            * score_scale
        )
        value_grad = jnp.einsum(
            "hqk,qhd->khd",
            attention_weights.astype(jnp.bfloat16),
            out_grad_rows,
            preferred_element_type=jnp.float32,
        )
        return (query_grad, key_grad, value_grad)

    query_grads, key_grads, value_grads = lax.map(
        attend_back, jnp.arange(block_count, dtype=jnp.int32)
    )
    query_grads = query_grads.reshape(group_rows, heads_here, HD)
    key_grads = (
        key_grads.reshape(sequences, blocks_per_seq, SEQ, heads_here, HD)
        .sum(axis=1)
        .reshape(group_rows, heads_here, HD)
    )
    value_grads = (
        value_grads.reshape(sequences, blocks_per_seq, SEQ, heads_here, HD)
        .sum(axis=1)
        .reshape(group_rows, heads_here, HD)
    )
    query_raw_grad = rotate_back(query_grads, cosine, sine_table).reshape(
        group_rows, heads_here * HD
    )
    key_raw_grad = rotate_back(key_grads, cosine, sine_table).reshape(group_rows, heads_here * HD)
    joint_grad = jnp.stack(
        [query_raw_grad, key_raw_grad, value_grads.reshape(group_rows, heads_here * HD)], axis=1
    ).astype(jnp.bfloat16)
    attention_in_grad = jnp.einsum(
        "td,tkf->dkf", rows_one, joint_grad, preferred_element_type=jnp.float32
    )
    normed_one_part = jnp.einsum(
        "tkf,dkf->td", joint_grad, attention_in, preferred_element_type=jnp.float32
    )
    normed_one_grad = lax.psum_scatter(
        normed_one_part.astype(jnp.bfloat16), "mp", scatter_dimension=0, tiled=True
    ).astype(jnp.float32)
    first_gain_grad, input_norm_grad = norm_back(tokens, scale_one, gain_one, normed_one_grad)
    input_grad = hidden_grad + input_norm_grad
    attention_in_own, attention_out_own = (
        lax.psum_scatter(attention_in_grad, "dp", scatter_dimension=0, tiled=True),
        lax.psum_scatter(output_weight_grad, "dp", scatter_dimension=1, tiled=True),
    )
    expert_in_grad = exchange_back(input_side_grad[None], 2)
    expert_out_grad = exchange_back(output_side_grad[None], 2)
    small_sums = lax.psum(
        (
            first_gain_grad,
            second_gain_grad,
            router_grad,
            logit_carry_grad,
            constant_mix_grad,
            constant_values_grad,
        ),
        ("dp", "mp"),
    )
    return (
        output,
        input_grad,
        logits_grad,
        attention_in_own,
        attention_out_own,
        expert_in_grad,
        expert_out_grad,
        small_sums[0],
        small_sums[1],
        small_sums[2],
        small_sums[3],
        small_sums[4],
        small_sums[5],
    )


def solution(mesh):
    in_specs = (
        P(("dp", "mp"), None),
        P("dp", None, "mp"),
        P("mp", "dp"),
        P(None, None, "dp", "mp"),
        P(None, "mp", "dp"),
        P(),
        P(),
        P(),
        P(),
        P(),
        P(),
        P("dp", None),
        P("dp", None),
        P(("dp", "mp"), None),
    )
    out_specs = (
        P(("dp", "mp"), None),
        P(("dp", "mp"), None),
        P(("dp", "mp"), None),
        P("dp", None, "mp"),
        P("mp", "dp"),
        P(None, None, "dp", "mp"),
        P(None, "mp", "dp"),
        P(),
        P(),
        P(),
        P(),
        P(),
        P(),
    )
    return jax.shard_map(
        per_device, mesh=mesh, in_specs=in_specs, out_specs=out_specs, check_vma=False
    )
```

```python
import functools
import numpy as np
import jax
import jax.numpy as jnp
from jax import lax
from jax.sharding import PartitionSpec as P
from jax.experimental import pallas as pl
from jax.experimental.pallas import tpu as pltpu

HD = 64
NFFN = 8
NEXP = 12
SEQ = 1024
CAP = 256
MP = 4
QUARTER = CAP // MP

epsilon = 1e-06
rope_base = 10000.0
highest = lax.Precision.HIGHEST
f32 = jnp.float32
bf16 = jnp.bfloat16
MESH = pl.DeviceIdType.MESH
VM = pl.BlockSpec(memory_space=pltpu.VMEM)
HB = pl.BlockSpec(memory_space=pl.ANY)
NT = (((1,), (1,)), ((), ()))
TN = (((0,), (0,)), ((), ()))


def flip(index, distance):
    out = index
    bit = 1
    while bit <= distance:
        if distance & bit:
            out = out + bit - 2 * bit * ((index // bit) % 2)
        bit *= 2
    return out


def dotf(a, b, dims=None):
    if dims is None:
        return jnp.dot(a, b, preferred_element_type=f32)
    return lax.dot_general(a, b, dims, preferred_element_type=f32)


def remote(src, dst, send, recv, **where):
    return pltpu.make_async_remote_copy(
        src_ref=src, dst_ref=dst, send_sem=send, recv_sem=recv, device_id=where, device_id_type=MESH
    )


def greet(mp_me, near, base):
    barrier = pltpu.get_barrier_semaphore()
    for k in range(1, MP):
        pl.semaphore_signal(barrier, inc=1, device_id={"mp": flip(mp_me, k)}, device_id_type=MESH)
    for k in range(1, NFFN):
        pl.semaphore_signal(
            barrier, inc=1, device_id={"dp": base + flip(near, k)}, device_id_type=MESH
        )
    pl.semaphore_wait(barrier, MP - 1 + NFFN - 1)


def rope_constants():
    half = HD // 2
    positions = np.arange(SEQ, dtype=np.float32)
    frequency = (rope_base ** (-np.arange(half, dtype=np.float32) / half)).astype(np.float32)
    angles = (positions[:, None] * frequency[None, :]).astype(np.float32)
    cosine, sine = np.cos(angles), np.sin(angles)
    return (
        np.concatenate([cosine, cosine], axis=1),
        np.concatenate([-sine, sine], axis=1),
    )


def swap_halves(x):
    half = HD // 2
    return jnp.concatenate([x[:, half:], x[:, :half]], axis=1)


class Gather:
    def __init__(self, ref, mp_me, send, recv):
        self.me, self.core, self.chip = mp_me, flip(mp_me, 1), flip(mp_me, 2)
        own = ref.at[mp_me]
        far = ref.at[self.chip]
        self.to_chip = remote(own, own, send.at[0], recv.at[0], mp=self.chip)
        self.to_core = remote(own, own, send.at[1], recv.at[1], mp=self.core)
        self.relay = remote(far, far, send.at[2], recv.at[2], mp=self.core)

    def start(self):
        self.to_chip.start()
        self.to_core.start()

    def forward(self):
        self.to_chip.wait_recv()
        self.relay.start()

    def finish(self):
        self.to_core.wait_recv()
        self.relay.wait_recv()
        self.to_chip.wait_send()
        self.to_core.wait_send()
        self.relay.wait_send()


def attention_kernel(
    inside,
    x_ref, gain1_ref, gain2_ref, cos_ref, sin_ref, wshard_ref, win_shard, wout_shard,
    rows1_ref, w_ref, q_ref, k_ref, v_ref, mixed_ref, lse_ref, hidden_ref, rows2_ref, *rest,
):
    if inside:
        win_ref, wout_ref, *rest = rest
    (part_ref, core_in, chip_out, chip_in, core_out,
     sends, recvs, wsend, wrecv, esend, erecv, local) = rest
    mp_me = lax.axis_index("mp")
    dp_me = lax.axis_index("dp")
    near = lax.rem(dp_me, NFFN)
    base = dp_me - near
    core, chip = flip(mp_me, 1), flip(mp_me, 2)
    rows = x_ref.shape[0]
    depth = w_ref.shape[1]
    greet(mp_me, near, base)

    tokens = x_ref[...].astype(f32)
    scale = lax.rsqrt(jnp.mean(tokens * tokens, axis=-1, keepdims=True) + epsilon)
    rows1_ref[mp_me] = (tokens * scale * gain1_ref[...]).astype(bf16)
    gather1 = Gather(rows1_ref, mp_me, sends.at[pl.ds(0, 3)], recvs.at[pl.ds(0, 3)])
    gather1.start()

    if inside:
        w_ref[near] = wshard_ref[...]
        own = w_ref.at[near]
        along = [
            remote(own, own, wsend.at[k], wrecv.at[k], dp=base + flip(near, k)) for k in (2, 4, 6)
        ]
        for copy in along:
            copy.start()
        mate = base + flip(near, 1)
        across = [remote(own, own, wsend.at[0], wrecv.at[0], dp=mate)]
        across[0].start()
        for k, copy in zip((2, 4, 6), along):
            copy.wait_recv()
            block = w_ref.at[flip(near, k)]
            onward = remote(block, block, wsend.at[k + 1], wrecv.at[k + 1], dp=mate)
            onward.start()
            across.append(onward)
        gather1.forward()
        for copy in across:
            copy.wait_recv()
        for copy in along + across:
            copy.wait_send()
        experts = []
        din = win_shard.shape[2]
        place = pl.ds(pl.multiple_of(near * din, din), din)
        for k in (6, 4, 7, 5, 2, 3, 1):
            peer = flip(near, k)
            for i, (src, dst) in enumerate(
                [(win_shard.at[peer], win_ref.at[:, place]), (wout_shard.at[peer], wout_ref.at[place])]
            ):
                experts.append(
                    remote(src, dst, esend.at[i, k], erecv.at[i, k], dp=base + peer)
                )
        for copy in experts:
            copy.start()
        mine = [
            pltpu.make_async_copy(win_shard.at[near], win_ref.at[:, place], local.at[0]),
            pltpu.make_async_copy(wout_shard.at[near], wout_ref.at[place], local.at[1]),
        ]
        for copy in mine:
            copy.start()
    else:
        w_ref[...] = wshard_ref[...]
        gather1.forward()
    gather1.finish()

    width = x_ref.shape[1]
    w_all = w_ref[...].reshape(width, w_ref.shape[2])
    heads = q_ref.shape[0]
    cols = heads * HD

    def project(i, carry):
        at = pl.ds(pl.multiple_of(i * rows, rows), rows)
        joint = dotf(rows1_ref[i], w_all[:, : 3 * cols])
        cosine, sine = cos_ref[at], sin_ref[at]
        for h in range(heads):
            query = joint[:, h * HD : (h + 1) * HD]
            key = joint[:, cols + h * HD : cols + (h + 1) * HD]
            q_ref[h, at] = (query * cosine + swap_halves(query) * sine).astype(bf16)
            k_ref[h, at] = (key * cosine + swap_halves(key) * sine).astype(bf16)
            v_ref[h, at] = joint[:, 2 * cols + h * HD : 2 * cols + (h + 1) * HD].astype(bf16)
        return carry

    lax.fori_loop(0, MP, project, 0)
    out_weight = w_all[:, 3 * cols :]

    to_core = [
        remote(core_out.at[j], core_in.at[j], sends.at[3 + j], recvs.at[3 + j], mp=core)
        for j in range(2)
    ]
    to_chip = remote(chip_out, chip_in, sends.at[5], recvs.at[5], mp=chip)

    def attend(step, carry):
        block = flip(mp_me, 3)
        block = jnp.where(step == 1, core, jnp.where(step == 2, chip, jnp.where(step == 3, mp_me, block)))
        at = pl.ds(pl.multiple_of(block * rows, rows), rows)
        row_ids = block * rows + lax.broadcasted_iota(jnp.int32, (rows, SEQ), 0)
        seen = row_ids >= lax.broadcasted_iota(jnp.int32, (rows, SEQ), 1)
        for h in range(heads):
            scores = dotf(q_ref[h, at], k_ref[h], NT) * HD**-0.5
            scores = jnp.where(seen, scores, -jnp.inf)
            peak = jnp.max(scores, axis=-1, keepdims=True)
            exponent = jnp.exp(scores - peak)
            total = jnp.sum(exponent, axis=-1, keepdims=True)
            probs = (exponent * (1.0 / total)).astype(bf16)
            mixed_ref[at, h * HD : (h + 1) * HD] = dotf(probs, v_ref[h]).astype(bf16)
            lse_ref[at, h : h + 1] = peak + jnp.log(total)
        part = dotf(mixed_ref[at], out_weight, NT)

        @pl.when(step == 0)
        def _():
            core_out[0] = part.astype(bf16)
            to_core[0].start()

        @pl.when(step == 1)
        def _():
            core_out[1] = part.astype(bf16)
            to_core[1].start()

        @pl.when(step == 2)
        def _():
            to_core[0].wait_recv()
            chip_out[...] = (part + core_in[0].astype(f32)).astype(bf16)
            to_chip.start()

        @pl.when(step == 3)
        def _():
            part_ref[...] = part

        return carry

    lax.fori_loop(0, MP, attend, 0)
    to_core[1].wait_recv()
    partial = part_ref[...] + core_in[1].astype(f32)
    to_chip.wait_recv()
    hidden = x_ref[...].astype(f32) + (partial + chip_in[...].astype(f32))
    hidden_ref[...] = hidden
    scale2 = lax.rsqrt(jnp.mean(hidden * hidden, axis=-1, keepdims=True) + epsilon)
    rows2_ref[mp_me] = (hidden * scale2 * gain2_ref[...]).astype(bf16)
    gather2 = Gather(rows2_ref, mp_me, sends.at[pl.ds(6, 3)], recvs.at[pl.ds(6, 3)])
    gather2.start()
    for copy in to_core + [to_chip]:
        copy.wait_send()
    gather2.forward()
    gather2.finish()
    if inside:
        for copy in experts:
            copy.wait_recv()
        for copy in experts:
            copy.wait_send()
        for copy in mine:
            copy.wait()


def attention(x, gain1, gain2, wshard, win, wout, groups):
    rows, width = x.shape
    cos, sin = rope_constants()
    inside = groups == 1
    cols = wshard.shape[-1]
    depth = width // NFFN
    hidden_cols = win.shape[-1]
    heads = cols // 4 // HD
    sd = jax.ShapeDtypeStruct
    outs = [
        sd((MP, rows, width), bf16),
        sd((NFFN, depth, cols), bf16),
        sd((heads, SEQ, HD), bf16),
        sd((heads, SEQ, HD), bf16),
        sd((heads, SEQ, HD), bf16),
        sd((SEQ, heads * HD), bf16),
        sd((SEQ, 128), f32),
        sd((rows, width), f32),
        sd((MP, rows, width), bf16),
    ]
    specs = [VM] * len(outs)
    if inside:
        outs += [sd((2, width, hidden_cols), bf16), sd((width, hidden_cols), bf16)]
        specs += [HB, HB]
    else:
        wshard = wshard.reshape(NFFN, depth, cols)
    dma = pltpu.SemaphoreType.DMA
    return pl.pallas_call(
        functools.partial(attention_kernel, inside),
        out_shape=outs,
        in_specs=[VM] * 6 + [HB, HB],
        out_specs=specs,
        scratch_shapes=[
            pltpu.VMEM((rows, width), f32),
            pltpu.VMEM((2, rows, width), bf16),
            pltpu.VMEM((rows, width), bf16),
            pltpu.VMEM((rows, width), bf16),
            pltpu.VMEM((2, rows, width), bf16),
            dma((9,)), dma((9,)),
            dma((8,)), dma((8,)),
            dma((2, 8)), dma((2, 8)),
            dma((2,)),
        ],
        compiler_params=pltpu.CompilerParams(
            collective_id=0, has_side_effects=True, vmem_limit_bytes=56 * 2**20
        ),
        name="attention_forward",
    )(x, gain1, gain2, jnp.asarray(cos), jnp.asarray(sin), wshard, win, wout)


def pack3(value):
    high = value.astype(bf16).astype(f32)
    rest = value - high
    mid = rest.astype(bf16).astype(f32)
    low = (rest - mid).astype(bf16).astype(f32)
    lane = lax.broadcasted_iota(jnp.int32, (value.shape[0], 128), 1)
    return jnp.where(
        lane == 0, high, jnp.where(lane == 1, mid, jnp.where(lane == 2, low, 0.0))
    ).astype(bf16)


def unpack3(parts):
    return jnp.sum(parts.astype(f32), axis=-1, keepdims=True)


def exact(left, right, dims=None):
    high = left.astype(bf16)
    rest = left - high.astype(f32)
    mid = rest.astype(bf16)
    low = (rest - mid.astype(f32)).astype(bf16)
    return dotf(high, right, dims) + (dotf(mid, right, dims) + dotf(low, right, dims))


class Scatter:
    def __init__(self, mp_me, core_out, core_in, chip_out, chip_in, send, recv):
        self.me, self.core, self.chip = mp_me, flip(mp_me, 1), flip(mp_me, 2)
        self.core_out, self.core_in = core_out, core_in
        self.chip_out, self.chip_in = chip_out, chip_in
        self.to_core = [
            remote(core_out.at[j], core_in.at[j], send.at[j], recv.at[j], mp=self.core)
            for j in range(2)
        ]
        self.to_chip = remote(chip_out, chip_in, send.at[2], recv.at[2], mp=self.chip)

    def run(self, blocks):
        for j, block in enumerate((flip(self.me, 3), self.core)):
            self.core_out[j] = blocks(block).astype(bf16)
            self.to_core[j].start()
        term = blocks(self.chip)
        self.to_core[0].wait_recv()
        self.chip_out[...] = (term + self.core_in[0].astype(f32)).astype(bf16)
        self.to_chip.start()
        term = blocks(self.me)
        self.to_core[1].wait_recv()
        term = term + self.core_in[1].astype(f32)
        self.to_chip.wait_recv()
        return term + self.chip_in[...].astype(f32)

    def drain(self):
        for copy in self.to_core + [self.to_chip]:
            copy.wait_send()


def expert_kernel(
    rows2_ref, hidden_ref, cot_ref, gain2_ref, router_ref, mix_ref, values_ref, prior_ref,
    carry_ref, previous_ref, routes_ref, routes_own_ref, prior_own_ref, win_ref, wout_ref,
    residual_ref, hgrad_ref, agrad_ref, lgrad_ref, small_ref, carry_grad_ref, pick_ref, gate_ref,
    outq_ref, dwin_ref, dwout_ref,
    cot_all, place_ref, gates_ref, msgx, msgc, xs, cs, pre_ref, units_ref, pgrad_ref,
    ocore_out, ocore_in, ochip_out, ochip_in,
    gpart_ref, gcore_out, gcore_in, gchip_out, gchip_in, gret,
    score_out, score_in, ncore_out, ncore_in, nchip_out, nchip_in,
    csend, crecv, xsend, xrecv, dsend, drecv, xgs, xgr, cgs, cgr, osend, orecv,
    gsend, grecv, rsend, rrecv, ssend, srecv, nsend, nrecv,
):
    mp_me = lax.axis_index("mp")
    dp_me = lax.axis_index("dp")
    near = lax.rem(dp_me, NFFN)
    base = dp_me - near
    core, chip = flip(mp_me, 1), flip(mp_me, 2)
    far = flip(mp_me, 3)
    rows, width = cot_ref.shape
    everyone = MP * rows
    greet(mp_me, near, base)
    cot_all[mp_me] = cot_ref[...]
    gather = Gather(cot_all, mp_me, csend, crecv)
    gather.start()

    tokens = rows2_ref[...].reshape(everyone, width)
    logits = dotf(router_ref[...], tokens, NT) + prior_ref[...]
    ids = lax.broadcasted_iota(jnp.int32, (16, everyone), 0)
    chosen = (ids == routes_ref[0:1]) | (ids == routes_ref[1:2])
    masked = jnp.where(chosen, logits, -jnp.inf)
    exponent = jnp.exp(masked - jnp.max(masked, axis=0, keepdims=True))
    gates_ref[...] = exponent / jnp.sum(exponent, axis=0, keepdims=True)
    earlier = lax.broadcasted_iota(jnp.int32, (everyone, everyone), 0) < lax.broadcasted_iota(
        jnp.int32, (everyone, everyone), 1
    )
    counts = dotf(
        jnp.where(chosen, 1.0, 0.0).astype(bf16), jnp.where(earlier, 1.0, 0.0).astype(bf16)
    )
    place_ref[...] = jnp.where(chosen, counts, -1.0)
    wanted = (lax.broadcasted_iota(jnp.int32, (QUARTER, everyone), 0) + QUARTER * mp_me).astype(f32)

    def x_copy(k):
        return remote(
            msgx.at[lax.rem(near + k, NFFN)], xs.at[near, mp_me], xsend.at[k], xrecv.at[k],
            dp=base + lax.rem(near + k, NFFN),
        )

    def c_copy(k):
        return remote(
            msgc.at[lax.rem(near + k, NFFN)], cs.at[near, mp_me], dsend.at[k], drecv.at[k],
            dp=base + lax.rem(near + k, NFFN),
        )

    def send_x(i, carry):
        k = lax.rem(i + 1, NFFN)
        expert = lax.rem(near + k, NFFN)
        pick = wanted == place_ref[pl.ds(expert, 1)]
        onehot = jnp.where(pick, 1.0, 0.0).astype(bf16)
        gate = jnp.sum(
            jnp.where(pick, gates_ref[pl.ds(expert, 1)], 0.0), axis=1, keepdims=True
        )
        pick_ref[expert] = onehot
        gate_ref[expert] = jnp.broadcast_to(gate, (QUARTER, 128))
        block = dotf(onehot, tokens).astype(bf16)
        extra = pack3(gate)
        msgx[expert, :, :width] = block
        msgx[expert, :, width:] = extra

        @pl.when(k > 0)
        def _():
            x_copy(k).start()

        @pl.when(k == 0)
        def _():
            xs[near, mp_me] = msgx[expert]

        return carry

    lax.fori_loop(0, NFFN, send_x, 0)
    gather.forward()
    gather.finish()

    def send_c(i, carry):
        k = lax.rem(i + 1, NFFN)
        expert = lax.rem(near + k, NFFN)
        msgc[expert] = dotf(pick_ref[expert], cot_all[...].reshape(everyone, width)).astype(bf16)

        @pl.when(k > 0)
        def _():
            c_copy(k).start()

        @pl.when(k == 0)
        def _():
            cs[near, mp_me] = msgc[expert]

        return carry

    lax.fori_loop(0, NFFN, send_c, 0)

    def source(k):
        return lax.rem(near - k + NFFN, NFFN)

    def scatter_at(k, bufs, send, recv):
        core_out, core_in, chip_out, chip_in = bufs
        slot = lax.rem(k, 3)
        return Scatter(
            mp_me, core_out.at[slot], core_in.at[k], chip_out.at[slot], chip_in.at[k],
            send.at[k], recv.at[k],
        )

    obufs = (ocore_out, ocore_in, ochip_out, ochip_in)
    gbufs = (gcore_out, gcore_in, gchip_out, gchip_in)
    hidden_cols = wout_ref.shape[1]

    def forward_step(i, carry):
        @pl.when(i < NFFN)
        def _():
            @pl.when(i > 0)
            def _():
                x_copy(i).wait_recv()

            Gather(xs.at[source(i)], mp_me, xgs.at[i], xgr.at[i]).start()

        @pl.when((i >= 1) & (i < NFFN + 1))
        def _():
            k = i - 1
            Gather(xs.at[source(k)], mp_me, xgs.at[k], xgr.at[k]).forward()

        @pl.when((i >= 2) & (i < NFFN + 2))
        def _():
            k = i - 2
            src = source(k)
            at = pl.ds(pl.multiple_of(src * CAP, CAP), CAP)
            Gather(xs.at[src], mp_me, xgs.at[k], xgr.at[k]).finish()
            x = xs[src].reshape(CAP, width + 128)[:, :width]
            gate_pre = dotf(x, win_ref[0])
            up_pre = dotf(x, win_ref[1])
            pre_ref[0, at] = gate_pre
            pre_ref[1, at] = up_pre
            units = (gate_pre * jax.nn.sigmoid(gate_pre) * up_pre).astype(bf16)
            units_ref[at] = units
            slot = lax.rem(k, 3)
            gpart_ref[slot, :, :, :width] = dotf(units, wout_ref[...], NT).reshape(
                MP, QUARTER, width
            )
            ocore_out[slot, 0] = gpart_ref[slot, far, :, :width].astype(bf16)
            ocore_out[slot, 1] = gpart_ref[slot, core, :, :width].astype(bf16)
            trip = scatter_at(k, obufs, osend, orecv)
            trip.to_core[0].start()
            trip.to_core[1].start()

        @pl.when((i >= 3) & (i < NFFN + 3))
        def _():
            k = i - 3
            trip = scatter_at(k, obufs, osend, orecv)
            trip.to_core[0].wait_recv()
            ochip_out[lax.rem(k, 3)] = (
                gpart_ref[lax.rem(k, 3), chip, :, :width] + ocore_in[k, 0].astype(f32)
            ).astype(bf16)
            trip.to_chip.start()

        @pl.when(i >= 4)
        def _():
            k = i - 4
            trip = scatter_at(k, obufs, osend, orecv)
            trip.to_core[1].wait_recv()
            trip.to_chip.wait_recv()
            outq_ref[source(k)] = (
                gpart_ref[lax.rem(k, 3), mp_me, :, :width]
                + ocore_in[k, 1].astype(f32)
                + ochip_in[k].astype(f32)
            ).astype(bf16)
            trip.drain()

        return carry

    lax.fori_loop(0, NFFN + 4, forward_step, 0)

    def g_copy(k):
        return remote(
            msgx.at[lax.rem(near + k, NFFN)], gret.at[near], rsend.at[k], rrecv.at[k], dp=base + source(k)
        )

    def seal(ref, index, total):
        ref[index + (slice(None), slice(0, width))] = total[:, :width].astype(bf16)
        ref[index + (slice(None), slice(width, None))] = pack3(unpack3(total[:, width:]))

    def backward_step(i, carry):
        @pl.when(i < NFFN)
        def _():
            @pl.when(i > 0)
            def _():
                c_copy(i).wait_recv()

            Gather(cs.at[source(i)], mp_me, cgs.at[i], cgr.at[i]).start()

        @pl.when((i >= 1) & (i < NFFN + 1))
        def _():
            k = i - 1
            Gather(cs.at[source(k)], mp_me, cgs.at[k], cgr.at[k]).forward()

        @pl.when((i >= 2) & (i < NFFN + 2))
        def _():
            k = i - 2
            src = source(k)
            at = pl.ds(pl.multiple_of(src * CAP, CAP), CAP)
            Gather(cs.at[src], mp_me, cgs.at[k], cgr.at[k]).finish()
            gate = unpack3(xs[src].reshape(CAP, width + 128)[:, width:])
            c = cs[src].reshape(CAP, width)
            gate_pre = pre_ref[0, at]
            up_pre = pre_ref[1, at]
            raw = dotf(c, wout_ref[...])
            score = jnp.sum(units_ref[at].astype(f32) * raw, axis=1, keepdims=True)
            units_grad = raw * gate
            cs[src] = (c.astype(f32) * gate).astype(bf16).reshape(MP, QUARTER, width)
            sig = jax.nn.sigmoid(gate_pre)
            gate_grad = (units_grad * up_pre * sig * (1.0 + gate_pre * (1.0 - sig))).astype(bf16)
            up_grad = (units_grad * (gate_pre * sig)).astype(bf16)
            pgrad_ref[at, :hidden_cols] = gate_grad
            pgrad_ref[at, hidden_cols:] = up_grad
            slot = lax.rem(k, 3)
            back = dotf(gate_grad, win_ref[0], NT) + dotf(up_grad, win_ref[1], NT)
            gpart_ref[slot, :, :, :width] = back.reshape(MP, QUARTER, width)
            gpart_ref[slot, :, :, width:] = pack3(score).astype(f32).reshape(MP, QUARTER, 128)
            seal(gcore_out, (slot, 0), gpart_ref[slot, far])
            seal(gcore_out, (slot, 1), gpart_ref[slot, core])
            trip = scatter_at(k, gbufs, gsend, grecv)
            trip.to_core[0].start()
            trip.to_core[1].start()

        @pl.when((i >= 3) & (i < NFFN + 3))
        def _():
            k = i - 3
            trip = scatter_at(k, gbufs, gsend, grecv)
            trip.to_core[0].wait_recv()
            seal(gchip_out, (lax.rem(k, 3),), gpart_ref[lax.rem(k, 3), chip] + gcore_in[k, 0].astype(f32))
            trip.to_chip.start()

        @pl.when(i >= 4)
        def _():
            k = i - 4
            trip = scatter_at(k, gbufs, gsend, grecv)
            trip.to_core[1].wait_recv()
            trip.to_chip.wait_recv()
            total = (
                gpart_ref[lax.rem(k, 3), mp_me]
                + gcore_in[k, 1].astype(f32)
                + gchip_in[k].astype(f32)
            )
            trip.drain()

            @pl.when(k > 0)
            def _():
                x_copy(k).wait_send()

            seal(msgx, (lax.rem(near + k, NFFN),), total)

            @pl.when(k > 0)
            def _():
                g_copy(k).start()

            @pl.when(k == 0)
            def _():
                gret[near] = msgx[near]

        return carry

    lax.fori_loop(0, NFFN + 4, backward_step, 0)

    def weights_step(j, carry):
        at = pl.ds(pl.multiple_of(j * 128, 128), 128)
        x = xs[:, :, :, at].reshape(NFFN * CAP, 128)
        both = dotf(x, pgrad_ref[...], TN)
        dwin_ref[0, at] = both[:, :hidden_cols].astype(bf16)
        dwin_ref[1, at] = both[:, hidden_cols:].astype(bf16)
        c = cs[:, :, :, at].reshape(NFFN * CAP, 128)
        dwout_ref[at] = dotf(c, units_ref[...], TN).astype(bf16)
        return carry

    lax.fori_loop(0, width // 128, weights_step, 0)

    def returned(k, carry):
        g_copy(k).wait_recv()
        return carry

    lax.fori_loop(1, NFFN, returned, 0)
    ret = gret[...].reshape(NFFN * QUARTER, width + 128)
    slots = unpack3(ret[:, width:])
    picks = pick_ref[...].reshape(NFFN * QUARTER, everyone)
    for expert in range(NFFN):
        at = slice(expert * QUARTER, (expert + 1) * QUARTER)
        row = jnp.sum(picks[at].astype(f32) * slots[at], axis=0, keepdims=True)
        for q in range(MP):
            score_out[q, expert : expert + 1] = row[:, q * rows : (q + 1) * rows]
    score_copies = [
        remote(score_out.at[flip(mp_me, k)], score_in.at[k], ssend.at[k], srecv.at[k], mp=flip(mp_me, k))
        for k in range(1, MP)
    ]
    for copy in score_copies:
        copy.start()

    def grad_block(q):
        at = pl.ds(pl.multiple_of(q * rows, rows), rows)
        return dotf(
            pick_ref[:, :, at].reshape(NFFN * QUARTER, rows), ret[:, :width], TN
        )

    trip = Scatter(mp_me, ncore_out, ncore_in, nchip_out, nchip_in, nsend, nrecv)
    normed_grad = trip.run(grad_block)

    n_bf = rows2_ref[mp_me]
    n = n_bf.astype(f32)
    cot = cot_ref[...].astype(f32)
    hidden = hidden_ref[...]
    lane = lax.broadcasted_iota(jnp.int32, (rows, 128), 1)
    own_logits = dotf(n_bf, router_ref[...], NT) + prior_own_ref[...]
    lane16 = lax.broadcasted_iota(jnp.int32, (rows, 16), 1)
    own_chosen = (lane16 == routes_own_ref[:, 0:1]) | (lane16 == routes_own_ref[:, 1:2])
    own_masked = jnp.where(own_chosen, own_logits, -jnp.inf)
    own_exp = jnp.exp(own_masked - jnp.max(own_masked, axis=1, keepdims=True))
    own_gates = own_exp / jnp.sum(own_exp, axis=1, keepdims=True)
    copy_gate = own_gates[:, NFFN + 1 : NFFN + 2]
    const_gates = [own_gates[:, NFFN + 2 : NFFN + 3], own_gates[:, NFFN + 3 : NFFN + 4]]
    mix_logits = dotf(n_bf, mix_ref[...], NT)
    with_normed = jnp.sum(cot * n, axis=1, keepdims=True)
    residual = hidden + copy_gate * n
    normed_grad = normed_grad + copy_gate * cot
    local_scores = jnp.where(lane == NFFN + 1, with_normed, 0.0)
    mix_grads = jnp.zeros((rows, 128), f32)
    for c in range(2):
        first, second = mix_logits[:, 2 * c : 2 * c + 1], mix_logits[:, 2 * c + 1 : 2 * c + 2]
        top = jnp.maximum(first, second)
        first, second = jnp.exp(first - top), jnp.exp(second - top)
        share = 1.0 / (first + second)
        first, second = first * share, second * share
        constant = values_ref[c : c + 1].astype(f32)
        with_constant = jnp.sum(cot * constant, axis=1, keepdims=True)
        gate = const_gates[c]
        residual = residual + gate * (first * n + second * constant)
        local_scores = jnp.where(
            lane == NFFN + 2 + c, first * with_normed + second * with_constant, local_scores
        )
        normed_grad = normed_grad + (first * gate) * cot
        small_ref[20 + c : 21 + c] = jnp.sum((second * gate) * cot, axis=0, keepdims=True)
        grad_first, grad_second = gate * with_normed, gate * with_constant
        mean = first * grad_first + second * grad_second
        mix_grads = jnp.where(lane == 2 * c, first * (grad_first - mean), mix_grads)
        mix_grads = jnp.where(lane == 2 * c + 1, second * (grad_second - mean), mix_grads)
    residual_ref[...] = residual

    for copy in score_copies:
        copy.wait_recv()
    ffn_scores = (score_out[mp_me] + score_in[1]) + (score_in[2] + score_in[3])
    scores = local_scores.T[:16] + jnp.concatenate([ffn_scores, jnp.zeros((8, rows), f32)], axis=0)
    own_at = pl.ds(pl.multiple_of(mp_me * rows, rows), rows)
    gates_t = gates_ref[:, own_at]
    logit_grad = gates_t * (scores - jnp.sum(gates_t * scores, axis=0, keepdims=True))
    lgrad_ref[...] = lax.dot_general(
        carry_ref[...], logit_grad, (((1,), (0,)), ((), ())),
        preferred_element_type=f32, precision=highest,
    )
    carry_grad_ref[...] = lax.dot_general(
        previous_ref[...], logit_grad, NT, preferred_element_type=f32, precision=highest
    )
    stacked = jnp.concatenate([logit_grad, mix_grads.T[:16]], axis=0)
    heads = jnp.concatenate([router_ref[...], mix_ref[...]], axis=0)
    feature_grads = exact(stacked, n_bf)
    small_ref[0:20] = feature_grads[0:20]
    normed_grad = normed_grad + exact(stacked, heads, TN)
    scale = lax.rsqrt(jnp.mean(hidden * hidden, axis=-1, keepdims=True) + epsilon)
    scaled = hidden * scale
    small_ref[22:23] = jnp.sum(normed_grad * scaled, axis=0, keepdims=True)
    small_ref[23:24] = jnp.zeros((1, width), f32)
    weighted = normed_grad * gain2_ref[...]
    hidden_grad = cot + scale * (
        weighted - scaled * jnp.mean(weighted * scaled, axis=-1, keepdims=True)
    )
    hgrad_ref[...] = hidden_grad
    agrad_ref[...] = hidden_grad.astype(bf16)

    trip.drain()
    for copy in score_copies:
        copy.wait_send()

    def drain(k, carry):
        c_copy(k).wait_send()
        g_copy(k).wait_send()
        return carry

    lax.fori_loop(1, NFFN, drain, 0)


def experts(
    rows2, hidden, cot, gain2, router_t, mix_t, values, prior_t, carry, previous_t, routes_t,
    routes_own, prior_own, win, wout,
):
    rows, width = cot.shape
    everyone = MP * rows
    cols = wout.shape[1]
    sd = jax.ShapeDtypeStruct
    vm = pltpu.VMEM
    dma = pltpu.SemaphoreType.DMA
    outs = [
        sd((rows, width), f32),
        sd((rows, width), f32),
        sd((rows, width), bf16),
        sd((16, rows), f32),
        sd((24, width), f32),
        sd((16, 16), f32),
        sd((NFFN, QUARTER, everyone), bf16),
        sd((NFFN, QUARTER, 128), f32),
        sd((NFFN, QUARTER, width), bf16),
        sd((2, width, cols), bf16),
        sd((width, cols), bf16),
    ]
    wide = width + 128
    return pl.pallas_call(
        expert_kernel,
        out_shape=outs,
        in_specs=[VM] * 15,
        out_specs=[VM] * len(outs),
        scratch_shapes=[
            vm((MP, rows, width), bf16),
            vm((16, everyone), f32),
            vm((16, everyone), f32),
            vm((NFFN, QUARTER, wide), bf16),
            vm((NFFN, QUARTER, width), bf16),
            vm((NFFN, MP, QUARTER, wide), bf16),
            vm((NFFN, MP, QUARTER, width), bf16),
            vm((2, NFFN * CAP, cols), f32),
            vm((NFFN * CAP, cols), bf16),
            vm((NFFN * CAP, 2 * cols), bf16),
            vm((3, 2, QUARTER, width), bf16),
            vm((NFFN, 2, QUARTER, width), bf16),
            vm((3, QUARTER, width), bf16),
            vm((NFFN, QUARTER, width), bf16),
            vm((3, MP, QUARTER, wide), f32),
            vm((3, 2, QUARTER, wide), bf16),
            vm((NFFN, 2, QUARTER, wide), bf16),
            vm((3, QUARTER, wide), bf16),
            vm((NFFN, QUARTER, wide), bf16),
            vm((NFFN, QUARTER, wide), bf16),
            vm((MP, 8, rows), f32),
            vm((MP, 8, rows), f32),
            vm((2, rows, width), bf16),
            vm((2, rows, width), bf16),
            vm((rows, width), bf16),
            vm((rows, width), bf16),
            dma((3,)), dma((3,)),
            dma((8,)), dma((8,)),
            dma((8,)), dma((8,)),
            dma((8, 3)), dma((8, 3)),
            dma((8, 3)), dma((8, 3)),
            dma((8, 3)), dma((8, 3)),
            dma((8, 3)), dma((8, 3)),
            dma((8,)), dma((8,)),
            dma((4,)), dma((4,)),
            dma((3,)), dma((3,)),
        ],
        compiler_params=pltpu.CompilerParams(
            collective_id=1, has_side_effects=True, vmem_limit_bytes=60 * 2**20
        ),
        name="experts",
    )(
        rows2, hidden, cot, gain2, router_t, mix_t, values, prior_t, carry, previous_t, routes_t,
        routes_own, prior_own, win, wout,
    )


def back_kernel(
    inside,
    agrad_ref, hgrad_ref, x_ref, gain1_ref, cos_ref, sin_ref, rows1_ref, w_ref, q_ref, k_ref, v_ref,
    mixed_ref, lse_ref, pick_ref, gate_ref, residual_ref, outq_ref, small_ref, carry_ref,
    dwin_ref, dwout_ref,
    output_ref, xgrad_ref, wgrad_ref, sums_ref, first_ref, *rest,
):
    if inside:
        dwin_own, dwout_own, *rest = rest
    (agrad_all, mgrad_ref, joint_ref, key_acc, value_acc, grads_ref, wsend_ref, wrecv_ref,
     ret_ref, ocore_out, ocore_in, ochip_out, ochip_in, xcore_out, xcore_in, xchip_out, xchip_in,
     sum_out, sum_in, first_mp, first_dp, first_out,
     asend, arecv, osend, orecv, esend, erecv, local, rsend, rrecv, xsend, xrecv, wsend, wrecv,
     ssend, srecv, fsend, frecv) = rest
    mp_me = lax.axis_index("mp")
    dp_me = lax.axis_index("dp")
    near = lax.rem(dp_me, NFFN)
    base = dp_me - near
    rows, width = agrad_ref.shape
    everyone = MP * rows
    heads = q_ref.shape[0]
    cols = heads * HD
    greet(mp_me, near, base)

    agrad_all[mp_me] = agrad_ref[...]
    gather = Gather(agrad_all, mp_me, asend, arecv)
    gather.start()
    returns = [
        remote(outq_ref.at[flip(near, k)], ret_ref.at[near], osend.at[k], orecv.at[k],
               dp=base + flip(near, k))
        for k in range(1, NFFN)
    ]
    for copy in returns:
        copy.start()
    ret_ref[near] = outq_ref[near]

    sum_out[0, 0:24] = small_ref[...]
    sum_out[0, 24:40] = jnp.zeros((16, width), f32)
    sum_out[0, 24:40, 0:16] = carry_ref[...]
    places = [{"mp": flip(mp_me, 1)}, {"mp": flip(mp_me, 2)}] + [
        {"dp": base + flip(near, k)} for k in (1, 2, 4)
    ]
    stages = [
        remote(sum_out.at[j], sum_in.at[j], ssend.at[j], srecv.at[j], **where)
        for j, where in enumerate(places)
    ]

    def stage(j):
        if j > 0:
            stages[j - 1].wait_recv()
            total = sum_out[j - 1] + sum_in[j - 1]
            if j == len(stages):
                sums_ref[...] = total
                return
            sum_out[j] = total
        stages[j].start()

    stage(0)
    moved = []
    if inside:
        din = dwin_own.shape[2]
        for k in (6, 4, 7, 5, 2, 3, 1):
            peer = flip(near, k)
            place = pl.ds(pl.multiple_of(peer * din, din), din)
            moved.append(
                remote(dwin_ref.at[:, place], dwin_own.at[near], esend.at[0, k], erecv.at[0, k],
                       dp=base + peer)
            )
            moved.append(
                remote(dwout_ref.at[place], dwout_own.at[near], esend.at[1, k], erecv.at[1, k],
                       dp=base + peer)
            )
        place = pl.ds(pl.multiple_of(near * din, din), din)
        mine = [
            pltpu.make_async_copy(dwin_ref.at[:, place], dwin_own.at[near], local.at[0]),
            pltpu.make_async_copy(dwout_ref.at[place], dwout_own.at[near], local.at[1]),
        ]
        for copy in moved + mine:
            copy.start()
    gather.forward()
    stage(1)
    gather.finish()

    w_all = w_ref[...].reshape(width, w_ref.shape[2])
    out_weight = w_all[:, 3 * cols :]
    for i in range(MP):
        mgrad_ref[i * rows : (i + 1) * rows] = dotf(agrad_all[i], out_weight).astype(bf16)
    grads_ref[:, 3 * cols :] = dotf(agrad_all[...].reshape(everyone, width), mixed_ref[...], TN)

    combine = Scatter(mp_me, ocore_out, ocore_in, ochip_out, ochip_in, rsend, rrecv)

    def out_block(q):
        at = pl.ds(pl.multiple_of(q * rows, rows), rows)
        weighted = (ret_ref[...].astype(f32) * gate_ref[:, :, 0:1]).astype(bf16)
        return dotf(
            pick_ref[:, :, at].reshape(NFFN * QUARTER, rows),
            weighted.reshape(NFFN * QUARTER, width), TN,
        )

    def head_back(h):
        lanes = slice(h * HD, (h + 1) * HD)
        for b in range(MP):
            at = slice(b * rows, (b + 1) * rows)
            seen = (b + 1) * rows
            query = q_ref[h, at]
            keys = k_ref[h, :seen]
            out_grad = mgrad_ref[at, lanes]
            scores = dotf(query, keys, NT) * HD**-0.5
            allowed = b * rows + lax.broadcasted_iota(
                jnp.int32, (rows, seen), 0
            ) >= lax.broadcasted_iota(jnp.int32, (rows, seen), 1)
            probs = jnp.where(allowed, jnp.exp(scores - lse_ref[at, h : h + 1]), 0.0)
            probs_grad = dotf(out_grad, v_ref[h, :seen], NT)
            inner = jnp.sum(probs * probs_grad, axis=1, keepdims=True)
            score_grad = (probs * (probs_grad - inner)).astype(bf16)
            query_grad = dotf(score_grad, keys) * HD**-0.5
            joint_ref[at, lanes] = (
                query_grad * cos_ref[at] - swap_halves(query_grad) * sin_ref[at]
            ).astype(bf16)
            key_grad = dotf(score_grad, query, TN) * HD**-0.5
            value_grad = dotf(probs.astype(bf16), out_grad, TN)
            if b == 0:
                key_acc[...] = jnp.zeros_like(key_acc)
                value_acc[...] = jnp.zeros_like(value_acc)
            key_acc[:seen] += key_grad
            value_acc[:seen] += value_grad
        key_grad = key_acc[...]
        joint_ref[:, cols + h * HD : cols + (h + 1) * HD] = (
            key_grad * cos_ref[...] - swap_halves(key_grad) * sin_ref[...]
        ).astype(bf16)
        joint_ref[:, 2 * cols + h * HD : 2 * cols + (h + 1) * HD] = value_acc[...].astype(bf16)

    for h in range(heads):
        head_back(h)
        if h == 0:
            stage(2)
            for copy in returns:
                copy.wait_recv()
            for j, q in enumerate((flip(mp_me, 3), flip(mp_me, 1))):
                ocore_out[j] = out_block(q).astype(bf16)
                combine.to_core[j].start()
            combine.to_core[0].wait_recv()
            ochip_out[...] = (
                out_block(combine.chip) + ocore_in[0].astype(f32)
            ).astype(bf16)
            combine.to_chip.start()
        if h == min(1, heads - 1):
            stage(3)
    combine.to_core[1].wait_recv()
    combine.to_chip.wait_recv()
    routed = out_block(mp_me) + ocore_in[1].astype(f32) + ochip_in[...].astype(f32)
    output_ref[...] = (residual_ref[...] + routed).astype(bf16)

    depth = width // NFFN
    grads_ref[:, : 3 * cols] = dotf(
        rows1_ref[...].reshape(everyone, width), joint_ref[...], TN
    )
    if inside:
        for p in range(NFFN):
            wsend_ref[p] = grads_ref[p * depth : (p + 1) * depth].astype(bf16)
        wcopies = [
            remote(wsend_ref.at[flip(near, k)], wrecv_ref.at[near], wsend.at[k], wrecv.at[k],
                   dp=base + flip(near, k))
            for k in (6, 4, 7, 5, 2, 3, 1)
        ]
        for copy in wcopies:
            copy.start()
        wrecv_ref[near] = wsend_ref[near]
    else:
        wgrad_ref[...] = grads_ref[...]
    stage(4)

    trip = Scatter(mp_me, xcore_out, xcore_in, xchip_out, xchip_in, xsend, xrecv)

    def x_block(q):
        at = pl.ds(pl.multiple_of(q * rows, rows), rows)
        return dotf(joint_ref[at], w_all[:, : 3 * cols], NT)

    normed_grad = trip.run(x_block)
    tokens = x_ref[...].astype(f32)
    scale = lax.rsqrt(jnp.mean(tokens * tokens, axis=-1, keepdims=True) + epsilon)
    scaled = tokens * scale
    first_out[0] = jnp.sum(normed_grad * scaled, axis=0, keepdims=True)
    firsts = [
        remote(first_out.at[0], first_mp.at[k], fsend.at[k], frecv.at[k], mp=flip(mp_me, k))
        for k in range(1, MP)
    ]
    for copy in firsts:
        copy.start()
    weighted = normed_grad * gain1_ref[...]
    xgrad_ref[...] = hgrad_ref[...] + scale * (
        weighted - scaled * jnp.mean(weighted * scaled, axis=-1, keepdims=True)
    )
    for copy in firsts:
        copy.wait_recv()
    first_out[1] = first_out[0] + first_mp[1] + first_mp[2] + first_mp[3]
    seconds = [
        remote(first_out.at[1], first_dp.at[k], fsend.at[MP + k], frecv.at[MP + k],
               dp=base + flip(near, k))
        for k in range(1, NFFN)
    ]
    for copy in seconds:
        copy.start()
    stage(5)
    if inside:
        for copy in wcopies:
            copy.wait_recv()
        total = wrecv_ref[0].astype(f32)
        for p in range(1, NFFN):
            total = total + wrecv_ref[p].astype(f32)
        wgrad_ref[...] = total
    for copy in seconds:
        copy.wait_recv()
    total = first_out[1]
    for k in range(1, NFFN):
        total = total + first_dp[k]
    first_ref[...] = total

    for copy in moved:
        copy.wait_recv()
    if inside:
        for copy in mine:
            copy.wait()
        for copy in wcopies:
            copy.wait_send()
    for copy in moved + returns + stages + firsts + seconds:
        copy.wait_send()
    combine.drain()
    trip.drain()


def attention_back(
    agrad, hgrad, x, gain1, rows1, w, q, k, v, mixed, lse, pick, gate, residual, outq, small,
    carry_grad, dwin, dwout, groups,
):
    rows, width = x.shape
    everyone = MP * rows
    cos, sin = rope_constants()
    inside = groups == 1
    cols = w.shape[-1]
    heads = q.shape[0]
    depth = width // NFFN
    hidden_cols = dwout.shape[-1]
    sd = jax.ShapeDtypeStruct
    vm = pltpu.VMEM
    dma = pltpu.SemaphoreType.DMA
    outs = [
        sd((rows, width), bf16),
        sd((rows, width), f32),
        sd((depth if inside else width, cols), f32),
        sd((40, width), f32),
        sd((1, width), f32),
    ]
    specs = [VM] * len(outs)
    if inside:
        outs += [sd((NFFN, 2, depth, hidden_cols), bf16), sd((NFFN, depth, hidden_cols), bf16)]
        specs += [HB, HB]
    return pl.pallas_call(
        functools.partial(back_kernel, inside),
        out_shape=outs,
        in_specs=[VM] * 19 + [HB, HB],
        out_specs=specs,
        scratch_shapes=[
            vm((MP, rows, width), bf16),
            vm((everyone, heads * HD), bf16),
            vm((everyone, 3 * heads * HD), bf16),
            vm((everyone, HD), f32),
            vm((everyone, HD), f32),
            vm((width, cols), f32),
            vm((NFFN, depth, cols), bf16),
            vm((NFFN, depth, cols), bf16),
            vm((NFFN, QUARTER, width), bf16),
            vm((2, rows, width), bf16),
            vm((2, rows, width), bf16),
            vm((rows, width), bf16),
            vm((rows, width), bf16),
            vm((2, rows, width), bf16),
            vm((2, rows, width), bf16),
            vm((rows, width), bf16),
            vm((rows, width), bf16),
            vm((5, 40, width), f32),
            vm((5, 40, width), f32),
            vm((MP, 1, width), f32),
            vm((NFFN, 1, width), f32),
            vm((2, 1, width), f32),
            dma((3,)), dma((3,)),
            dma((8,)), dma((8,)),
            dma((2, 8)), dma((2, 8)), dma((2,)),
            dma((3,)), dma((3,)),
            dma((3,)), dma((3,)),
            dma((8,)), dma((8,)),
            dma((5,)), dma((5,)),
            dma((MP + NFFN,)), dma((MP + NFFN,)),
        ],
        compiler_params=pltpu.CompilerParams(
            collective_id=2, has_side_effects=True, vmem_limit_bytes=60 * 2**20
        ),
        name="attention_backward",
    )(
        agrad, hgrad, x, gain1, jnp.asarray(cos), jnp.asarray(sin), rows1, w, q, k, v, mixed, lse,
        pick, gate, residual, outq, small, carry_grad, dwin, dwout,
    )


def clusters():
    groups = lax.axis_size("dp") // NFFN
    near = [[group * NFFN + expert for expert in range(NFFN)] for group in range(groups)]
    far = [[group * NFFN + expert for group in range(groups)] for expert in range(NFFN)]
    return groups, near, far


def exchange(shard, dim):
    _, near, far = clusters()
    own = lax.all_to_all(shard, "dp", 0, dim, axis_index_groups=near, tiled=True)
    return lax.all_gather(own, "dp", axis=dim, axis_index_groups=far, tiled=True)


def exchange_back(grads, dim):
    _, near, far = clusters()
    grads = lax.psum_scatter(
        grads.astype(f32), "dp", scatter_dimension=dim, axis_index_groups=far, tiled=True
    )
    return lax.all_to_all(grads.astype(bf16), "dp", dim, 0, axis_index_groups=near, tiled=True)


def per_device(
    inputs,
    query_key_value,
    output_weight,
    expert_input,
    expert_output,
    first_gain,
    second_gain,
    router_weight,
    logit_carry,
    constant_mix,
    constant_values,
    previous_logits,
    routes,
    cotangent,
):
    rows, width = inputs.shape
    offset = lax.axis_index("mp") * rows
    groups, _, far = clusters()
    gain_one = first_gain.astype(f32)[None]
    gain_two = second_gain.astype(f32)[None]

    def own(array):
        return lax.dynamic_slice_in_dim(array, offset, rows, 0)

    def sixteen(array):
        return jnp.pad(array.T, ((0, 16 - array.shape[1]), (0, 0)))

    prior = jnp.dot(previous_logits, logit_carry, precision=highest)
    routes_t = jnp.pad(routes.T, ((0, 6), (0, 0)), constant_values=-1)
    routes_own = jnp.pad(own(routes), ((0, 0), (0, 126)), constant_values=-1)
    prior_own = jnp.pad(own(prior), ((0, 0), (0, 16 - NEXP)))
    carry = jnp.pad(logit_carry, ((0, 16 - NEXP), (0, 16 - NEXP)))
    shard_depth = query_key_value.shape[0]
    shard = jnp.concatenate(
        [query_key_value.reshape(shard_depth, -1), output_weight.T], axis=1
    )
    cols = output_weight.shape[0]
    expert_output_t = expert_output.transpose(0, 2, 1)
    if groups > 1:
        shard = lax.all_gather(shard, "dp", axis=0, tiled=True)
        win = exchange(expert_input, 2)[0]
        wout = exchange(expert_output_t, 1)[0]
    got = attention(inputs, gain_one, gain_two, shard, expert_input, expert_output_t, groups)
    rows1, w, q, k, v, mixed, lse, hidden, rows2 = got[:9]
    if groups == 1:
        win, wout = got[9:]
    (residual, hidden_grad, attended_grad, logits_grad, small, carry_grad, pick, gate, outq, dwin,
     dwout) = experts(
        rows2, hidden, cotangent, gain_two, sixteen(router_weight), sixteen(constant_mix),
        constant_values, sixteen(prior), carry, sixteen(own(previous_logits)), routes_t,
        routes_own, prior_own, win, wout,
    )
    output, input_grad, weight_grad, sums, first_grad, *expert_grads = attention_back(
        attended_grad, hidden_grad, inputs, gain_one, rows1, w, q, k, v, mixed, lse, pick, gate,
        residual, outq, small, carry_grad, dwin, dwout, groups,
    )
    if groups > 1:
        weight_grad = lax.psum_scatter(weight_grad, "dp", scatter_dimension=0, tiled=True)
        expert_grads = [exchange_back(dwin[None], 2), exchange_back(dwout[None], 1)]
        sums, first_grad = lax.psum((sums, first_grad), "dp", axis_index_groups=far)
    expert_in_grad = expert_grads[0].astype(f32)
    expert_out_grad = expert_grads[1].transpose(0, 2, 1).astype(f32)
    return (
        output,
        input_grad,
        logits_grad[:NEXP].T,
        weight_grad[:, : 3 * cols].reshape(shard_depth, 3, cols),
        weight_grad[:, 3 * cols :].T,
        expert_in_grad,
        expert_out_grad,
        first_grad[0],
        sums[22],
        sums[:NEXP].T,
        sums[24 : 24 + NEXP, :NEXP],
        sums[16:20].T,
        sums[20:22],
    )


def solution(mesh):
    in_specs = (
        P(("dp", "mp"), None),
        P("dp", None, "mp"),
        P("mp", "dp"),
        P(None, None, "dp", "mp"),
        P(None, "mp", "dp"),
        P(),
        P(),
        P(),
        P(),
        P(),
        P(),
        P("dp", None),
        P("dp", None),
        P(("dp", "mp"), None),
    )
    out_specs = (
        P(("dp", "mp"), None),
        P(("dp", "mp"), None),
        P(("dp", "mp"), None),
        P("dp", None, "mp"),
        P("mp", "dp"),
        P(None, None, "dp", "mp"),
        P(None, "mp", "dp"),
        P(),
        P(),
        P(),
        P(),
        P(),
        P(),
    )
    return jax.shard_map(
        per_device, mesh=mesh, in_specs=in_specs, out_specs=out_specs, check_vma=False
    )
```

```python
import functools
import numpy as np
import jax
import jax.numpy as jnp
from jax import lax
from jax.sharding import PartitionSpec as P
from jax.experimental import pallas as pl
from jax.experimental.pallas import tpu as pltpu

HD = 64
NFFN = 8
NEXP = 12
SEQ = 1024
CAP = 256
MP = 4
QUARTER = CAP // MP

epsilon = 1e-06
rope_base = 10000.0
highest = lax.Precision.HIGHEST
f32 = jnp.float32
bf16 = jnp.bfloat16
MESH = pl.DeviceIdType.MESH
VM = pl.BlockSpec(memory_space=pltpu.VMEM)
HB = pl.BlockSpec(memory_space=pl.ANY)
NT = (((1,), (1,)), ((), ()))
TN = (((0,), (0,)), ((), ()))


def flip(index, distance):
    out = index
    bit = 1
    while bit <= distance:
        if distance & bit:
            out = out + bit - 2 * bit * ((index // bit) % 2)
        bit *= 2
    return out


def dotf(a, b, dims=None):
    if dims is None:
        return jnp.dot(a, b, preferred_element_type=f32)
    return lax.dot_general(a, b, dims, preferred_element_type=f32)


def remote(src, dst, send, recv, **where):
    return pltpu.make_async_remote_copy(
        src_ref=src, dst_ref=dst, send_sem=send, recv_sem=recv, device_id=where, device_id_type=MESH
    )


def greet(mp_me, near, base):
    barrier = pltpu.get_barrier_semaphore()
    for k in range(1, MP):
        pl.semaphore_signal(barrier, inc=1, device_id={"mp": flip(mp_me, k)}, device_id_type=MESH)
    for k in range(1, NFFN):
        pl.semaphore_signal(
            barrier, inc=1, device_id={"dp": base + flip(near, k)}, device_id_type=MESH
        )
    pl.semaphore_wait(barrier, MP - 1 + NFFN - 1)


def rope_constants():
    half = HD // 2
    positions = np.arange(SEQ, dtype=np.float32)
    frequency = (rope_base ** (-np.arange(half, dtype=np.float32) / half)).astype(np.float32)
    angles = (positions[:, None] * frequency[None, :]).astype(np.float32)
    cosine, sine = np.cos(angles), np.sin(angles)
    return (
        np.concatenate([cosine, cosine], axis=1),
        np.concatenate([-sine, sine], axis=1),
    )


def swap_halves(x):
    half = HD // 2
    return jnp.concatenate([x[:, half:], x[:, :half]], axis=1)


class Gather:
    def __init__(self, ref, mp_me, send, recv):
        self.me, self.core, self.chip = mp_me, flip(mp_me, 1), flip(mp_me, 2)
        own = ref.at[mp_me]
        far = ref.at[self.chip]
        self.to_chip = remote(own, own, send.at[0], recv.at[0], mp=self.chip)
        self.to_core = remote(own, own, send.at[1], recv.at[1], mp=self.core)
        self.relay = remote(far, far, send.at[2], recv.at[2], mp=self.core)

    def start(self):
        self.to_chip.start()
        self.to_core.start()

    def forward(self):
        self.to_chip.wait_recv()
        self.relay.start()

    def finish(self):
        self.to_core.wait_recv()
        self.relay.wait_recv()
        self.to_chip.wait_send()
        self.to_core.wait_send()
        self.relay.wait_send()


def pack3(value):
    high = value.astype(bf16).astype(f32)
    rest = value - high
    mid = rest.astype(bf16).astype(f32)
    low = (rest - mid).astype(bf16).astype(f32)
    lane = lax.broadcasted_iota(jnp.int32, (value.shape[0], 128), 1)
    return jnp.where(
        lane == 0, high, jnp.where(lane == 1, mid, jnp.where(lane == 2, low, 0.0))
    ).astype(bf16)


def unpack3(parts):
    return jnp.sum(parts.astype(f32), axis=-1, keepdims=True)


def exact(left, right, dims=None):
    high = left.astype(bf16)
    rest = left - high.astype(f32)
    mid = rest.astype(bf16)
    low = (rest - mid.astype(f32)).astype(bf16)
    return dotf(high, right, dims) + (dotf(mid, right, dims) + dotf(low, right, dims))


class Scatter:
    def __init__(self, mp_me, core_out, core_in, chip_out, chip_in, send, recv):
        self.me, self.core, self.chip = mp_me, flip(mp_me, 1), flip(mp_me, 2)
        self.core_out, self.core_in = core_out, core_in
        self.chip_out, self.chip_in = chip_out, chip_in
        self.to_core = [
            remote(core_out.at[j], core_in.at[j], send.at[j], recv.at[j], mp=self.core)
            for j in range(2)
        ]
        self.to_chip = remote(chip_out, chip_in, send.at[2], recv.at[2], mp=self.chip)

    def run(self, blocks):
        for j, block in enumerate((flip(self.me, 3), self.core)):
            self.core_out[j] = blocks(block).astype(bf16)
            self.to_core[j].start()
        term = blocks(self.chip)
        self.to_core[0].wait_recv()
        self.chip_out[...] = (term + self.core_in[0].astype(f32)).astype(bf16)
        self.to_chip.start()
        term = blocks(self.me)
        self.to_core[1].wait_recv()
        term = term + self.core_in[1].astype(f32)
        self.to_chip.wait_recv()
        return term + self.chip_in[...].astype(f32)

    def drain(self):
        for copy in self.to_core + [self.to_chip]:
            copy.wait_send()


def forward_kernel(
    inside,
    x_ref, cot_ref, params_ref, routing_ref, cos_ref, sin_ref, wshard_ref, win_shard, wout_shard,
    rows1_ref, w_ref, q_ref, k_ref, v_ref, mixed_ref, lse_ref,
    residual_ref, hgrad_ref, agrad_ref, lgrad_ref, small_ref, pick_ref, gate_ref, outp_ref, dw_ref,
    rows2_ref, hidden_ref, sum_ref, core_in, chip_out, chip_in, core_out,
    cot_all, place_ref, gates_ref, prior_ref, msgx, msgc, xs, cs, units_ref, pgrad_ref,
    part_ref, keep_ref, gcore_out, gcore_in, gchip_out, gchip_in, gret, score_out, score_in,
    ncore_in, nchip_in,
    sends, recvs, wsend, wrecv, esend, erecv, local,
    csend, crecv, xsend, xrecv, dsend, drecv, xgs, xgr, cgs, cgr, gsend, grecv,
    rsend, rrecv, ssend, srecv, nsend, nrecv,
):
    mp_me = lax.axis_index("mp")
    dp_me = lax.axis_index("dp")
    near = lax.rem(dp_me, NFFN)
    base = dp_me - near
    core, chip, far = flip(mp_me, 1), flip(mp_me, 2), flip(mp_me, 3)
    rows, width = x_ref.shape
    everyone = MP * rows
    greet(mp_me, near, base)

    tokens = x_ref[...].astype(f32)
    scale = lax.rsqrt(jnp.mean(tokens * tokens, axis=-1, keepdims=True) + epsilon)
    rows1_ref[mp_me] = (tokens * scale * params_ref[23:24]).astype(bf16)
    gather1 = Gather(rows1_ref, mp_me, sends.at[pl.ds(0, 3)], recvs.at[pl.ds(0, 3)])
    gather1.start()
    if inside:
        w_ref[near] = wshard_ref[...]
        own = w_ref.at[near]
        along = [
            remote(own, own, wsend.at[k], wrecv.at[k], dp=base + flip(near, k)) for k in (2, 4, 6)
        ]
        for copy in along:
            copy.start()
        mate = base + flip(near, 1)
        across = [remote(own, own, wsend.at[0], wrecv.at[0], dp=mate)]
        across[0].start()
    cot_all[mp_me] = cot_ref[...]
    cot_gather = Gather(cot_all, mp_me, csend, crecv)
    cot_gather.start()

    ids = lax.broadcasted_iota(jnp.int32, (16, everyone), 0).astype(f32)
    chosen = (ids == routing_ref[16:17]) | (ids == routing_ref[17:18])
    earlier = lax.broadcasted_iota(jnp.int32, (everyone, everyone), 0) < lax.broadcasted_iota(
        jnp.int32, (everyone, everyone), 1
    )
    counts = dotf(
        jnp.where(chosen, 1.0, 0.0).astype(bf16), jnp.where(earlier, 1.0, 0.0).astype(bf16)
    )
    place_ref[...] = jnp.where(chosen, counts, -1.0)
    wanted = (lax.broadcasted_iota(jnp.int32, (QUARTER, everyone), 0) + QUARTER * mp_me).astype(f32)

    def target(k):
        return lax.rem(near + k, NFFN)

    def choose(k, carried):
        pick = wanted == place_ref[pl.ds(target(k), 1)]
        pick_ref[k] = jnp.where(pick, 1.0, 0.0).astype(bf16)
        return carried

    lax.fori_loop(0, NFFN, choose, 0)
    carry = params_ref[24:40, 0:16]
    prior_ref[...] = lax.dot_general(
        carry, routing_ref[0:16], TN, preferred_element_type=f32, precision=highest
    )

    if inside:
        for k, copy in zip((2, 4, 6), along):
            copy.wait_recv()
            block = w_ref.at[flip(near, k)]
            onward = remote(block, block, wsend.at[k + 1], wrecv.at[k + 1], dp=mate)
            onward.start()
            across.append(onward)
        gather1.forward()
        for copy in across:
            copy.wait_recv()
        for copy in along + across:
            copy.wait_send()
        weights = []
        din = win_shard.shape[2]
        place = pl.ds(pl.multiple_of(near * din, din), din)
        for k in (4, 2, 6, 5, 7, 3, 1):
            peer = flip(near, k)
            for i, (src, dst) in enumerate([
                (win_shard.at[peer], dw_ref.at[0:2, place]),
                (wout_shard.at[peer], dw_ref.at[2, place]),
            ]):
                weights.append(
                    remote(src, dst, esend.at[i, k], erecv.at[i, k], dp=base + peer)
                )
        first = 4
        for copy in weights[:first]:
            copy.start()
        mine = [
            pltpu.make_async_copy(win_shard.at[near], dw_ref.at[0:2, place], local.at[0]),
            pltpu.make_async_copy(wout_shard.at[near], dw_ref.at[2, place], local.at[1]),
        ]
        for copy in mine:
            copy.start()
    else:
        w_ref[...] = wshard_ref[...]
        mine = [
            pltpu.make_async_copy(win_shard, dw_ref.at[0:2], local.at[0]),
            pltpu.make_async_copy(wout_shard, dw_ref.at[2], local.at[1]),
        ]
        for copy in mine:
            copy.start()
        gather1.forward()
    gather1.finish()

    cot_gather.forward()
    cot_gather.finish()

    def c_copy(k):
        return remote(
            msgc.at[k], cs.at[k, mp_me], dsend.at[k], drecv.at[k], dp=base + target(k)
        )

    def send(picked, ref, copy, lanes):
        def half(i, carried):
            start = 4 - 4 * i
            blocks = dotf(pick_ref[pl.ds(start, 4)].reshape(4 * QUARTER, everyone), picked())
            ref[(pl.ds(start, 4),) + lanes] = blocks.astype(bf16).reshape(4, QUARTER, width)

            def go(k, inner):
                @pl.when(k > 0)
                def _():
                    copy(k).start()

                return inner

            return lax.fori_loop(start, start + 4, go, carried)

        lax.fori_loop(0, 2, half, 0)

    send(lambda: cot_all[...].reshape(everyone, width), msgc, c_copy, ())
    cs[0, mp_me] = msgc[0]
    if inside:
        for copy in weights[first:]:
            copy.start()

    w_all = w_ref[...].reshape(width, w_ref.shape[2])
    heads = q_ref.shape[0]
    cols = heads * HD

    def project(i, carry):
        at = pl.ds(pl.multiple_of(i * rows, rows), rows)
        joint = dotf(rows1_ref[i], w_all[:, : 3 * cols])
        cosine, sine = cos_ref[at], sin_ref[at]
        for h in range(heads):
            query = joint[:, h * HD : (h + 1) * HD]
            key = joint[:, cols + h * HD : cols + (h + 1) * HD]
            q_ref[h, at] = (query * cosine + swap_halves(query) * sine).astype(bf16)
            k_ref[h, at] = (key * cosine + swap_halves(key) * sine).astype(bf16)
            v_ref[h, at] = joint[:, 2 * cols + h * HD : 2 * cols + (h + 1) * HD].astype(bf16)
        return carry

    lax.fori_loop(0, MP, project, 0)
    out_weight = w_all[:, 3 * cols :]

    to_core = [
        remote(core_out.at[j], core_in.at[j], sends.at[3 + j], recvs.at[3 + j], mp=core)
        for j in range(2)
    ]
    to_chip = remote(chip_out, chip_in, sends.at[5], recvs.at[5], mp=chip)

    def attend(step, carry):
        block = flip(mp_me, 3)
        block = jnp.where(step == 1, core, jnp.where(step == 2, chip, jnp.where(step == 3, mp_me, block)))
        at = pl.ds(pl.multiple_of(block * rows, rows), rows)
        row_ids = block * rows + lax.broadcasted_iota(jnp.int32, (rows, SEQ), 0)
        seen = row_ids >= lax.broadcasted_iota(jnp.int32, (rows, SEQ), 1)
        for h in range(heads):
            scores = dotf(q_ref[h, at], k_ref[h], NT) * HD**-0.5
            scores = jnp.where(seen, scores, -jnp.inf)
            peak = jnp.max(scores, axis=-1, keepdims=True)
            exponent = jnp.exp(scores - peak)
            total = jnp.sum(exponent, axis=-1, keepdims=True)
            probs = (exponent * (1.0 / total)).astype(bf16)
            mixed_ref[at, h * HD : (h + 1) * HD] = dotf(probs, v_ref[h]).astype(bf16)
            lse_ref[at, h : h + 1] = peak + jnp.log(total)
        part = dotf(mixed_ref[at], out_weight, NT)

        @pl.when(step == 0)
        def _():
            core_out[0] = part.astype(bf16)
            to_core[0].start()

        @pl.when(step == 1)
        def _():
            core_out[1] = part.astype(bf16)
            to_core[1].start()

        @pl.when(step == 2)
        def _():
            to_core[0].wait_recv()
            chip_out[...] = (part + core_in[0].astype(f32)).astype(bf16)
            to_chip.start()

        @pl.when(step == 3)
        def _():
            sum_ref[...] = part

        return carry

    lax.fori_loop(0, MP, attend, 0)
    to_core[1].wait_recv()
    partial = sum_ref[...] + core_in[1].astype(f32)
    to_chip.wait_recv()
    hidden = x_ref[...].astype(f32) + (partial + chip_in[...].astype(f32))
    hidden_ref[...] = hidden
    scale2 = lax.rsqrt(jnp.mean(hidden * hidden, axis=-1, keepdims=True) + epsilon)
    rows2_ref[mp_me] = (hidden * scale2 * params_ref[22:23]).astype(bf16)
    gather2 = Gather(rows2_ref, mp_me, sends.at[pl.ds(6, 3)], recvs.at[pl.ds(6, 3)])
    gather2.start()
    for copy in to_core + [to_chip]:
        copy.wait_send()
    gather2.forward()

    def turn(i):
        return lax.rem(i + 4, NFFN)

    def c_gather(k):
        return Gather(cs.at[k], mp_me, cgs.at[k], cgr.at[k])

    def at_step(i, first, body):
        @pl.when((i >= first) & (i < NFFN + first))
        def _():
            body(turn(i - first))

    def cot_step(i, carried):
        def arrived(k):
            @pl.when(k > 0)
            def _():
                c_copy(k).wait_recv()

            c_gather(k).start()

        at_step(i, 0, arrived)
        at_step(i, 1, lambda k: c_gather(k).forward())
        return carried

    lax.fori_loop(0, NFFN + 1, cot_step, 0)
    gather2.finish()

    router = params_ref[0:16].astype(bf16)
    mix = params_ref[16:20].astype(bf16)
    tokens = rows2_ref[...].reshape(everyone, width)
    logits = dotf(router, tokens, NT) + prior_ref[...]
    masked = jnp.where(place_ref[...] >= 0.0, logits, -jnp.inf)
    exponent = jnp.exp(masked - jnp.max(masked, axis=0, keepdims=True))
    gates_ref[...] = exponent / jnp.sum(exponent, axis=0, keepdims=True)

    def weigh(k, carried):
        gate = jnp.sum(
            pick_ref[k].astype(f32) * gates_ref[pl.ds(target(k), 1)], axis=1, keepdims=True
        )
        gate_ref[k] = jnp.broadcast_to(gate, (QUARTER, 128))
        msgx[k, :, width:] = pack3(gate)
        return carried

    lax.fori_loop(0, NFFN, weigh, 0)

    def x_copy(k):
        return remote(
            msgx.at[k], xs.at[k, mp_me], xsend.at[k], xrecv.at[k], dp=base + target(k)
        )

    send(
        lambda: rows2_ref[...].reshape(everyone, width), msgx, x_copy,
        (slice(None), slice(0, width)),
    )
    xs[0, mp_me] = msgx[0]

    def x_gather(k):
        return Gather(xs.at[k], mp_me, xgs.at[k], xgr.at[k])

    def slots_of(k):
        return pl.ds(pl.multiple_of(k * CAP, CAP), CAP)

    def x_step(i, carried):
        def arrived(k):
            @pl.when(k > 0)
            def _():
                x_copy(k).wait_recv()

            x_gather(k).start()

        def passed(k):
            x_gather(k).forward()

        at_step(i, 0, arrived)
        at_step(i, 1, passed)
        return carried

    lax.fori_loop(0, NFFN + 1, x_step, 0)
    if inside:
        for copy in weights:
            copy.wait_recv()
    for copy in mine:
        copy.wait()

    def r_trip(k):
        slot = lax.rem(k, 4)
        return Scatter(
            mp_me, gcore_out.at[slot], gcore_in.at[k], gchip_out.at[slot], gchip_in.at[k],
            gsend.at[k], grecv.at[k],
        )

    def g_copy(k):
        return remote(
            msgx.at[k], gret.at[k], rsend.at[k], rrecv.at[k],
            dp=base + lax.rem(near - k + NFFN, NFFN),
        )

    def seal(ref, index, total):
        ref[index + (slice(None), slice(0, width))] = total[:, :width].astype(bf16)
        ref[index + (slice(None), slice(width, None))] = pack3(unpack3(total[:, width:]))

    def expert_step(i, carried):
        def compute(k):
            c_gather(k).finish()
            x_gather(k).finish()
            x = xs[k].reshape(CAP, width + 128)[:, :width]
            gate = unpack3(xs[k].reshape(CAP, width + 128)[:, width:])
            c = cs[k].reshape(CAP, width)
            gate_pre = dotf(x, dw_ref[0])
            up_pre = dotf(x, dw_ref[1])
            sig = jax.nn.sigmoid(gate_pre)
            units = (gate_pre * sig * up_pre).astype(bf16)
            units_ref[slots_of(k)] = units
            outp_ref[k] = dotf(units, dw_ref[2], NT).astype(bf16).reshape(MP, QUARTER, width)
            raw = dotf(c, dw_ref[2])
            score = jnp.sum(units.astype(f32) * raw, axis=1, keepdims=True)
            units_grad = raw * gate
            gate_grad = (units_grad * up_pre * sig * (1.0 + gate_pre * (1.0 - sig))).astype(bf16)
            up_grad = (units_grad * (gate_pre * sig)).astype(bf16)
            pgrad_ref[0, slots_of(k)] = gate_grad
            pgrad_ref[1, slots_of(k)] = up_grad
            back = dotf(gate_grad, dw_ref[0], NT) + dotf(up_grad, dw_ref[1], NT)
            cs[k] = (c.astype(f32) * gate).astype(bf16).reshape(MP, QUARTER, width)
            part_ref[:, :, :width] = back.reshape(MP, QUARTER, width)
            part_ref[:, :, width:] = pack3(score).astype(f32).reshape(MP, QUARTER, 128)
            slot = lax.rem(k, 4)
            gcore_out[slot, 0] = part_ref[far].astype(bf16)
            gcore_out[slot, 1] = part_ref[core].astype(bf16)
            keep_ref[slot, 0] = part_ref[chip]
            keep_ref[slot, 1] = part_ref[mp_me]
            for copy in r_trip(k).to_core:
                copy.start()

        def across(k):
            trip = r_trip(k)
            trip.to_core[0].wait_recv()
            seal(gchip_out, (lax.rem(k, 4),), keep_ref[lax.rem(k, 4), 0] + gcore_in[k, 0].astype(f32))
            trip.to_chip.start()

        def away(k):
            trip = r_trip(k)
            trip.to_core[1].wait_recv()
            trip.to_chip.wait_recv()
            total = (
                keep_ref[lax.rem(k, 4), 1]
                + gcore_in[k, 1].astype(f32)
                + gchip_in[k].astype(f32)
            )
            trip.drain()

            @pl.when(k > 0)
            def _():
                x_copy(k).wait_send()

            seal(msgx, (k,), total)

            @pl.when(k > 0)
            def _():
                g_copy(k).start()

            @pl.when(k == 0)
            def _():
                gret[0] = msgx[0]

        at_step(i, 4, away)
        at_step(i, 0, compute)
        at_step(i, 2, across)
        return carried

    lax.fori_loop(0, NFFN + 4, expert_step, 0)

    def weights_step(j, carried):
        at = pl.ds(pl.multiple_of(j * 128, 128), 128)
        x = xs[:, :, :, at].reshape(NFFN * CAP, 128)
        c = cs[:, :, :, at].reshape(NFFN * CAP, 128)
        dw_ref[0, at] = dotf(x, pgrad_ref[0], TN).astype(bf16)
        dw_ref[1, at] = dotf(x, pgrad_ref[1], TN).astype(bf16)
        dw_ref[2, at] = dotf(c, units_ref[...], TN).astype(bf16)
        return carried

    lax.fori_loop(0, width // 128, weights_step, 0)

    n_bf = rows2_ref[mp_me]
    n = n_bf.astype(f32)
    cot = cot_ref[...].astype(f32)
    hidden = hidden_ref[...]
    lane = lax.broadcasted_iota(jnp.int32, (rows, 128), 1)
    own_at = pl.ds(pl.multiple_of(mp_me * rows, rows), rows)
    gates_t = gates_ref[:, own_at]
    own_gates = jnp.concatenate([gates_t, jnp.zeros((112, rows), f32)], axis=0).T
    copy_gate = own_gates[:, NFFN + 1 : NFFN + 2]
    const_gates = [own_gates[:, NFFN + 2 : NFFN + 3], own_gates[:, NFFN + 3 : NFFN + 4]]
    mix_logits = dotf(n_bf, mix, NT)
    with_normed = jnp.sum(cot * n, axis=1, keepdims=True)
    residual = hidden + copy_gate * n
    local_grad = copy_gate * cot
    local_scores = jnp.where(lane == NFFN + 1, with_normed, 0.0)
    mix_grads = jnp.zeros((rows, 128), f32)
    for c in range(2):
        first, second = mix_logits[:, 2 * c : 2 * c + 1], mix_logits[:, 2 * c + 1 : 2 * c + 2]
        top = jnp.maximum(first, second)
        first, second = jnp.exp(first - top), jnp.exp(second - top)
        share = 1.0 / (first + second)
        first, second = first * share, second * share
        constant = params_ref[20 + c : 21 + c]
        with_constant = jnp.sum(cot * constant, axis=1, keepdims=True)
        gate = const_gates[c]
        residual = residual + gate * (first * n + second * constant)
        local_scores = jnp.where(
            lane == NFFN + 2 + c, first * with_normed + second * with_constant, local_scores
        )
        local_grad = local_grad + (first * gate) * cot
        small_ref[20 + c : 21 + c] = jnp.sum((second * gate) * cot, axis=0, keepdims=True)
        grad_first, grad_second = gate * with_normed, gate * with_constant
        mean = first * grad_first + second * grad_second
        mix_grads = jnp.where(lane == 2 * c, first * (grad_first - mean), mix_grads)
        mix_grads = jnp.where(lane == 2 * c + 1, second * (grad_second - mean), mix_grads)
    residual_ref[...] = residual

    def returned(k, carried):
        g_copy(k).wait_recv()
        return carried

    lax.fori_loop(1, NFFN, returned, 0)
    ret = gret[...].reshape(NFFN * QUARTER, width + 128)
    score_out[...] = jnp.zeros_like(score_out)

    def give_scores(k, carried):
        slots = unpack3(gret[k, :, width:])
        row = jnp.sum(pick_ref[k].astype(f32) * slots, axis=0, keepdims=True)
        for q in range(MP):
            score_out[q, pl.ds(target(k), 1)] = row[:, q * rows : (q + 1) * rows]
        return carried

    lax.fori_loop(0, NFFN, give_scores, 0)
    score_copies = [
        remote(score_out.at[flip(mp_me, k)], score_in.at[k], ssend.at[k], srecv.at[k], mp=flip(mp_me, k))
        for k in range(1, MP)
    ]
    for copy in score_copies:
        copy.start()

    def grad_block(q):
        at = pl.ds(pl.multiple_of(q * rows, rows), rows)
        return dotf(
            pick_ref[:, :, at].reshape(NFFN * QUARTER, rows), ret[:, :width], TN
        )

    trip = Scatter(mp_me, core_out, ncore_in, chip_out, nchip_in, nsend, nrecv)
    normed_grad = trip.run(grad_block) + local_grad

    for copy in score_copies:
        copy.wait_recv()
    ffn_scores = (score_out[mp_me] + score_in[1]) + (score_in[2] + score_in[3])
    scores = local_scores.T[:16] + jnp.concatenate([ffn_scores, jnp.zeros((8, rows), f32)], axis=0)
    logit_grad = gates_t * (scores - jnp.sum(gates_t * scores, axis=0, keepdims=True))
    lgrad_ref[...] = lax.dot_general(
        carry, logit_grad, (((1,), (0,)), ((), ())),
        preferred_element_type=f32, precision=highest,
    )
    small_ref[24:40] = jnp.zeros((16, width), f32)
    small_ref[24:40, 0:16] = lax.dot_general(
        routing_ref[0:16, own_at], logit_grad, NT, preferred_element_type=f32, precision=highest
    )
    stacked = jnp.concatenate([logit_grad, mix_grads.T[:16]], axis=0)
    heads = params_ref[0:32]
    sublane = lax.broadcasted_iota(jnp.int32, (32, width), 0)
    heads = jnp.where(sublane < 20, heads, 0.0).astype(bf16)
    feature_grads = exact(stacked, n_bf)
    small_ref[0:20] = feature_grads[0:20]
    normed_grad = normed_grad + exact(stacked, heads, TN)
    scale = lax.rsqrt(jnp.mean(hidden * hidden, axis=-1, keepdims=True) + epsilon)
    scaled = hidden * scale
    small_ref[22:23] = jnp.sum(normed_grad * scaled, axis=0, keepdims=True)
    small_ref[23:24] = jnp.zeros((1, width), f32)
    weighted = normed_grad * params_ref[22:23]
    hidden_grad = cot + scale * (
        weighted - scaled * jnp.mean(weighted * scaled, axis=-1, keepdims=True)
    )
    hgrad_ref[...] = hidden_grad
    agrad_ref[...] = hidden_grad.astype(bf16)

    trip.drain()
    for copy in score_copies:
        copy.wait_send()

    def drain(k, carried):
        c_copy(k).wait_send()
        g_copy(k).wait_send()
        return carried

    lax.fori_loop(1, NFFN, drain, 0)
    if inside:
        for copy in weights:
            copy.wait_send()


def forward(x, cot, params, routing, wshard, win, wout, groups):
    rows, width = x.shape
    cos, sin = rope_constants()
    inside = groups == 1
    cols = wshard.shape[-1]
    depth = width // NFFN
    hidden_cols = win.shape[-1]
    heads = cols // 4 // HD
    everyone = MP * rows
    slots = NFFN * CAP
    wide = width + 128
    sd = jax.ShapeDtypeStruct
    vm = pltpu.VMEM
    dma = pltpu.SemaphoreType.DMA
    outs = [
        sd((MP, rows, width), bf16),
        sd((NFFN, depth, cols), bf16),
        sd((heads, SEQ, HD), bf16),
        sd((heads, SEQ, HD), bf16),
        sd((heads, SEQ, HD), bf16),
        sd((SEQ, heads * HD), bf16),
        sd((SEQ, 128), f32),
        sd((rows, width), f32),
        sd((rows, width), f32),
        sd((rows, width), bf16),
        sd((16, rows), f32),
        sd((40, width), f32),
        sd((NFFN, QUARTER, everyone), bf16),
        sd((NFFN, QUARTER, 128), f32),
        sd((NFFN, MP, QUARTER, width), bf16),
        sd((3, width, hidden_cols), bf16),
    ]
    if not inside:
        wshard = wshard.reshape(NFFN, depth, cols)
    return pl.pallas_call(
        functools.partial(forward_kernel, inside),
        out_shape=outs,
        in_specs=[VM] * 7 + [HB, HB],
        out_specs=[VM] * len(outs),
        scratch_shapes=[
            vm((MP, rows, width), bf16),
            vm((rows, width), f32),
            vm((rows, width), f32),
            vm((2, rows, width), bf16),
            vm((rows, width), bf16),
            vm((rows, width), bf16),
            vm((2, rows, width), bf16),
            vm((MP, rows, width), bf16),
            vm((16, everyone), f32),
            vm((16, everyone), f32),
            vm((16, everyone), f32),
            vm((NFFN, QUARTER, wide), bf16),
            vm((NFFN, QUARTER, width), bf16),
            vm((NFFN, MP, QUARTER, wide), bf16),
            vm((NFFN, MP, QUARTER, width), bf16),
            vm((slots, hidden_cols), bf16),
            vm((2, slots, hidden_cols), bf16),
            vm((MP, QUARTER, wide), f32),
            vm((4, 2, QUARTER, wide), f32),
            vm((4, 2, QUARTER, wide), bf16),
            vm((NFFN, 2, QUARTER, wide), bf16),
            vm((4, QUARTER, wide), bf16),
            vm((NFFN, QUARTER, wide), bf16),
            vm((NFFN, QUARTER, wide), bf16),
            vm((MP, 8, rows), f32),
            vm((MP, 8, rows), f32),
            vm((2, rows, width), bf16),
            vm((rows, width), bf16),
            dma((9,)), dma((9,)),
            dma((8,)), dma((8,)),
            dma((2, 8)), dma((2, 8)),
            dma((2,)),
            dma((3,)), dma((3,)),
            dma((8,)), dma((8,)),
            dma((8,)), dma((8,)),
            dma((8, 3)), dma((8, 3)),
            dma((8, 3)), dma((8, 3)),
            dma((8, 3)), dma((8, 3)),
            dma((8,)), dma((8,)),
            dma((4,)), dma((4,)),
            dma((3,)), dma((3,)),
        ],
        compiler_params=pltpu.CompilerParams(
            collective_id=0, has_side_effects=True, vmem_limit_bytes=60 * 2**20
        ),
        name="forward",
    )(x, cot, params, routing, jnp.asarray(cos), jnp.asarray(sin), wshard, win, wout)


def back_kernel(
    inside,
    agrad_ref, hgrad_ref, x_ref, params_ref, cos_ref, sin_ref, rows1_ref, w_ref, q_ref, k_ref, v_ref,
    mixed_ref, lse_ref, pick_ref, gate_ref, residual_ref, outp_ref, small_ref, dw_ref,
    output_ref, xgrad_ref, wgrad_ref, sums_ref, first_ref, dw_own,
    agrad_all, mgrad_ref, joint_ref, key_acc, value_acc, grads_ref, across_out, across_in,
    along_out, along_in, ret_ref, ocore_out, ocore_in, ochip_out, ochip_in,
    xcore_out, xcore_in, xchip_out, xchip_in, sum_out, sum_in, first_mp, first_dp, first_out,
    pcore_in, pchip_out, pchip_in, outq_ref,
    asend, arecv, osend, orecv, esend, erecv, psend, precv, local, rsend, rrecv, xsend, xrecv,
    wsend, wrecv, ssend, srecv, fsend, frecv,
):
    mp_me = lax.axis_index("mp")
    dp_me = lax.axis_index("dp")
    near = lax.rem(dp_me, NFFN)
    base = dp_me - near
    rows, width = agrad_ref.shape
    everyone = MP * rows
    heads = q_ref.shape[0]
    cols = heads * HD
    greet(mp_me, near, base)

    agrad_all[mp_me] = agrad_ref[...]
    gather = Gather(agrad_all, mp_me, asend, arecv)
    gather.start()
    core, chip, far = flip(mp_me, 1), flip(mp_me, 2), flip(mp_me, 3)
    din = dw_own.shape[2]

    def rows_of(index):
        return pl.ds(pl.multiple_of(index * din, din), din)

    if inside:
        moved = [
            remote(dw_ref.at[:, rows_of(flip(near, k))], dw_own.at[near], esend.at[k],
                   erecv.at[k], dp=base + flip(near, k))
            for k in (4, 6, 5, 7, 2, 3, 1)
        ]
        mine = [pltpu.make_async_copy(dw_ref.at[:, rows_of(near)], dw_own.at[near], local.at[0])]
    else:
        moved = []
        mine = [
            pltpu.make_async_copy(dw_ref.at[:, rows_of(p)], dw_own.at[p], local.at[p])
            for p in range(NFFN)
        ]
    for copy in moved + mine:
        copy.start()

    p_core = [
        remote(outp_ref.at[:, far], pcore_in.at[0], psend.at[0], precv.at[0], mp=core),
        remote(outp_ref.at[:, core], pcore_in.at[1], psend.at[1], precv.at[1], mp=core),
    ]
    for copy in p_core:
        copy.start()
    parts = (slice(4, 8), slice(0, 4))
    p_chip = [
        remote(pchip_out.at[part], pchip_in.at[part], psend.at[2 + j], precv.at[2 + j], mp=chip)
        for j, part in enumerate(parts)
    ]
    returns = {
        k: remote(outq_ref.at[k], ret_ref.at[k], osend.at[k], orecv.at[k],
                  dp=base + lax.rem(near - k + NFFN, NFFN))
        for k in range(1, NFFN)
    }

    def results_across():
        p_core[0].wait_recv()
        for j, part in enumerate(parts):
            pchip_out[part] = (
                outp_ref[part, chip].astype(f32) + pcore_in[0, part].astype(f32)
            ).astype(bf16)
            p_chip[j].start()

    def results_away(j):
        part = parts[j]
        if j == 0:
            p_core[1].wait_recv()
        p_chip[j].wait_recv()
        outq_ref[part] = (
            outp_ref[part, mp_me].astype(f32)
            + (pcore_in[1, part].astype(f32) + pchip_in[part].astype(f32))
        ).astype(bf16)
        for k in range(part.start, part.stop):
            if k > 0:
                returns[k].start()
            else:
                ret_ref[0] = outq_ref[0]

    sum_out[0] = small_ref[...]
    places = [{"mp": flip(mp_me, 1)}, {"mp": flip(mp_me, 2)}] + [
        {"dp": base + flip(near, k)} for k in (1, 2, 4)
    ]
    stages = [
        remote(sum_out.at[j], sum_in.at[j], ssend.at[j], srecv.at[j], **where)
        for j, where in enumerate(places)
    ]

    def stage(j):
        if j > 0:
            stages[j - 1].wait_recv()
            total = sum_out[j - 1] + sum_in[j - 1]
            if j == len(stages):
                sums_ref[...] = total
                return
            sum_out[j] = total
        stages[j].start()

    stage(0)
    gather.forward()
    stage(1)
    gather.finish()

    w_all = w_ref[...].reshape(width, w_ref.shape[2])
    out_weight = w_all[:, 3 * cols :]
    for i in range(MP):
        mgrad_ref[i * rows : (i + 1) * rows] = dotf(agrad_all[i], out_weight).astype(bf16)
    grads_ref[:, 3 * cols :] = dotf(agrad_all[...].reshape(everyone, width), mixed_ref[...], TN)

    combine = Scatter(mp_me, ocore_out, ocore_in, ochip_out, ochip_in, rsend, rrecv)

    def out_block(q):
        at = pl.ds(pl.multiple_of(q * rows, rows), rows)
        weighted = (ret_ref[...].astype(f32) * gate_ref[:, :, 0:1]).astype(bf16)
        return dotf(
            pick_ref[:, :, at].reshape(NFFN * QUARTER, rows),
            weighted.reshape(NFFN * QUARTER, width), TN,
        )

    def head_back(h):
        lanes = slice(h * HD, (h + 1) * HD)
        for b in range(MP):
            at = slice(b * rows, (b + 1) * rows)
            seen = (b + 1) * rows
            query = q_ref[h, at]
            keys = k_ref[h, :seen]
            out_grad = mgrad_ref[at, lanes]
            scores = dotf(query, keys, NT) * HD**-0.5
            allowed = b * rows + lax.broadcasted_iota(
                jnp.int32, (rows, seen), 0
            ) >= lax.broadcasted_iota(jnp.int32, (rows, seen), 1)
            probs = jnp.where(allowed, jnp.exp(scores - lse_ref[at, h : h + 1]), 0.0)
            probs_grad = dotf(out_grad, v_ref[h, :seen], NT)
            inner = jnp.sum(probs * probs_grad, axis=1, keepdims=True)
            score_grad = (probs * (probs_grad - inner)).astype(bf16)
            query_grad = dotf(score_grad, keys) * HD**-0.5
            joint_ref[at, lanes] = (
                query_grad * cos_ref[at] - swap_halves(query_grad) * sin_ref[at]
            ).astype(bf16)
            key_grad = dotf(score_grad, query, TN) * HD**-0.5
            value_grad = dotf(probs.astype(bf16), out_grad, TN)
            if b == 0:
                key_acc[...] = jnp.zeros_like(key_acc)
                value_acc[...] = jnp.zeros_like(value_acc)
            key_acc[:seen] += key_grad
            value_acc[:seen] += value_grad
        key_grad = key_acc[...]
        joint_ref[:, cols + h * HD : cols + (h + 1) * HD] = (
            key_grad * cos_ref[...] - swap_halves(key_grad) * sin_ref[...]
        ).astype(bf16)
        joint_ref[:, 2 * cols + h * HD : 2 * cols + (h + 1) * HD] = value_acc[...].astype(bf16)

    last = heads - 1
    for h in range(heads):
        head_back(h)
        if h == 0:
            stage(2)
            results_across()
        if h == min(1, last):
            results_away(0)
        if h == last:
            stage(3)
            results_away(1)

    depth = width // NFFN
    grads_ref[:, : 3 * cols] = dotf(
        rows1_ref[...].reshape(everyone, width), joint_ref[...], TN
    )
    if inside:
        lean = lax.rem(near, 2)
        tall = grads_ref[...].reshape(NFFN // 2, 2, depth, grads_ref.shape[1])
        keep = jnp.where(lean == 0, tall[:, 0], tall[:, 1])
        across_out[...] = jnp.where(lean == 0, tall[:, 1], tall[:, 0]).astype(bf16)
        over = remote(across_out, across_in, wsend.at[0], wrecv.at[0], dp=base + flip(near, 1))
        over.start()
    else:
        wgrad_ref[...] = grads_ref[...]
    stage(4)

    trip = Scatter(mp_me, xcore_out, xcore_in, xchip_out, xchip_in, xsend, xrecv)

    def x_block(q):
        at = pl.ds(pl.multiple_of(q * rows, rows), rows)
        return dotf(joint_ref[at], w_all[:, : 3 * cols], NT)

    normed_grad = trip.run(x_block)
    if inside:
        over.wait_recv()
        along_out[...] = (keep + across_in[...].astype(f32)).astype(bf16)
        up = near // 2
        alongs = [
            remote(along_out.at[flip(near, k) // 2], along_in.at[k // 2], wsend.at[k], wrecv.at[k],
                   dp=base + flip(near, k))
            for k in (4, 6, 2)
        ]
        for copy in alongs:
            copy.start()
    tokens = x_ref[...].astype(f32)
    scale = lax.rsqrt(jnp.mean(tokens * tokens, axis=-1, keepdims=True) + epsilon)
    scaled = tokens * scale
    first_out[0] = jnp.sum(normed_grad * scaled, axis=0, keepdims=True)
    firsts = [
        remote(first_out.at[0], first_mp.at[k], fsend.at[k], frecv.at[k], mp=flip(mp_me, k))
        for k in range(1, MP)
    ]
    for copy in firsts:
        copy.start()
    weighted = normed_grad * params_ref[23:24]
    xgrad_ref[...] = hgrad_ref[...] + scale * (
        weighted - scaled * jnp.mean(weighted * scaled, axis=-1, keepdims=True)
    )
    for copy in firsts:
        copy.wait_recv()
    first_out[1] = first_out[0] + first_mp[1] + first_mp[2] + first_mp[3]
    seconds = [
        remote(first_out.at[1], first_dp.at[k], fsend.at[MP + k], frecv.at[MP + k],
               dp=base + flip(near, k))
        for k in range(1, NFFN)
    ]
    for copy in seconds:
        copy.start()
    stage(5)
    for copy in returns.values():
        copy.wait_recv()
    routed = combine.run(out_block)
    output_ref[...] = (residual_ref[...] + routed).astype(bf16)
    if inside:
        for copy in alongs:
            copy.wait_recv()
        wgrad_ref[...] = along_out[up].astype(f32) + (
            along_in[1].astype(f32) + along_in[2].astype(f32) + along_in[3].astype(f32)
        )
    for copy in seconds:
        copy.wait_recv()
    total = first_out[1]
    for k in range(1, NFFN):
        total = total + first_dp[k]
    first_ref[...] = total

    for copy in moved:
        copy.wait_recv()
    for copy in mine:
        copy.wait()
    if inside:
        for copy in [over] + alongs:
            copy.wait_send()
    for copy in moved + p_core + p_chip + list(returns.values()) + stages + firsts + seconds:
        copy.wait_send()
    combine.drain()
    trip.drain()


def attention_back(
    agrad, hgrad, x, params, rows1, w, q, k, v, mixed, lse, pick, gate, residual, outp, small, dw,
    groups,
):
    rows, width = x.shape
    everyone = MP * rows
    cos, sin = rope_constants()
    inside = groups == 1
    cols = w.shape[-1]
    heads = q.shape[0]
    depth = width // NFFN
    hidden_cols = dw.shape[-1]
    sd = jax.ShapeDtypeStruct
    vm = pltpu.VMEM
    dma = pltpu.SemaphoreType.DMA
    outs = [
        sd((rows, width), bf16),
        sd((rows, width), f32),
        sd((depth if inside else width, cols), f32),
        sd((40, width), f32),
        sd((1, width), f32),
        sd((NFFN, 3, depth, hidden_cols), bf16),
    ]
    return pl.pallas_call(
        functools.partial(back_kernel, inside),
        out_shape=outs,
        in_specs=[VM] * 19,
        out_specs=[VM] * 5 + [HB],
        scratch_shapes=[
            vm((MP, rows, width), bf16),
            vm((everyone, heads * HD), bf16),
            vm((everyone, 3 * heads * HD), bf16),
            vm((everyone, HD), f32),
            vm((everyone, HD), f32),
            vm((width, cols), f32),
            vm((NFFN // 2, depth, cols), bf16),
            vm((NFFN // 2, depth, cols), bf16),
            vm((NFFN // 2, depth, cols), bf16),
            vm((NFFN // 2, depth, cols), bf16),
            vm((NFFN, QUARTER, width), bf16),
            vm((2, rows, width), bf16),
            vm((2, rows, width), bf16),
            vm((rows, width), bf16),
            vm((rows, width), bf16),
            vm((2, rows, width), bf16),
            vm((2, rows, width), bf16),
            vm((rows, width), bf16),
            vm((rows, width), bf16),
            vm((5, 40, width), f32),
            vm((5, 40, width), f32),
            vm((MP, 1, width), f32),
            vm((NFFN, 1, width), f32),
            vm((2, 1, width), f32),
            vm((2, NFFN, QUARTER, width), bf16),
            vm((NFFN, QUARTER, width), bf16),
            vm((NFFN, QUARTER, width), bf16),
            vm((NFFN, QUARTER, width), bf16),
            dma((3,)), dma((3,)),
            dma((8,)), dma((8,)),
            dma((8,)), dma((8,)),
            dma((4,)), dma((4,)), dma((8,)),
            dma((3,)), dma((3,)),
            dma((3,)), dma((3,)),
            dma((8,)), dma((8,)),
            dma((5,)), dma((5,)),
            dma((MP + NFFN,)), dma((MP + NFFN,)),
        ],
        compiler_params=pltpu.CompilerParams(
            collective_id=1, has_side_effects=True, vmem_limit_bytes=60 * 2**20
        ),
        name="attention_backward",
    )(
        agrad, hgrad, x, params, jnp.asarray(cos), jnp.asarray(sin), rows1, w, q, k, v, mixed, lse,
        pick, gate, residual, outp, small, dw,
    )


def clusters():
    groups = lax.axis_size("dp") // NFFN
    near = [[group * NFFN + expert for expert in range(NFFN)] for group in range(groups)]
    far = [[group * NFFN + expert for group in range(groups)] for expert in range(NFFN)]
    return groups, near, far


def exchange(shard, dim):
    _, near, far = clusters()
    own = lax.all_to_all(shard, "dp", 0, dim, axis_index_groups=near, tiled=True)
    return lax.all_gather(own, "dp", axis=dim, axis_index_groups=far, tiled=True)


def exchange_back(grads, dim):
    _, near, far = clusters()
    grads = lax.psum_scatter(
        grads.astype(f32), "dp", scatter_dimension=dim, axis_index_groups=far, tiled=True
    )
    return lax.all_to_all(grads.astype(bf16), "dp", dim, 0, axis_index_groups=near, tiled=True)


def per_device(
    inputs,
    query_key_value,
    output_weight,
    expert_input,
    expert_output,
    first_gain,
    second_gain,
    router_weight,
    logit_carry,
    constant_mix,
    constant_values,
    previous_logits,
    routes,
    cotangent,
):
    rows, width = inputs.shape
    groups, _, far = clusters()

    def padded(array, high, wide, value=0.0):
        return jnp.pad(
            array.astype(f32), ((0, high - array.shape[0]), (0, wide - array.shape[1])),
            constant_values=value,
        )

    params = jnp.concatenate(
        [
            padded(router_weight.T, 16, width),
            constant_mix.T.astype(f32),
            constant_values.astype(f32),
            second_gain.astype(f32)[None],
            first_gain.astype(f32)[None],
            padded(logit_carry, 16, width),
        ],
        axis=0,
    )
    everyone = rows * MP
    routing = jnp.concatenate(
        [padded(previous_logits.T, 16, everyone), padded(routes.T, 8, everyone, -1.0)], axis=0
    )
    shard_depth = query_key_value.shape[0]
    shard = jnp.concatenate(
        [query_key_value.reshape(shard_depth, -1), output_weight.T], axis=1
    )
    cols = output_weight.shape[0]
    expert_output_t = expert_output.transpose(0, 2, 1)
    if groups > 1:
        shard = lax.all_gather(shard, "dp", axis=0, tiled=True)
        win = exchange(expert_input, 2)[0]
        wout = exchange(expert_output_t, 1)[0]
    if groups == 1:
        win, wout = expert_input, expert_output_t
    (rows1, w, q, k, v, mixed, lse, residual, hidden_grad, attended_grad, logits_grad, small, pick,
     gate, outp, dw) = forward(
        inputs, cotangent, params, routing, shard, win, wout, groups
    )
    output, input_grad, weight_grad, sums, first_grad, expert_grad = attention_back(
        attended_grad, hidden_grad, inputs, params, rows1, w, q, k, v, mixed, lse, pick, gate,
        residual, outp, small, dw, groups,
    )
    if groups > 1:
        weight_grad = lax.psum_scatter(weight_grad, "dp", scatter_dimension=0, tiled=True)
        whole = expert_grad.transpose(1, 0, 2, 3).reshape(1, 3, width, -1)
        expert_grad = exchange_back(whole, 2)
        sums, first_grad = lax.psum((sums, first_grad), "dp", axis_index_groups=far)
    expert_in_grad = expert_grad[:, :2].astype(f32)
    expert_out_grad = expert_grad[:, 2].transpose(0, 2, 1).astype(f32)
    return (
        output,
        input_grad,
        logits_grad[:NEXP].T,
        weight_grad[:, : 3 * cols].reshape(shard_depth, 3, cols),
        weight_grad[:, 3 * cols :].T,
        expert_in_grad,
        expert_out_grad,
        first_grad[0],
        sums[22],
        sums[:NEXP].T,
        sums[24 : 24 + NEXP, :NEXP],
        sums[16:20].T,
        sums[20:22],
    )


def solution(mesh):
    in_specs = (
        P(("dp", "mp"), None),
        P("dp", None, "mp"),
        P("mp", "dp"),
        P(None, None, "dp", "mp"),
        P(None, "mp", "dp"),
        P(),
        P(),
        P(),
        P(),
        P(),
        P(),
        P("dp", None),
        P("dp", None),
        P(("dp", "mp"), None),
    )
    out_specs = (
        P(("dp", "mp"), None),
        P(("dp", "mp"), None),
        P(("dp", "mp"), None),
        P("dp", None, "mp"),
        P("mp", "dp"),
        P(None, None, "dp", "mp"),
        P(None, "mp", "dp"),
        P(),
        P(),
        P(),
        P(),
        P(),
        P(),
    )
    return jax.shard_map(
        per_device, mesh=mesh, in_specs=in_specs, out_specs=out_specs, check_vma=False
    )
```

```python
import functools
import numpy as np
import jax
import jax.numpy as jnp
from jax import lax
from jax.sharding import PartitionSpec as P
from jax.experimental import pallas as pl
from jax.experimental.pallas import tpu as pltpu

HD = 64
NFFN = 8
NEXP = 12
SEQ = 1024
CAP = 256
MP = 4
QUARTER = CAP // MP
WIDE = 640
VMEM_LIMIT = 62 * 2**20

epsilon = 1e-06
rope_base = 10000.0
highest = lax.Precision.HIGHEST
f32 = jnp.float32
bf16 = jnp.bfloat16
MESH = pl.DeviceIdType.MESH
VM = pl.BlockSpec(memory_space=pltpu.VMEM)
HB = pl.BlockSpec(memory_space=pl.ANY)
NT = (((1,), (1,)), ((), ()))
TN = (((0,), (0,)), ((), ()))


def flip(index, distance):
    out = index
    bit = 1
    while bit <= distance:
        if distance & bit:
            out = out + bit - 2 * bit * ((index // bit) % 2)
        bit *= 2
    return out


def dotf(a, b, dims=None):
    if dims is None:
        return jnp.dot(a, b, preferred_element_type=f32)
    return lax.dot_general(a, b, dims, preferred_element_type=f32)


def remote(src, dst, send, recv, **where):
    return pltpu.make_async_remote_copy(
        src_ref=src, dst_ref=dst, send_sem=send, recv_sem=recv, device_id=where, device_id_type=MESH
    )


def greet(mp_me, near, base):
    barrier = pltpu.get_barrier_semaphore()
    for k in range(1, MP):
        pl.semaphore_signal(barrier, inc=1, device_id={"mp": flip(mp_me, k)}, device_id_type=MESH)
    for k in range(1, NFFN):
        pl.semaphore_signal(
            barrier, inc=1, device_id={"dp": base + flip(near, k)}, device_id_type=MESH
        )
    pl.semaphore_wait(barrier, MP - 1 + NFFN - 1)


def rope_constants():
    half = HD // 2
    positions = np.arange(SEQ, dtype=np.float32)
    frequency = (rope_base ** (-np.arange(half, dtype=np.float32) / half)).astype(np.float32)
    angles = (positions[:, None] * frequency[None, :]).astype(np.float32)
    cosine, sine = np.cos(angles), np.sin(angles)
    return (
        np.concatenate([cosine, cosine], axis=1),
        np.concatenate([-sine, sine], axis=1),
    )


def swap_halves(x):
    half = HD // 2
    return jnp.concatenate([x[:, half:], x[:, :half]], axis=1)


class Gather:
    def __init__(self, ref, mp_me, send, recv):
        self.me, self.core, self.chip = mp_me, flip(mp_me, 1), flip(mp_me, 2)
        own = ref.at[mp_me]
        far = ref.at[self.chip]
        self.to_chip = remote(own, own, send.at[0], recv.at[0], mp=self.chip)
        self.to_core = remote(own, own, send.at[1], recv.at[1], mp=self.core)
        self.relay = remote(far, far, send.at[2], recv.at[2], mp=self.core)

    def start(self):
        self.to_chip.start()
        self.to_core.start()

    def forward(self):
        self.to_chip.wait_recv()
        self.relay.start()

    def finish(self):
        self.to_core.wait_recv()
        self.relay.wait_recv()
        self.to_chip.wait_send()
        self.to_core.wait_send()
        self.relay.wait_send()


def pack3(value):
    high = value.astype(bf16).astype(f32)
    rest = value - high
    mid = rest.astype(bf16).astype(f32)
    low = (rest - mid).astype(bf16).astype(f32)
    lane = lax.broadcasted_iota(jnp.int32, (value.shape[0], 128), 1)
    return jnp.where(
        lane == 0, high, jnp.where(lane == 1, mid, jnp.where(lane == 2, low, 0.0))
    ).astype(bf16)


def unpack3(parts):
    return jnp.sum(parts.astype(f32), axis=-1, keepdims=True)


def exact(left, right, dims=None):
    high = left.astype(bf16)
    rest = left - high.astype(f32)
    mid = rest.astype(bf16)
    low = (rest - mid.astype(f32)).astype(bf16)
    return dotf(high, right, dims) + (dotf(mid, right, dims) + dotf(low, right, dims))


class Scatter:
    def __init__(self, mp_me, core_out, core_in, chip_out, chip_in, send, recv):
        self.me, self.core, self.chip = mp_me, flip(mp_me, 1), flip(mp_me, 2)
        self.core_out, self.core_in = core_out, core_in
        self.chip_out, self.chip_in = chip_out, chip_in
        self.to_core = [
            remote(core_out.at[j], core_in.at[j], send.at[j], recv.at[j], mp=self.core)
            for j in range(2)
        ]
        self.to_chip = remote(chip_out, chip_in, send.at[2], recv.at[2], mp=self.chip)

    def run(self, blocks):
        for j, block in enumerate((flip(self.me, 3), self.core)):
            self.core_out[j] = blocks(block).astype(bf16)
            self.to_core[j].start()
        term = blocks(self.chip)
        self.to_core[0].wait_recv()
        self.chip_out[...] = (term + self.core_in[0].astype(f32)).astype(bf16)
        self.to_chip.start()
        term = blocks(self.me)
        self.to_core[1].wait_recv()
        term = term + self.core_in[1].astype(f32)
        self.to_chip.wait_recv()
        return term + self.chip_in[...].astype(f32)

    def drain(self):
        for copy in self.to_core + [self.to_chip]:
            copy.wait_send()


def layer_kernel(
    inside,
    x_ref, cot_ref, params_ref, routing_ref, cos_ref, sin_ref, wshard_ref, win_shard, wout_shard,
    output_ref, xgrad_ref, lgrad_ref, wgrad_ref, sums_ref, first_ref, dw_own,
    rows1_ref, w_ref, q_ref, k_ref, v_ref, mixed_ref, lse_ref, pick_ref, gate_ref, outp_ref, dw_ref,
    rows2_ref, hidden_ref, sum_ref, core_in, chip_out, chip_in, core_out,
    place_ref, gates_ref, prior_ref, msgx, msgc, xs, cs, units_ref, pgrad_ref,
    part_ref, keep_ref, gcore_out, gcore_in, gchip_out, gchip_in, gret, score_out, score_in,
    ncore_in, nchip_in,
    key_acc, value_acc, grads_ref, across_out, across_in, along_in, ret_ref,
    sum_out, sum_in, first_mp, first_dp, first_out,
    sends, recvs, wsend, wrecv, esend, erecv, local,
    csend, crecv, xsend, xrecv, dsend, drecv, xgs, xgr, cgs, cgr, gsend, grecv,
    rsend, rrecv, ssend, srecv, nsend, nrecv,
    asend, arecv, osend, orecv, msend, mrecv, psend, precv, mlocal, bsend, brecv, tsend, trecv,
    vsend, vrecv, zsend, zrecv, fsend, frecv,
):
    cot_all = rows2_ref
    residual_ref = sum_ref
    hgrad_ref = xgrad_ref
    small_ref = sum_out.at[0]
    mp_me = lax.axis_index("mp")
    dp_me = lax.axis_index("dp")
    near = lax.rem(dp_me, NFFN)
    base = dp_me - near
    core, chip, far = flip(mp_me, 1), flip(mp_me, 2), flip(mp_me, 3)
    rows, width = x_ref.shape
    everyone = MP * rows
    greet(mp_me, near, base)

    tokens = x_ref[...].astype(f32)
    scale = lax.rsqrt(jnp.mean(tokens * tokens, axis=-1, keepdims=True) + epsilon)
    rows1_ref[mp_me] = (tokens * scale * params_ref[23:24]).astype(bf16)
    gather1 = Gather(rows1_ref, mp_me, sends.at[pl.ds(0, 3)], recvs.at[pl.ds(0, 3)])
    gather1.start()
    if inside:
        w_ref[near] = wshard_ref[...]
        own = w_ref.at[near]
        along = [
            remote(own, own, wsend.at[k], wrecv.at[k], dp=base + flip(near, k)) for k in (2, 4, 6)
        ]
        for copy in along:
            copy.start()
        mate = base + flip(near, 1)
        across = [remote(own, own, wsend.at[0], wrecv.at[0], dp=mate)]
        across[0].start()
    cot_all[mp_me] = cot_ref[...]
    cot_gather = Gather(cot_all, mp_me, csend, crecv)
    cot_gather.start()

    ids = lax.broadcasted_iota(jnp.int32, (16, everyone), 0).astype(f32)
    chosen = (ids == routing_ref[16:17]) | (ids == routing_ref[17:18])
    earlier = lax.broadcasted_iota(jnp.int32, (everyone, everyone), 0) < lax.broadcasted_iota(
        jnp.int32, (everyone, everyone), 1
    )
    counts = dotf(
        jnp.where(chosen, 1.0, 0.0).astype(bf16), jnp.where(earlier, 1.0, 0.0).astype(bf16)
    )
    place_ref[...] = jnp.where(chosen, counts, -1.0)
    wanted = (lax.broadcasted_iota(jnp.int32, (QUARTER, everyone), 0) + QUARTER * mp_me).astype(f32)

    def target(k):
        return lax.rem(near + k, NFFN)

    def choose(k, carried):
        pick = wanted == place_ref[pl.ds(target(k), 1)]
        pick_ref[k] = jnp.where(pick, 1.0, 0.0).astype(bf16)
        return carried

    lax.fori_loop(0, NFFN, choose, 0)
    carry = params_ref[24:40, 0:16]
    prior_ref[...] = lax.dot_general(
        carry, routing_ref[0:16], TN, preferred_element_type=f32, precision=highest
    )

    if inside:
        for k, copy in zip((2, 4, 6), along):
            copy.wait_recv()
            block = w_ref.at[flip(near, k)]
            onward = remote(block, block, wsend.at[k + 1], wrecv.at[k + 1], dp=mate)
            onward.start()
            across.append(onward)
        gather1.forward()
        for copy in across:
            copy.wait_recv()
        for copy in along + across:
            copy.wait_send()
        weights = []
        din = win_shard.shape[2]
        place = pl.ds(pl.multiple_of(near * din, din), din)
        for k in (4, 2, 6, 5, 7, 3, 1):
            peer = flip(near, k)
            for i, (src, dst) in enumerate([
                (win_shard.at[peer], dw_ref.at[0:2, place]),
                (wout_shard.at[peer], dw_ref.at[2, place]),
            ]):
                weights.append(
                    remote(src, dst, esend.at[i, k], erecv.at[i, k], dp=base + peer)
                )
        first = 4
        for copy in weights[:first]:
            copy.start()
        mine = [
            pltpu.make_async_copy(win_shard.at[near], dw_ref.at[0:2, place], local.at[0]),
            pltpu.make_async_copy(wout_shard.at[near], dw_ref.at[2, place], local.at[1]),
        ]
        for copy in mine:
            copy.start()
    else:
        w_ref[...] = wshard_ref[...]
        mine = [
            pltpu.make_async_copy(win_shard, dw_ref.at[0:2], local.at[0]),
            pltpu.make_async_copy(wout_shard, dw_ref.at[2], local.at[1]),
        ]
        for copy in mine:
            copy.start()
        gather1.forward()
    gather1.finish()

    cot_gather.forward()
    cot_gather.finish()

    def c_copy(k):
        return remote(
            msgc.at[k], cs.at[k, mp_me], dsend.at[k], drecv.at[k], dp=base + target(k)
        )

    def send(picked, ref, copy, lanes):
        def half(i, carried):
            start = 4 - 4 * i
            blocks = dotf(pick_ref[pl.ds(start, 4)].reshape(4 * QUARTER, everyone), picked())
            ref[(pl.ds(start, 4),) + lanes] = blocks.astype(bf16).reshape(4, QUARTER, width)

            def go(k, inner):
                @pl.when(k > 0)
                def _():
                    copy(k).start()

                return inner

            return lax.fori_loop(start, start + 4, go, carried)

        lax.fori_loop(0, 2, half, 0)

    send(lambda: cot_all[...].reshape(everyone, width), msgc, c_copy, ())
    cs[0, mp_me] = msgc[0]
    if inside:
        for copy in weights[first:]:
            copy.start()

    w_all = w_ref[...].reshape(width, w_ref.shape[2])
    heads = q_ref.shape[0]
    cols = heads * HD

    def project(i, carry):
        at = pl.ds(pl.multiple_of(i * rows, rows), rows)
        joint = dotf(rows1_ref[i], w_all[:, : 3 * cols])
        cosine, sine = cos_ref[at], sin_ref[at]
        for h in range(heads):
            query = joint[:, h * HD : (h + 1) * HD]
            key = joint[:, cols + h * HD : cols + (h + 1) * HD]
            q_ref[h, at] = (query * cosine + swap_halves(query) * sine).astype(bf16)
            k_ref[h, at] = (key * cosine + swap_halves(key) * sine).astype(bf16)
            v_ref[h, at] = joint[:, 2 * cols + h * HD : 2 * cols + (h + 1) * HD].astype(bf16)
        return carry

    lax.fori_loop(0, MP, project, 0)
    out_weight = w_all[:, 3 * cols :]

    to_core = [
        remote(core_out.at[j], core_in.at[j], sends.at[3 + j], recvs.at[3 + j], mp=core)
        for j in range(2)
    ]
    to_chip = remote(chip_out, chip_in, sends.at[5], recvs.at[5], mp=chip)

    def attend(step, carry):
        block = flip(mp_me, 3)
        block = jnp.where(step == 1, core, jnp.where(step == 2, chip, jnp.where(step == 3, mp_me, block)))
        at = pl.ds(pl.multiple_of(block * rows, rows), rows)
        row_ids = block * rows + lax.broadcasted_iota(jnp.int32, (rows, SEQ), 0)
        seen = row_ids >= lax.broadcasted_iota(jnp.int32, (rows, SEQ), 1)
        for h in range(heads):
            scores = dotf(q_ref[h, at], k_ref[h], NT) * HD**-0.5
            scores = jnp.where(seen, scores, -jnp.inf)
            peak = jnp.max(scores, axis=-1, keepdims=True)
            exponent = jnp.exp(scores - peak)
            total = jnp.sum(exponent, axis=-1, keepdims=True)
            probs = (exponent * (1.0 / total)).astype(bf16)
            mixed_ref[at, h * HD : (h + 1) * HD] = dotf(probs, v_ref[h]).astype(bf16)
            lse_ref[at, h : h + 1] = peak + jnp.log(total)
        part = dotf(mixed_ref[at], out_weight, NT)

        @pl.when(step == 0)
        def _():
            core_out[0] = part.astype(bf16)
            to_core[0].start()

        @pl.when(step == 1)
        def _():
            core_out[1] = part.astype(bf16)
            to_core[1].start()

        @pl.when(step == 2)
        def _():
            to_core[0].wait_recv()
            chip_out[...] = (part + core_in[0].astype(f32)).astype(bf16)
            to_chip.start()

        @pl.when(step == 3)
        def _():
            sum_ref[...] = part

        return carry

    lax.fori_loop(0, MP, attend, 0)
    to_core[1].wait_recv()
    partial = sum_ref[...] + core_in[1].astype(f32)
    to_chip.wait_recv()
    hidden = x_ref[...].astype(f32) + (partial + chip_in[...].astype(f32))
    hidden_ref[...] = hidden
    scale2 = lax.rsqrt(jnp.mean(hidden * hidden, axis=-1, keepdims=True) + epsilon)
    rows2_ref[mp_me] = (hidden * scale2 * params_ref[22:23]).astype(bf16)
    gather2 = Gather(rows2_ref, mp_me, sends.at[pl.ds(6, 3)], recvs.at[pl.ds(6, 3)])
    gather2.start()
    for copy in to_core + [to_chip]:
        copy.wait_send()
    gather2.forward()

    def turn(i):
        return lax.rem(i + 4, NFFN)

    def c_gather(k):
        return Gather(cs.at[k], mp_me, cgs.at[k], cgr.at[k])

    def at_step(i, first, body):
        @pl.when((i >= first) & (i < NFFN + first))
        def _():
            body(turn(i - first))

    def cot_step(i, carried):
        def arrived(k):
            @pl.when(k > 0)
            def _():
                c_copy(k).wait_recv()

            c_gather(k).start()

        at_step(i, 0, arrived)
        at_step(i, 1, lambda k: c_gather(k).forward())
        return carried

    lax.fori_loop(0, NFFN + 1, cot_step, 0)
    gather2.finish()

    router = params_ref[0:16].astype(bf16)
    mix = params_ref[16:20].astype(bf16)
    tokens = rows2_ref[...].reshape(everyone, width)
    logits = dotf(router, tokens, NT) + prior_ref[...]
    masked = jnp.where(place_ref[...] >= 0.0, logits, -jnp.inf)
    exponent = jnp.exp(masked - jnp.max(masked, axis=0, keepdims=True))
    gates_ref[...] = exponent / jnp.sum(exponent, axis=0, keepdims=True)

    def weigh(k, carried):
        gate = jnp.sum(
            pick_ref[k].astype(f32) * gates_ref[pl.ds(target(k), 1)], axis=1, keepdims=True
        )
        gate_ref[k] = jnp.broadcast_to(gate, (QUARTER, 128))
        msgx[k, :, width:] = pack3(gate)
        return carried

    lax.fori_loop(0, NFFN, weigh, 0)

    def x_copy(k):
        return remote(
            msgx.at[k], xs.at[k, mp_me], xsend.at[k], xrecv.at[k], dp=base + target(k)
        )

    send(
        lambda: rows2_ref[...].reshape(everyone, width), msgx, x_copy,
        (slice(None), slice(0, width)),
    )
    xs[0, mp_me] = msgx[0]

    def x_gather(k):
        return Gather(xs.at[k], mp_me, xgs.at[k], xgr.at[k])

    def slots_of(k):
        return pl.ds(pl.multiple_of(k * CAP, CAP), CAP)

    def x_step(i, carried):
        def arrived(k):
            @pl.when(k > 0)
            def _():
                x_copy(k).wait_recv()

            x_gather(k).start()

        def passed(k):
            x_gather(k).forward()

        at_step(i, 0, arrived)
        at_step(i, 1, passed)
        return carried

    lax.fori_loop(0, NFFN + 1, x_step, 0)
    if inside:
        for copy in weights:
            copy.wait_recv()
    for copy in mine:
        copy.wait()

    def r_trip(k):
        slot = lax.rem(k, 4)
        return Scatter(
            mp_me, gcore_out.at[slot], gcore_in.at[k], gchip_out.at[slot], gchip_in.at[k],
            gsend.at[k], grecv.at[k],
        )

    def g_copy(k):
        return remote(
            msgx.at[k], gret.at[k], rsend.at[k], rrecv.at[k],
            dp=base + lax.rem(near - k + NFFN, NFFN),
        )

    def seal(ref, index, total):
        ref[index + (slice(None), slice(0, width))] = total[:, :width].astype(bf16)
        ref[index + (slice(None), slice(width, None))] = pack3(unpack3(total[:, width:]))

    def expert_step(i, carried):
        def compute(k):
            c_gather(k).finish()
            x_gather(k).finish()
            x = xs[k].reshape(CAP, width + 128)[:, :width]
            gate = unpack3(xs[k].reshape(CAP, width + 128)[:, width:])
            c = cs[k].reshape(CAP, width)
            gate_pre = dotf(x, dw_ref[0])
            up_pre = dotf(x, dw_ref[1])
            sig = jax.nn.sigmoid(gate_pre)
            units = (gate_pre * sig * up_pre).astype(bf16)
            units_ref[slots_of(k)] = units
            outp_ref[k] = dotf(units, dw_ref[2], NT).astype(bf16).reshape(MP, QUARTER, width)
            raw = dotf(c, dw_ref[2])
            score = jnp.sum(units.astype(f32) * raw, axis=1, keepdims=True)
            units_grad = raw * gate
            gate_grad = (units_grad * up_pre * sig * (1.0 + gate_pre * (1.0 - sig))).astype(bf16)
            up_grad = (units_grad * (gate_pre * sig)).astype(bf16)
            pgrad_ref[0, slots_of(k)] = gate_grad
            pgrad_ref[1, slots_of(k)] = up_grad
            back = dotf(gate_grad, dw_ref[0], NT) + dotf(up_grad, dw_ref[1], NT)
            cs[k] = (c.astype(f32) * gate).astype(bf16).reshape(MP, QUARTER, width)
            part_ref[:, :, :width] = back.reshape(MP, QUARTER, width)
            part_ref[:, :, width:] = pack3(score).astype(f32).reshape(MP, QUARTER, 128)
            slot = lax.rem(k, 4)
            gcore_out[slot, 0] = part_ref[far].astype(bf16)
            gcore_out[slot, 1] = part_ref[core].astype(bf16)
            keep_ref[slot, 0] = part_ref[chip]
            keep_ref[slot, 1] = part_ref[mp_me]
            for copy in r_trip(k).to_core:
                copy.start()

        def across(k):
            trip = r_trip(k)
            trip.to_core[0].wait_recv()
            seal(gchip_out, (lax.rem(k, 4),), keep_ref[lax.rem(k, 4), 0] + gcore_in[k, 0].astype(f32))
            trip.to_chip.start()

        def away(k):
            trip = r_trip(k)
            trip.to_core[1].wait_recv()
            trip.to_chip.wait_recv()
            total = (
                keep_ref[lax.rem(k, 4), 1]
                + gcore_in[k, 1].astype(f32)
                + gchip_in[k].astype(f32)
            )
            trip.drain()

            @pl.when(k > 0)
            def _():
                x_copy(k).wait_send()

            seal(msgx, (k,), total)

            @pl.when(k > 0)
            def _():
                g_copy(k).start()

            @pl.when(k == 0)
            def _():
                gret[0] = msgx[0]

        at_step(i, 4, away)
        at_step(i, 0, compute)
        at_step(i, 2, across)
        return carried

    lax.fori_loop(0, NFFN + 4, expert_step, 0)

    def weights_step(j, carried):
        at = pl.ds(pl.multiple_of(j * 128, 128), 128)
        x = xs[:, :, :, at].reshape(NFFN * CAP, 128)
        c = cs[:, :, :, at].reshape(NFFN * CAP, 128)
        dw_ref[0, at] = dotf(x, pgrad_ref[0], TN).astype(bf16)
        dw_ref[1, at] = dotf(x, pgrad_ref[1], TN).astype(bf16)
        dw_ref[2, at] = dotf(c, units_ref[...], TN).astype(bf16)
        return carried

    lax.fori_loop(0, width // 128, weights_step, 0)

    din = dw_own.shape[2]

    def rows_of(index):
        return pl.ds(pl.multiple_of(index * din, din), din)

    if inside:
        moved = [
            remote(dw_ref.at[:, rows_of(flip(near, k))], dw_own.at[near], msend.at[k],
                   mrecv.at[k], dp=base + flip(near, k))
            for k in (4, 6, 5, 7, 2, 3, 1)
        ]
        kept = [pltpu.make_async_copy(dw_ref.at[:, rows_of(near)], dw_own.at[near], mlocal.at[0])]
    else:
        moved = []
        kept = [
            pltpu.make_async_copy(dw_ref.at[:, rows_of(p)], dw_own.at[p], mlocal.at[p])
            for p in range(NFFN)
        ]
    for copy in moved + kept:
        copy.start()

    n_bf = rows2_ref[mp_me]
    n = n_bf.astype(f32)
    cot = cot_ref[...].astype(f32)
    hidden = hidden_ref[...]
    lane = lax.broadcasted_iota(jnp.int32, (rows, 128), 1)
    own_at = pl.ds(pl.multiple_of(mp_me * rows, rows), rows)
    gates_t = gates_ref[:, own_at]
    own_gates = jnp.concatenate([gates_t, jnp.zeros((112, rows), f32)], axis=0).T
    copy_gate = own_gates[:, NFFN + 1 : NFFN + 2]
    const_gates = [own_gates[:, NFFN + 2 : NFFN + 3], own_gates[:, NFFN + 3 : NFFN + 4]]
    mix_logits = dotf(n_bf, mix, NT)
    with_normed = jnp.sum(cot * n, axis=1, keepdims=True)
    residual = hidden + copy_gate * n
    local_grad = copy_gate * cot
    local_scores = jnp.where(lane == NFFN + 1, with_normed, 0.0)
    mix_grads = jnp.zeros((rows, 128), f32)
    for c in range(2):
        first, second = mix_logits[:, 2 * c : 2 * c + 1], mix_logits[:, 2 * c + 1 : 2 * c + 2]
        top = jnp.maximum(first, second)
        first, second = jnp.exp(first - top), jnp.exp(second - top)
        share = 1.0 / (first + second)
        first, second = first * share, second * share
        constant = params_ref[20 + c : 21 + c]
        with_constant = jnp.sum(cot * constant, axis=1, keepdims=True)
        gate = const_gates[c]
        residual = residual + gate * (first * n + second * constant)
        local_scores = jnp.where(
            lane == NFFN + 2 + c, first * with_normed + second * with_constant, local_scores
        )
        local_grad = local_grad + (first * gate) * cot
        small_ref[20 + c : 21 + c] = jnp.sum((second * gate) * cot, axis=0, keepdims=True)
        grad_first, grad_second = gate * with_normed, gate * with_constant
        mean = first * grad_first + second * grad_second
        mix_grads = jnp.where(lane == 2 * c, first * (grad_first - mean), mix_grads)
        mix_grads = jnp.where(lane == 2 * c + 1, second * (grad_second - mean), mix_grads)
    residual_ref[...] = residual

    def returned(k, carried):
        g_copy(k).wait_recv()
        return carried

    lax.fori_loop(1, NFFN, returned, 0)
    ret = gret[...].reshape(NFFN * QUARTER, width + 128)
    score_out[...] = jnp.zeros_like(score_out)

    def give_scores(k, carried):
        slots = unpack3(gret[k, :, width:])
        row = jnp.sum(pick_ref[k].astype(f32) * slots, axis=0, keepdims=True)
        for q in range(MP):
            score_out[q, pl.ds(target(k), 1)] = row[:, q * rows : (q + 1) * rows]
        return carried

    lax.fori_loop(0, NFFN, give_scores, 0)
    score_copies = [
        remote(score_out.at[flip(mp_me, k)], score_in.at[k], ssend.at[k], srecv.at[k], mp=flip(mp_me, k))
        for k in range(1, MP)
    ]
    for copy in score_copies:
        copy.start()

    def grad_block(q):
        at = pl.ds(pl.multiple_of(q * rows, rows), rows)
        return dotf(
            pick_ref[:, :, at].reshape(NFFN * QUARTER, rows), ret[:, :width], TN
        )

    trip = Scatter(mp_me, core_out, ncore_in, chip_out, nchip_in, nsend, nrecv)
    normed_grad = trip.run(grad_block) + local_grad

    for copy in score_copies:
        copy.wait_recv()
    ffn_scores = (score_out[mp_me] + score_in[1]) + (score_in[2] + score_in[3])
    scores = local_scores.T[:16] + jnp.concatenate([ffn_scores, jnp.zeros((8, rows), f32)], axis=0)
    logit_grad = gates_t * (scores - jnp.sum(gates_t * scores, axis=0, keepdims=True))
    lgrad_ref[...] = lax.dot_general(
        carry, logit_grad, (((1,), (0,)), ((), ())),
        preferred_element_type=f32, precision=highest,
    )
    small_ref[24:40] = jnp.zeros((16, width), f32)
    small_ref[24:40, 0:16] = lax.dot_general(
        routing_ref[0:16, own_at], logit_grad, NT, preferred_element_type=f32, precision=highest
    )
    stacked = jnp.concatenate([logit_grad, mix_grads.T[:16]], axis=0)
    stack = params_ref[0:32]
    sublane = lax.broadcasted_iota(jnp.int32, (32, width), 0)
    stack = jnp.where(sublane < 20, stack, 0.0).astype(bf16)
    feature_grads = exact(stacked, n_bf)
    small_ref[0:20] = feature_grads[0:20]
    normed_grad = normed_grad + exact(stacked, stack, TN)
    scale = lax.rsqrt(jnp.mean(hidden * hidden, axis=-1, keepdims=True) + epsilon)
    scaled = hidden * scale
    small_ref[22:23] = jnp.sum(normed_grad * scaled, axis=0, keepdims=True)
    small_ref[23:24] = jnp.zeros((1, width), f32)
    weighted = normed_grad * params_ref[22:23]
    hidden_grad = cot + scale * (
        weighted - scaled * jnp.mean(weighted * scaled, axis=-1, keepdims=True)
    )
    hgrad_ref[...] = hidden_grad
    rows2_ref[mp_me] = hidden_grad.astype(bf16)
    agather = Gather(rows2_ref, mp_me, asend, arecv)
    agather.start()

    trip.drain()
    for copy in score_copies:
        copy.wait_send()

    def drain(k, carried):
        c_copy(k).wait_send()
        g_copy(k).wait_send()
        return carried

    lax.fori_loop(1, NFFN, drain, 0)
    if inside:
        for copy in weights:
            copy.wait_send()

    p_core = [
        remote(outp_ref.at[:, far], cs.at[:, 0], psend.at[0], precv.at[0], mp=core),
        remote(outp_ref.at[:, core], cs.at[:, 1], psend.at[1], precv.at[1], mp=core),
    ]
    for copy in p_core:
        copy.start()
    parts = (slice(4, 8), slice(0, 4))
    p_chip = [
        remote(cs.at[part, 3], cs.at[part, 2], psend.at[2 + j], precv.at[2 + j], mp=chip)
        for j, part in enumerate(parts)
    ]
    returns = {
        k: remote(msgc.at[k], ret_ref.at[k], osend.at[k], orecv.at[k],
                  dp=base + lax.rem(near - k + NFFN, NFFN))
        for k in range(1, NFFN)
    }

    def results_across():
        p_core[0].wait_recv()
        for j, part in enumerate(parts):
            cs[part, 3] = (
                outp_ref[part, chip].astype(f32) + cs[part, 0].astype(f32)
            ).astype(bf16)
            p_chip[j].start()

    def results_away(j):
        part = parts[j]
        if j == 0:
            p_core[1].wait_recv()
        p_chip[j].wait_recv()
        msgc[part] = (
            outp_ref[part, mp_me].astype(f32)
            + (cs[part, 1].astype(f32) + cs[part, 2].astype(f32))
        ).astype(bf16)
        for k in range(part.start, part.stop):
            if k > 0:
                returns[k].start()
            else:
                ret_ref[0] = msgc[0]

    places = [{"mp": flip(mp_me, 1)}, {"mp": flip(mp_me, 2)}] + [
        {"dp": base + flip(near, k)} for k in (1, 2, 4)
    ]
    stages = [
        remote(sum_out.at[j], sum_in.at[j], zsend.at[j], zrecv.at[j], **where)
        for j, where in enumerate(places)
    ]

    def stage(j):
        if j > 0:
            stages[j - 1].wait_recv()
            total = sum_out[j - 1] + sum_in[j - 1]
            if j == len(stages):
                sums_ref[...] = total
                return
            sum_out[j] = total
        stages[j].start()

    stage(0)
    agather.forward()
    stage(1)
    agather.finish()

    w_all = w_ref[...].reshape(width, w_ref.shape[2])
    out_weight = w_all[:, 3 * cols :]
    for i in range(MP):
        xs[i, :, :, WIDE : WIDE + cols] = (
            dotf(rows2_ref[i], out_weight).astype(bf16).reshape(MP, QUARTER, cols)
        )
    grads_ref[:, 3 * cols :] = dotf(rows2_ref[...].reshape(everyone, width), mixed_ref[...], TN)

    combine = Scatter(mp_me, core_out, ncore_in, chip_out, nchip_in, bsend, brecv)

    def out_block(q):
        at = pl.ds(pl.multiple_of(q * rows, rows), rows)
        weighted = (ret_ref[...].astype(f32) * gate_ref[:, :, 0:1]).astype(bf16)
        return dotf(
            pick_ref[:, :, at].reshape(NFFN * QUARTER, rows),
            weighted.reshape(NFFN * QUARTER, width), TN,
        )

    def head_back(h):
        lanes = slice(h * HD, (h + 1) * HD)
        for b in range(MP):
            at = slice(b * rows, (b + 1) * rows)
            seen = (b + 1) * rows
            query = q_ref[h, at]
            keys = k_ref[h, :seen]
            out_grad = xs[b, :, :, WIDE + h * HD : WIDE + (h + 1) * HD].reshape(rows, HD)
            scores = dotf(query, keys, NT) * HD**-0.5
            allowed = b * rows + lax.broadcasted_iota(
                jnp.int32, (rows, seen), 0
            ) >= lax.broadcasted_iota(jnp.int32, (rows, seen), 1)
            probs = jnp.where(allowed, jnp.exp(scores - lse_ref[at, h : h + 1]), 0.0)
            probs_grad = dotf(out_grad, v_ref[h, :seen], NT)
            inner = jnp.sum(probs * probs_grad, axis=1, keepdims=True)
            score_grad = (probs * (probs_grad - inner)).astype(bf16)
            query_grad = dotf(score_grad, keys) * HD**-0.5
            xs[b, :, :, lanes] = (
                (query_grad * cos_ref[at] - swap_halves(query_grad) * sin_ref[at])
                .astype(bf16)
                .reshape(MP, QUARTER, HD)
            )
            key_grad = dotf(score_grad, query, TN) * HD**-0.5
            value_grad = dotf(probs.astype(bf16), out_grad, TN)
            if b == 0:
                key_acc[...] = jnp.zeros_like(key_acc)
                value_acc[...] = jnp.zeros_like(value_acc)
            key_acc[:seen] += key_grad
            value_acc[:seen] += value_grad
        key_grad = key_acc[...]
        key_grad = key_grad * cos_ref[...] - swap_halves(key_grad) * sin_ref[...]
        xs[0:MP, :, :, cols + h * HD : cols + (h + 1) * HD] = key_grad.astype(bf16).reshape(
            MP, MP, QUARTER, HD
        )
        xs[0:MP, :, :, 2 * cols + h * HD : 2 * cols + (h + 1) * HD] = (
            value_acc[...].astype(bf16).reshape(MP, MP, QUARTER, HD)
        )

    last = heads - 1
    for h in range(heads):
        head_back(h)
        if h == 0:
            stage(2)
            results_across()
        if h == min(1, last):
            results_away(0)
        if h == last:
            stage(3)
            results_away(1)

    depth = width // NFFN
    grads_ref[:, : 3 * cols] = dotf(
        rows1_ref[...].reshape(everyone, width),
        xs[0:MP, :, :, 0 : 3 * cols].reshape(everyone, 3 * cols), TN,
    )
    if inside:
        lean = lax.rem(near, 2)
        tall = grads_ref[...].reshape(NFFN // 2, 2, depth, grads_ref.shape[1])
        keep = jnp.where(lean == 0, tall[:, 0], tall[:, 1])
        across_out[...] = jnp.where(lean == 0, tall[:, 1], tall[:, 0]).astype(bf16)
        over = remote(across_out, across_in, vsend.at[0], vrecv.at[0], dp=base + flip(near, 1))
        over.start()
    else:
        wgrad_ref[...] = grads_ref[...]
    stage(4)

    home = Scatter(mp_me, core_out, core_in, chip_out, chip_in, tsend, trecv)

    def x_block(q):
        joint = xs[q, :, :, 0 : 3 * cols].reshape(rows, 3 * cols)
        return dotf(joint, w_all[:, : 3 * cols], NT)

    normed_grad = home.run(x_block)
    home.drain()
    if inside:
        over.wait_recv()
        over.wait_send()
        across_out[...] = (keep + across_in[...].astype(f32)).astype(bf16)
        up = near // 2
        alongs = [
            remote(across_out.at[flip(near, k) // 2], along_in.at[k // 2], vsend.at[k], vrecv.at[k],
                   dp=base + flip(near, k))
            for k in (4, 6, 2)
        ]
        for copy in alongs:
            copy.start()
    tokens = x_ref[...].astype(f32)
    scale = lax.rsqrt(jnp.mean(tokens * tokens, axis=-1, keepdims=True) + epsilon)
    scaled = tokens * scale
    first_out[0] = jnp.sum(normed_grad * scaled, axis=0, keepdims=True)
    firsts = [
        remote(first_out.at[0], first_mp.at[k], fsend.at[k], frecv.at[k], mp=flip(mp_me, k))
        for k in range(1, MP)
    ]
    for copy in firsts:
        copy.start()
    weighted = normed_grad * params_ref[23:24]
    xgrad_ref[...] = hgrad_ref[...] + scale * (
        weighted - scaled * jnp.mean(weighted * scaled, axis=-1, keepdims=True)
    )
    for copy in firsts:
        copy.wait_recv()
    first_out[1] = first_out[0] + first_mp[1] + first_mp[2] + first_mp[3]
    seconds = [
        remote(first_out.at[1], first_dp.at[k], fsend.at[MP + k], frecv.at[MP + k],
               dp=base + flip(near, k))
        for k in range(1, NFFN)
    ]
    for copy in seconds:
        copy.start()
    stage(5)
    for copy in returns.values():
        copy.wait_recv()
    routed = combine.run(out_block)
    output_ref[...] = (residual_ref[...] + routed).astype(bf16)
    if inside:
        for copy in alongs:
            copy.wait_recv()
        wgrad_ref[...] = across_out[up].astype(f32) + (
            along_in[1].astype(f32) + along_in[2].astype(f32) + along_in[3].astype(f32)
        )
    for copy in seconds:
        copy.wait_recv()
    total = first_out[1]
    for k in range(1, NFFN):
        total = total + first_dp[k]
    first_ref[...] = total

    for copy in moved:
        copy.wait_recv()
    for copy in kept:
        copy.wait()
    if inside:
        for copy in alongs:
            copy.wait_send()
    for copy in moved + p_core + p_chip + list(returns.values()) + stages + firsts + seconds:
        copy.wait_send()
    combine.drain()


def layer(x, cot, params, routing, wshard, win, wout, groups):
    rows, width = x.shape
    cos, sin = rope_constants()
    inside = groups == 1
    cols = wshard.shape[-1]
    depth = width // NFFN
    hidden_cols = win.shape[-1]
    heads = cols // 4 // HD
    everyone = MP * rows
    slots = NFFN * CAP
    wide = width + 128
    sd = jax.ShapeDtypeStruct
    vm = pltpu.VMEM
    dma = pltpu.SemaphoreType.DMA
    outs = [
        sd((rows, width), bf16),
        sd((rows, width), f32),
        sd((16, rows), f32),
        sd((depth if inside else width, cols), f32),
        sd((40, width), f32),
        sd((1, width), f32),
        sd((NFFN, 3, depth, hidden_cols), bf16),
    ]
    if not inside:
        wshard = wshard.reshape(NFFN, depth, cols)
    return pl.pallas_call(
        functools.partial(layer_kernel, inside),
        out_shape=outs,
        in_specs=[VM] * 7 + [HB, HB],
        out_specs=[VM] * 6 + [HB],
        scratch_shapes=[
            vm((MP, rows, width), bf16),
            vm((NFFN, depth, cols), bf16),
            vm((heads, SEQ, HD), bf16),
            vm((heads, SEQ, HD), bf16),
            vm((heads, SEQ, HD), bf16),
            vm((SEQ, heads * HD), bf16),
            vm((SEQ, 128), f32),
            vm((NFFN, QUARTER, everyone), bf16),
            vm((NFFN, QUARTER, 128), f32),
            vm((NFFN, MP, QUARTER, width), bf16),
            vm((3, width, hidden_cols), bf16),
            vm((MP, rows, width), bf16),
            vm((rows, width), f32),
            vm((rows, width), f32),
            vm((2, rows, width), bf16),
            vm((rows, width), bf16),
            vm((rows, width), bf16),
            vm((2, rows, width), bf16),
            vm((16, everyone), f32),
            vm((16, everyone), f32),
            vm((16, everyone), f32),
            vm((NFFN, QUARTER, wide), bf16),
            vm((NFFN, QUARTER, width), bf16),
            vm((NFFN, MP, QUARTER, wide), bf16),
            vm((NFFN, MP, QUARTER, width), bf16),
            vm((slots, hidden_cols), bf16),
            vm((2, slots, hidden_cols), bf16),
            vm((MP, QUARTER, wide), f32),
            vm((4, 2, QUARTER, wide), f32),
            vm((4, 2, QUARTER, wide), bf16),
            vm((NFFN, 2, QUARTER, wide), bf16),
            vm((4, QUARTER, wide), bf16),
            vm((NFFN, QUARTER, wide), bf16),
            vm((NFFN, QUARTER, wide), bf16),
            vm((MP, 8, rows), f32),
            vm((MP, 8, rows), f32),
            vm((2, rows, width), bf16),
            vm((rows, width), bf16),
            vm((everyone, HD), f32),
            vm((everyone, HD), f32),
            vm((width, cols), f32),
            vm((NFFN // 2, depth, cols), bf16),
            vm((NFFN // 2, depth, cols), bf16),
            vm((NFFN // 2, depth, cols), bf16),
            vm((NFFN, QUARTER, width), bf16),
            vm((5, 40, width), f32),
            vm((5, 40, width), f32),
            vm((MP, 1, width), f32),
            vm((NFFN, 1, width), f32),
            vm((2, 1, width), f32),
            dma((9,)), dma((9,)),
            dma((8,)), dma((8,)),
            dma((2, 8)), dma((2, 8)),
            dma((2,)),
            dma((3,)), dma((3,)),
            dma((8,)), dma((8,)),
            dma((8,)), dma((8,)),
            dma((8, 3)), dma((8, 3)),
            dma((8, 3)), dma((8, 3)),
            dma((8, 3)), dma((8, 3)),
            dma((8,)), dma((8,)),
            dma((4,)), dma((4,)),
            dma((3,)), dma((3,)),
            dma((3,)), dma((3,)),
            dma((8,)), dma((8,)),
            dma((8,)), dma((8,)),
            dma((4,)), dma((4,)), dma((8,)),
            dma((3,)), dma((3,)),
            dma((3,)), dma((3,)),
            dma((8,)), dma((8,)),
            dma((5,)), dma((5,)),
            dma((MP + NFFN,)), dma((MP + NFFN,)),
        ],
        compiler_params=pltpu.CompilerParams(
            collective_id=0, has_side_effects=True, vmem_limit_bytes=VMEM_LIMIT
        ),
        name="layer",
    )(x, cot, params, routing, jnp.asarray(cos), jnp.asarray(sin), wshard, win, wout)


def clusters():
    groups = lax.axis_size("dp") // NFFN
    near = [[group * NFFN + expert for expert in range(NFFN)] for group in range(groups)]
    far = [[group * NFFN + expert for group in range(groups)] for expert in range(NFFN)]
    return groups, near, far


def exchange(shard, dim):
    _, near, far = clusters()
    own = lax.all_to_all(shard, "dp", 0, dim, axis_index_groups=near, tiled=True)
    return lax.all_gather(own, "dp", axis=dim, axis_index_groups=far, tiled=True)


def exchange_back(grads, dim):
    _, near, far = clusters()
    grads = lax.psum_scatter(
        grads.astype(f32), "dp", scatter_dimension=dim, axis_index_groups=far, tiled=True
    )
    return lax.all_to_all(grads.astype(bf16), "dp", dim, 0, axis_index_groups=near, tiled=True)


def per_device(
    inputs,
    query_key_value,
    output_weight,
    expert_input,
    expert_output,
    first_gain,
    second_gain,
    router_weight,
    logit_carry,
    constant_mix,
    constant_values,
    previous_logits,
    routes,
    cotangent,
):
    rows, width = inputs.shape
    groups, _, far = clusters()

    def padded(array, high, wide, value=0.0):
        return jnp.pad(
            array.astype(f32), ((0, high - array.shape[0]), (0, wide - array.shape[1])),
            constant_values=value,
        )

    params = jnp.concatenate(
        [
            padded(router_weight.T, 16, width),
            constant_mix.T.astype(f32),
            constant_values.astype(f32),
            second_gain.astype(f32)[None],
            first_gain.astype(f32)[None],
            padded(logit_carry, 16, width),
        ],
        axis=0,
    )
    everyone = rows * MP
    routing = jnp.concatenate(
        [padded(previous_logits.T, 16, everyone), padded(routes.T, 8, everyone, -1.0)], axis=0
    )
    shard_depth = query_key_value.shape[0]
    shard = jnp.concatenate(
        [query_key_value.reshape(shard_depth, -1), output_weight.T], axis=1
    )
    cols = output_weight.shape[0]
    expert_output_t = expert_output.transpose(0, 2, 1)
    if groups > 1:
        shard = lax.all_gather(shard, "dp", axis=0, tiled=True)
        win = exchange(expert_input, 2)[0]
        wout = exchange(expert_output_t, 1)[0]
    if groups == 1:
        win, wout = expert_input, expert_output_t
    output, input_grad, logits_grad, weight_grad, sums, first_grad, expert_grad = layer(
        inputs, cotangent, params, routing, shard, win, wout, groups
    )
    if groups > 1:
        weight_grad = lax.psum_scatter(weight_grad, "dp", scatter_dimension=0, tiled=True)
        whole = expert_grad.transpose(1, 0, 2, 3).reshape(1, 3, width, -1)
        expert_grad = exchange_back(whole, 2)
        sums, first_grad = lax.psum((sums, first_grad), "dp", axis_index_groups=far)
    expert_in_grad = expert_grad[:, :2].astype(f32)
    expert_out_grad = expert_grad[:, 2].transpose(0, 2, 1).astype(f32)
    return (
        output,
        input_grad,
        logits_grad[:NEXP].T,
        weight_grad[:, : 3 * cols].reshape(shard_depth, 3, cols),
        weight_grad[:, 3 * cols :].T,
        expert_in_grad,
        expert_out_grad,
        first_grad[0],
        sums[22],
        sums[:NEXP].T,
        sums[24 : 24 + NEXP, :NEXP],
        sums[16:20].T,
        sums[20:22],
    )


def solution(mesh):
    in_specs = (
        P(("dp", "mp"), None),
        P("dp", None, "mp"),
        P("mp", "dp"),
        P(None, None, "dp", "mp"),
        P(None, "mp", "dp"),
        P(),
        P(),
        P(),
        P(),
        P(),
        P(),
        P("dp", None),
        P("dp", None),
        P(("dp", "mp"), None),
    )
    out_specs = (
        P(("dp", "mp"), None),
        P(("dp", "mp"), None),
        P(("dp", "mp"), None),
        P("dp", None, "mp"),
        P("mp", "dp"),
        P(None, None, "dp", "mp"),
        P(None, "mp", "dp"),
        P(),
        P(),
        P(),
        P(),
        P(),
        P(),
    )
    return jax.shard_map(
        per_device, mesh=mesh, in_specs=in_specs, out_specs=out_specs, check_vma=False
    )
```

```python
import functools
import numpy as np
import jax
import jax.numpy as jnp
from jax import lax
from jax.sharding import PartitionSpec as P
from jax.experimental import pallas as pl
from jax.experimental.pallas import tpu as pltpu

HD = 64
NFFN = 8
NEXP = 12
SEQ = 1024
CAP = 256
MP = 4
QUARTER = CAP // MP
WIDE = 640
VMEM_LIMIT = 63 * 2**20

epsilon = 1e-06
rope_base = 10000.0
highest = lax.Precision.HIGHEST
f32 = jnp.float32
bf16 = jnp.bfloat16
MESH = pl.DeviceIdType.MESH
VM = pl.BlockSpec(memory_space=pltpu.VMEM)
HB = pl.BlockSpec(memory_space=pl.ANY)
NT = (((1,), (1,)), ((), ()))
TN = (((0,), (0,)), ((), ()))


def flip(index, distance):
    out = index
    bit = 1
    while bit <= distance:
        if distance & bit:
            out = out + bit - 2 * bit * ((index // bit) % 2)
        bit *= 2
    return out


def dotf(a, b, dims=None):
    if dims is None:
        return jnp.dot(a, b, preferred_element_type=f32)
    return lax.dot_general(a, b, dims, preferred_element_type=f32)


def remote(src, dst, send, recv, **where):
    return pltpu.make_async_remote_copy(
        src_ref=src, dst_ref=dst, send_sem=send, recv_sem=recv, device_id=where, device_id_type=MESH
    )


def greet(mp_me, near, base):
    barrier = pltpu.get_barrier_semaphore()
    for k in range(1, MP):
        pl.semaphore_signal(barrier, inc=1, device_id={"mp": flip(mp_me, k)}, device_id_type=MESH)
    for k in range(1, NFFN):
        pl.semaphore_signal(
            barrier, inc=1, device_id={"dp": base + flip(near, k)}, device_id_type=MESH
        )
    pl.semaphore_wait(barrier, MP - 1 + NFFN - 1)


def rope_constants():
    half = HD // 2
    positions = np.arange(SEQ, dtype=np.float32)
    frequency = (rope_base ** (-np.arange(half, dtype=np.float32) / half)).astype(np.float32)
    angles = (positions[:, None] * frequency[None, :]).astype(np.float32)
    cosine, sine = np.cos(angles), np.sin(angles)
    return (
        np.concatenate([cosine, cosine], axis=1),
        np.concatenate([-sine, sine], axis=1),
    )


def swap_halves(x):
    half = HD // 2
    return jnp.concatenate([x[:, half:], x[:, :half]], axis=1)


class Gather:
    def __init__(self, ref, mp_me, send, recv):
        self.me, self.core, self.chip = mp_me, flip(mp_me, 1), flip(mp_me, 2)
        own = ref.at[mp_me]
        far = ref.at[self.chip]
        self.to_chip = remote(own, own, send.at[0], recv.at[0], mp=self.chip)
        self.to_core = remote(own, own, send.at[1], recv.at[1], mp=self.core)
        self.relay = remote(far, far, send.at[2], recv.at[2], mp=self.core)

    def start(self):
        self.to_chip.start()
        self.to_core.start()

    def forward(self):
        self.to_chip.wait_recv()
        self.relay.start()

    def finish(self):
        self.to_core.wait_recv()
        self.relay.wait_recv()
        self.to_chip.wait_send()
        self.to_core.wait_send()
        self.relay.wait_send()


def pack3(value):
    high = value.astype(bf16).astype(f32)
    rest = value - high
    mid = rest.astype(bf16).astype(f32)
    low = (rest - mid).astype(bf16).astype(f32)
    lane = lax.broadcasted_iota(jnp.int32, (value.shape[0], 128), 1)
    return jnp.where(
        lane == 0, high, jnp.where(lane == 1, mid, jnp.where(lane == 2, low, 0.0))
    ).astype(bf16)


def unpack3(parts):
    return jnp.sum(parts.astype(f32), axis=-1, keepdims=True)


def exact(left, right, dims=None):
    high = left.astype(bf16)
    rest = left - high.astype(f32)
    mid = rest.astype(bf16)
    low = (rest - mid.astype(f32)).astype(bf16)
    return dotf(high, right, dims) + (dotf(mid, right, dims) + dotf(low, right, dims))


class Scatter:
    def __init__(self, mp_me, core_out, core_in, chip_out, chip_in, send, recv):
        self.me, self.core, self.chip = mp_me, flip(mp_me, 1), flip(mp_me, 2)
        self.core_out, self.core_in = core_out, core_in
        self.chip_out, self.chip_in = chip_out, chip_in
        self.to_core = [
            remote(core_out.at[j], core_in.at[j], send.at[j], recv.at[j], mp=self.core)
            for j in range(2)
        ]
        self.to_chip = remote(chip_out, chip_in, send.at[2], recv.at[2], mp=self.chip)

    def run(self, blocks):
        for j, block in enumerate((flip(self.me, 3), self.core)):
            self.core_out[j] = blocks(block).astype(bf16)
            self.to_core[j].start()
        term = blocks(self.chip)
        self.to_core[0].wait_recv()
        self.chip_out[...] = (term + self.core_in[0].astype(f32)).astype(bf16)
        self.to_chip.start()
        term = blocks(self.me)
        self.to_core[1].wait_recv()
        term = term + self.core_in[1].astype(f32)
        self.to_chip.wait_recv()
        return term + self.chip_in[...].astype(f32)

    def drain(self):
        for copy in self.to_core + [self.to_chip]:
            copy.wait_send()


def layer_kernel(
    inside,
    x_ref, cot_ref, params_ref, routing_ref, cos_ref, sin_ref, wshard_ref, win_shard, wout_shard,
    output_ref, xgrad_ref, lgrad_ref, wgrad_ref, sums_ref, first_ref, dw_own,
    rows1_ref, w_ref, q_ref, k_ref, v_ref, mixed_ref, lse_ref, pick_ref, gate_ref, outp_ref, dw_ref,
    rows2_ref, hidden_ref, sum_ref, core_in, chip_out, chip_in, core_out,
    place_ref, gates_ref, prior_ref, msgx, msgc, xs, cs, units_ref, pgrad_ref,
    part_ref, keep_ref, gcore_out, gcore_in, gchip_out, gchip_in, gret, score_out, score_in,
    ncore_in, nchip_in,
    key_acc, value_acc, grads_ref, across_out, across_in, along_in, ret_ref,
    pcore_in, pchip_in,
    sum_out, sum_in, first_mp, first_dp, first_out,
    sends, recvs, wsend, wrecv, esend, erecv, local,
    csend, crecv, xsend, xrecv, dsend, drecv, xgs, xgr, cgs, cgr, gsend, grecv,
    rsend, rrecv, ssend, srecv, nsend, nrecv,
    asend, arecv, osend, orecv, msend, mrecv, psend, precv, mlocal, bsend, brecv, tsend, trecv,
    vsend, vrecv, zsend, zrecv, fsend, frecv,
):
    cot_all = rows2_ref
    residual_ref = sum_ref
    hgrad_ref = xgrad_ref
    small_ref = sum_out.at[0]
    mp_me = lax.axis_index("mp")
    dp_me = lax.axis_index("dp")
    near = lax.rem(dp_me, NFFN)
    base = dp_me - near
    core, chip, far = flip(mp_me, 1), flip(mp_me, 2), flip(mp_me, 3)
    rows, width = x_ref.shape
    everyone = MP * rows
    greet(mp_me, near, base)

    tokens = x_ref[...].astype(f32)
    scale = lax.rsqrt(jnp.mean(tokens * tokens, axis=-1, keepdims=True) + epsilon)
    rows1_ref[mp_me] = (tokens * scale * params_ref[23:24]).astype(bf16)
    gather1 = Gather(rows1_ref, mp_me, sends.at[pl.ds(0, 3)], recvs.at[pl.ds(0, 3)])
    gather1.start()
    if inside:
        w_ref[near] = wshard_ref[...]
        own = w_ref.at[near]
        along = [
            remote(own, own, wsend.at[k], wrecv.at[k], dp=base + flip(near, k)) for k in (2, 4, 6)
        ]
        for copy in along:
            copy.start()
        mate = base + flip(near, 1)
        across = [remote(own, own, wsend.at[0], wrecv.at[0], dp=mate)]
        across[0].start()
    cot_all[mp_me] = cot_ref[...]
    cot_gather = Gather(cot_all, mp_me, csend, crecv)
    cot_gather.start()

    ids = lax.broadcasted_iota(jnp.int32, (16, everyone), 0).astype(f32)
    chosen = (ids == routing_ref[16:17]) | (ids == routing_ref[17:18])
    earlier = lax.broadcasted_iota(jnp.int32, (everyone, everyone), 0) < lax.broadcasted_iota(
        jnp.int32, (everyone, everyone), 1
    )
    counts = dotf(
        jnp.where(chosen, 1.0, 0.0).astype(bf16), jnp.where(earlier, 1.0, 0.0).astype(bf16)
    )
    place_ref[...] = jnp.where(chosen, counts, -1.0)
    wanted = (lax.broadcasted_iota(jnp.int32, (QUARTER, everyone), 0) + QUARTER * mp_me).astype(f32)

    def target(k):
        return lax.rem(near + k, NFFN)

    def choose(k, carried):
        pick = wanted == place_ref[pl.ds(target(k), 1)]
        pick_ref[k] = jnp.where(pick, 1.0, 0.0).astype(bf16)
        return carried

    lax.fori_loop(0, NFFN, choose, 0)
    carry = params_ref[24:40, 0:16]
    prior_ref[...] = lax.dot_general(
        carry, routing_ref[0:16], TN, preferred_element_type=f32, precision=highest
    )

    if inside:
        for k, copy in zip((2, 4, 6), along):
            copy.wait_recv()
            block = w_ref.at[flip(near, k)]
            onward = remote(block, block, wsend.at[k + 1], wrecv.at[k + 1], dp=mate)
            onward.start()
            across.append(onward)
        gather1.forward()
        for copy in across:
            copy.wait_recv()
        for copy in along + across:
            copy.wait_send()
        weights = []
        din = win_shard.shape[2]
        place = pl.ds(pl.multiple_of(near * din, din), din)
        for k in (4, 2, 6, 5, 7, 3, 1):
            peer = flip(near, k)
            for i, (src, dst) in enumerate([
                (win_shard.at[peer], dw_ref.at[0:2, place]),
                (wout_shard.at[peer], dw_ref.at[2, place]),
            ]):
                weights.append(
                    remote(src, dst, esend.at[i, k], erecv.at[i, k], dp=base + peer)
                )
        first = 4
        for copy in weights[:first]:
            copy.start()
        mine = [
            pltpu.make_async_copy(win_shard.at[near], dw_ref.at[0:2, place], local.at[0]),
            pltpu.make_async_copy(wout_shard.at[near], dw_ref.at[2, place], local.at[1]),
        ]
        for copy in mine:
            copy.start()
    else:
        w_ref[...] = wshard_ref[...]
        mine = [
            pltpu.make_async_copy(win_shard, dw_ref.at[0:2], local.at[0]),
            pltpu.make_async_copy(wout_shard, dw_ref.at[2], local.at[1]),
        ]
        for copy in mine:
            copy.start()
        gather1.forward()
    gather1.finish()

    cot_gather.forward()
    cot_gather.finish()

    def c_copy(k):
        return remote(
            msgc.at[k], cs.at[k, mp_me], dsend.at[k], drecv.at[k], dp=base + target(k)
        )

    def send(picked, ref, copy, lanes):
        def half(i, carried):
            start = 4 - 4 * i
            blocks = dotf(pick_ref[pl.ds(start, 4)].reshape(4 * QUARTER, everyone), picked())
            ref[(pl.ds(start, 4),) + lanes] = blocks.astype(bf16).reshape(4, QUARTER, width)

            def go(k, inner):
                @pl.when(k > 0)
                def _():
                    copy(k).start()

                return inner

            return lax.fori_loop(start, start + 4, go, carried)

        lax.fori_loop(0, 2, half, 0)

    send(lambda: cot_all[...].reshape(everyone, width), msgc, c_copy, ())
    cs[0, mp_me] = msgc[0]
    if inside:
        for copy in weights[first:]:
            copy.start()

    w_all = w_ref[...].reshape(width, w_ref.shape[2])
    heads = q_ref.shape[0]
    cols = heads * HD

    def project(i, carry):
        at = pl.ds(pl.multiple_of(i * rows, rows), rows)
        joint = dotf(rows1_ref[i], w_all[:, : 3 * cols])
        cosine, sine = cos_ref[at], sin_ref[at]
        for h in range(heads):
            query = joint[:, h * HD : (h + 1) * HD]
            key = joint[:, cols + h * HD : cols + (h + 1) * HD]
            q_ref[h, at] = (query * cosine + swap_halves(query) * sine).astype(bf16)
            k_ref[h, at] = (key * cosine + swap_halves(key) * sine).astype(bf16)
            v_ref[h, at] = joint[:, 2 * cols + h * HD : 2 * cols + (h + 1) * HD].astype(bf16)
        return carry

    lax.fori_loop(0, MP, project, 0)
    out_weight = w_all[:, 3 * cols :]

    to_core = [
        remote(core_out.at[j], core_in.at[j], sends.at[3 + j], recvs.at[3 + j], mp=core)
        for j in range(2)
    ]
    to_chip = remote(chip_out, chip_in, sends.at[5], recvs.at[5], mp=chip)

    def attend(step, carry):
        block = flip(mp_me, 3)
        block = jnp.where(step == 1, core, jnp.where(step == 2, chip, jnp.where(step == 3, mp_me, block)))
        at = pl.ds(pl.multiple_of(block * rows, rows), rows)
        row_ids = block * rows + lax.broadcasted_iota(jnp.int32, (rows, SEQ), 0)
        seen = row_ids >= lax.broadcasted_iota(jnp.int32, (rows, SEQ), 1)
        for h in range(heads):
            scores = dotf(q_ref[h, at], k_ref[h], NT) * HD**-0.5
            scores = jnp.where(seen, scores, -jnp.inf)
            peak = jnp.max(scores, axis=-1, keepdims=True)
            exponent = jnp.exp(scores - peak)
            total = jnp.sum(exponent, axis=-1, keepdims=True)
            probs = (exponent * (1.0 / total)).astype(bf16)
            mixed_ref[at, h * HD : (h + 1) * HD] = dotf(probs, v_ref[h]).astype(bf16)
            lse_ref[at, h : h + 1] = peak + jnp.log(total)
        part = dotf(mixed_ref[at], out_weight, NT)

        @pl.when(step == 0)
        def _():
            core_out[0] = part.astype(bf16)
            to_core[0].start()

        @pl.when(step == 1)
        def _():
            core_out[1] = part.astype(bf16)
            to_core[1].start()

        @pl.when(step == 2)
        def _():
            to_core[0].wait_recv()
            chip_out[...] = (part + core_in[0].astype(f32)).astype(bf16)
            to_chip.start()

        @pl.when(step == 3)
        def _():
            sum_ref[...] = part

        return carry

    lax.fori_loop(0, MP, attend, 0)
    to_core[1].wait_recv()
    partial = sum_ref[...] + core_in[1].astype(f32)
    to_chip.wait_recv()
    hidden = x_ref[...].astype(f32) + (partial + chip_in[...].astype(f32))
    hidden_ref[...] = hidden
    scale2 = lax.rsqrt(jnp.mean(hidden * hidden, axis=-1, keepdims=True) + epsilon)
    rows2_ref[mp_me] = (hidden * scale2 * params_ref[22:23]).astype(bf16)
    gather2 = Gather(rows2_ref, mp_me, sends.at[pl.ds(6, 3)], recvs.at[pl.ds(6, 3)])
    gather2.start()
    for copy in to_core + [to_chip]:
        copy.wait_send()
    gather2.forward()

    def turn(i):
        return lax.rem(i + 4, NFFN)

    def c_gather(k):
        return Gather(cs.at[k], mp_me, cgs.at[k], cgr.at[k])

    def at_step(i, first, body):
        @pl.when((i >= first) & (i < NFFN + first))
        def _():
            body(turn(i - first))

    def cot_step(i, carried):
        def arrived(k):
            @pl.when(k > 0)
            def _():
                c_copy(k).wait_recv()

            c_gather(k).start()

        at_step(i, 0, arrived)
        at_step(i, 1, lambda k: c_gather(k).forward())
        return carried

    lax.fori_loop(0, NFFN + 1, cot_step, 0)
    gather2.finish()

    router = params_ref[0:16].astype(bf16)
    mix = params_ref[16:20].astype(bf16)
    tokens = rows2_ref[...].reshape(everyone, width)
    logits = dotf(router, tokens, NT) + prior_ref[...]
    masked = jnp.where(place_ref[...] >= 0.0, logits, -jnp.inf)
    exponent = jnp.exp(masked - jnp.max(masked, axis=0, keepdims=True))
    gates_ref[...] = exponent / jnp.sum(exponent, axis=0, keepdims=True)

    def weigh(k, carried):
        gate = jnp.sum(
            pick_ref[k].astype(f32) * gates_ref[pl.ds(target(k), 1)], axis=1, keepdims=True
        )
        gate_ref[k] = jnp.broadcast_to(gate, (QUARTER, 128))
        msgx[k, :, width:] = pack3(gate)
        return carried

    lax.fori_loop(0, NFFN, weigh, 0)

    def x_copy(k):
        return remote(
            msgx.at[k], xs.at[k, mp_me], xsend.at[k], xrecv.at[k], dp=base + target(k)
        )

    send(
        lambda: rows2_ref[...].reshape(everyone, width), msgx, x_copy,
        (slice(None), slice(0, width)),
    )
    xs[0, mp_me] = msgx[0]

    def x_gather(k):
        return Gather(xs.at[k], mp_me, xgs.at[k], xgr.at[k])

    def slots_of(k):
        return pl.ds(pl.multiple_of(k * CAP, CAP), CAP)

    def x_step(i, carried):
        def arrived(k):
            @pl.when(k > 0)
            def _():
                x_copy(k).wait_recv()

            x_gather(k).start()

        def passed(k):
            x_gather(k).forward()

        at_step(i, 0, arrived)
        at_step(i, 1, passed)
        return carried

    lax.fori_loop(0, NFFN + 1, x_step, 0)
    if inside:
        for copy in weights:
            copy.wait_recv()
    for copy in mine:
        copy.wait()

    def r_trip(k):
        slot = lax.rem(k, 4)
        return Scatter(
            mp_me, gcore_out.at[slot], gcore_in.at[k], gchip_out.at[slot], gchip_in.at[k],
            gsend.at[k], grecv.at[k],
        )

    def g_copy(k):
        return remote(
            msgx.at[k], gret.at[k], rsend.at[k], rrecv.at[k],
            dp=base + lax.rem(near - k + NFFN, NFFN),
        )

    def seal(ref, index, total):
        ref[index + (slice(None), slice(0, width))] = total[:, :width].astype(bf16)
        ref[index + (slice(None), slice(width, None))] = pack3(unpack3(total[:, width:]))

    def expert_step(i, carried):
        def compute(k):
            c_gather(k).finish()
            x_gather(k).finish()
            x = xs[k].reshape(CAP, width + 128)[:, :width]
            gate = unpack3(xs[k].reshape(CAP, width + 128)[:, width:])
            c = cs[k].reshape(CAP, width)
            gate_pre = dotf(x, dw_ref[0])
            up_pre = dotf(x, dw_ref[1])
            sig = jax.nn.sigmoid(gate_pre)
            units = (gate_pre * sig * up_pre).astype(bf16)
            units_ref[slots_of(k)] = units
            outp_ref[k] = dotf(units, dw_ref[2], NT).astype(bf16).reshape(MP, QUARTER, width)
            raw = dotf(c, dw_ref[2])
            score = jnp.sum(units.astype(f32) * raw, axis=1, keepdims=True)
            units_grad = raw * gate
            gate_grad = (units_grad * up_pre * sig * (1.0 + gate_pre * (1.0 - sig))).astype(bf16)
            up_grad = (units_grad * (gate_pre * sig)).astype(bf16)
            pgrad_ref[0, slots_of(k)] = gate_grad
            pgrad_ref[1, slots_of(k)] = up_grad
            back = dotf(gate_grad, dw_ref[0], NT) + dotf(up_grad, dw_ref[1], NT)
            cs[k] = (c.astype(f32) * gate).astype(bf16).reshape(MP, QUARTER, width)
            part_ref[:, :, :width] = back.reshape(MP, QUARTER, width)
            part_ref[:, :, width:] = pack3(score).astype(f32).reshape(MP, QUARTER, 128)
            slot = lax.rem(k, 4)
            gcore_out[slot, 0] = part_ref[far].astype(bf16)
            gcore_out[slot, 1] = part_ref[core].astype(bf16)
            keep_ref[slot, 0] = part_ref[chip]
            keep_ref[slot, 1] = part_ref[mp_me]
            for copy in r_trip(k).to_core:
                copy.start()

        def across(k):
            trip = r_trip(k)
            trip.to_core[0].wait_recv()
            seal(gchip_out, (lax.rem(k, 4),), keep_ref[lax.rem(k, 4), 0] + gcore_in[k, 0].astype(f32))
            trip.to_chip.start()

        def away(k):
            trip = r_trip(k)
            trip.to_core[1].wait_recv()
            trip.to_chip.wait_recv()
            total = (
                keep_ref[lax.rem(k, 4), 1]
                + gcore_in[k, 1].astype(f32)
                + gchip_in[k].astype(f32)
            )
            trip.drain()

            @pl.when(k > 0)
            def _():
                x_copy(k).wait_send()

            seal(msgx, (k,), total)

            @pl.when(k > 0)
            def _():
                g_copy(k).start()

            @pl.when(k == 0)
            def _():
                gret[0] = msgx[0]

        at_step(i, 4, away)
        at_step(i, 0, compute)
        at_step(i, 2, across)
        return carried

    lax.fori_loop(0, NFFN + 4, expert_step, 0)

    p_core = [
        remote(outp_ref.at[:, far], pcore_in.at[0], psend.at[0], precv.at[0], mp=core),
        remote(outp_ref.at[:, core], pcore_in.at[1], psend.at[1], precv.at[1], mp=core),
    ]
    for copy in p_core:
        copy.start()
    parts = (slice(4, 8), slice(0, 4))
    p_chip = [
        remote(cs.at[part, 3], pchip_in.at[part], psend.at[2 + j], precv.at[2 + j], mp=chip)
        for j, part in enumerate(parts)
    ]
    returns = {
        k: remote(msgc.at[k], ret_ref.at[k], osend.at[k], orecv.at[k],
                  dp=base + lax.rem(near - k + NFFN, NFFN))
        for k in range(1, NFFN)
    }

    def results_across():
        p_core[0].wait_recv()
        for j, part in enumerate(parts):
            cs[part, 3] = (
                outp_ref[part, chip].astype(f32) + pcore_in[0, part].astype(f32)
            ).astype(bf16)
            p_chip[j].start()

    def results_away(j):
        part = parts[j]
        if j == 0:
            p_core[1].wait_recv()
        p_chip[j].wait_recv()
        msgc[part] = (
            outp_ref[part, mp_me].astype(f32)
            + (pcore_in[1, part].astype(f32) + pchip_in[part].astype(f32))
        ).astype(bf16)
        for k in range(part.start, part.stop):
            if k > 0:
                returns[k].start()
            else:
                ret_ref[0] = msgc[0]

    def weights_step(j, carried):
        at = pl.ds(pl.multiple_of(j * 128, 128), 128)
        x = xs[:, :, :, at].reshape(NFFN * CAP, 128)
        c = cs[:, :, :, at].reshape(NFFN * CAP, 128)
        dw_ref[0, at] = dotf(x, pgrad_ref[0], TN).astype(bf16)
        dw_ref[1, at] = dotf(x, pgrad_ref[1], TN).astype(bf16)
        dw_ref[2, at] = dotf(c, units_ref[...], TN).astype(bf16)
        return carried

    lax.fori_loop(0, width // 128, weights_step, 0)

    din = dw_own.shape[2]

    def rows_of(index):
        return pl.ds(pl.multiple_of(index * din, din), din)

    if inside:
        moved = [
            remote(dw_ref.at[:, rows_of(flip(near, k))], dw_own.at[near], msend.at[k],
                   mrecv.at[k], dp=base + flip(near, k))
            for k in (4, 6, 5, 7, 2, 3, 1)
        ]
        kept = [pltpu.make_async_copy(dw_ref.at[:, rows_of(near)], dw_own.at[near], mlocal.at[0])]
    else:
        moved = []
        kept = [
            pltpu.make_async_copy(dw_ref.at[:, rows_of(p)], dw_own.at[p], mlocal.at[p])
            for p in range(NFFN)
        ]
    early = 7
    for copy in moved[:early] + kept:
        copy.start()
    results_across()

    n_bf = rows2_ref[mp_me]
    n = n_bf.astype(f32)
    cot = cot_ref[...].astype(f32)
    hidden = hidden_ref[...]
    lane = lax.broadcasted_iota(jnp.int32, (rows, 128), 1)
    own_at = pl.ds(pl.multiple_of(mp_me * rows, rows), rows)
    gates_t = gates_ref[:, own_at]
    own_gates = jnp.concatenate([gates_t, jnp.zeros((112, rows), f32)], axis=0).T
    copy_gate = own_gates[:, NFFN + 1 : NFFN + 2]
    const_gates = [own_gates[:, NFFN + 2 : NFFN + 3], own_gates[:, NFFN + 3 : NFFN + 4]]
    mix_logits = dotf(n_bf, mix, NT)
    with_normed = jnp.sum(cot * n, axis=1, keepdims=True)
    residual = hidden + copy_gate * n
    local_grad = copy_gate * cot
    local_scores = jnp.where(lane == NFFN + 1, with_normed, 0.0)
    mix_grads = jnp.zeros((rows, 128), f32)
    for c in range(2):
        first, second = mix_logits[:, 2 * c : 2 * c + 1], mix_logits[:, 2 * c + 1 : 2 * c + 2]
        top = jnp.maximum(first, second)
        first, second = jnp.exp(first - top), jnp.exp(second - top)
        share = 1.0 / (first + second)
        first, second = first * share, second * share
        constant = params_ref[20 + c : 21 + c]
        with_constant = jnp.sum(cot * constant, axis=1, keepdims=True)
        gate = const_gates[c]
        residual = residual + gate * (first * n + second * constant)
        local_scores = jnp.where(
            lane == NFFN + 2 + c, first * with_normed + second * with_constant, local_scores
        )
        local_grad = local_grad + (first * gate) * cot
        small_ref[20 + c : 21 + c] = jnp.sum((second * gate) * cot, axis=0, keepdims=True)
        grad_first, grad_second = gate * with_normed, gate * with_constant
        mean = first * grad_first + second * grad_second
        mix_grads = jnp.where(lane == 2 * c, first * (grad_first - mean), mix_grads)
        mix_grads = jnp.where(lane == 2 * c + 1, second * (grad_second - mean), mix_grads)
    residual_ref[...] = residual

    def returned(k, carried):
        g_copy(k).wait_recv()
        return carried

    lax.fori_loop(1, NFFN, returned, 0)
    ret = gret[...].reshape(NFFN * QUARTER, width + 128)
    score_out[...] = jnp.zeros_like(score_out)

    def give_scores(k, carried):
        slots = unpack3(gret[k, :, width:])
        row = jnp.sum(pick_ref[k].astype(f32) * slots, axis=0, keepdims=True)
        for q in range(MP):
            score_out[q, pl.ds(target(k), 1)] = row[:, q * rows : (q + 1) * rows]
        return carried

    lax.fori_loop(0, NFFN, give_scores, 0)
    score_copies = [
        remote(score_out.at[flip(mp_me, k)], score_in.at[k], ssend.at[k], srecv.at[k], mp=flip(mp_me, k))
        for k in range(1, MP)
    ]
    for copy in score_copies:
        copy.start()

    def grad_block(q):
        at = pl.ds(pl.multiple_of(q * rows, rows), rows)
        return dotf(
            pick_ref[:, :, at].reshape(NFFN * QUARTER, rows), ret[:, :width], TN
        )

    trip = Scatter(mp_me, core_out, ncore_in, chip_out, nchip_in, nsend, nrecv)
    normed_grad = trip.run(grad_block) + local_grad
    lax.fori_loop(1, NFFN, lambda k, carried: (c_copy(k).wait_send(), carried)[1], 0)
    results_away(0)
    results_away(1)
    for copy in moved[early:]:
        copy.start()

    for copy in score_copies:
        copy.wait_recv()
    ffn_scores = (score_out[mp_me] + score_in[1]) + (score_in[2] + score_in[3])
    scores = local_scores.T[:16] + jnp.concatenate([ffn_scores, jnp.zeros((8, rows), f32)], axis=0)
    logit_grad = gates_t * (scores - jnp.sum(gates_t * scores, axis=0, keepdims=True))
    lgrad_ref[...] = lax.dot_general(
        carry, logit_grad, (((1,), (0,)), ((), ())),
        preferred_element_type=f32, precision=highest,
    )
    small_ref[24:40] = jnp.zeros((16, width), f32)
    small_ref[24:40, 0:16] = lax.dot_general(
        routing_ref[0:16, own_at], logit_grad, NT, preferred_element_type=f32, precision=highest
    )
    stacked = jnp.concatenate([logit_grad, mix_grads.T[:16]], axis=0)
    stack = params_ref[0:32]
    sublane = lax.broadcasted_iota(jnp.int32, (32, width), 0)
    stack = jnp.where(sublane < 20, stack, 0.0).astype(bf16)
    feature_grads = exact(stacked, n_bf)
    small_ref[0:20] = feature_grads[0:20]
    normed_grad = normed_grad + exact(stacked, stack, TN)
    scale = lax.rsqrt(jnp.mean(hidden * hidden, axis=-1, keepdims=True) + epsilon)
    scaled = hidden * scale
    small_ref[22:23] = jnp.sum(normed_grad * scaled, axis=0, keepdims=True)
    small_ref[23:24] = jnp.zeros((1, width), f32)
    weighted = normed_grad * params_ref[22:23]
    hidden_grad = cot + scale * (
        weighted - scaled * jnp.mean(weighted * scaled, axis=-1, keepdims=True)
    )
    hgrad_ref[...] = hidden_grad
    rows2_ref[mp_me] = hidden_grad.astype(bf16)
    agather = Gather(rows2_ref, mp_me, asend, arecv)
    agather.start()

    trip.drain()
    for copy in score_copies:
        copy.wait_send()

    def drain(k, carried):
        g_copy(k).wait_send()
        return carried

    lax.fori_loop(1, NFFN, drain, 0)
    if inside:
        for copy in weights:
            copy.wait_send()

    places = [{"mp": flip(mp_me, 1)}, {"mp": flip(mp_me, 2)}] + [
        {"dp": base + flip(near, k)} for k in (1, 2, 4)
    ]
    stages = [
        remote(sum_out.at[j], sum_in.at[j], zsend.at[j], zrecv.at[j], **where)
        for j, where in enumerate(places)
    ]

    def stage(j):
        if j > 0:
            stages[j - 1].wait_recv()
            total = sum_out[j - 1] + sum_in[j - 1]
            if j == len(stages):
                sums_ref[...] = total
                return
            sum_out[j] = total
        stages[j].start()

    stage(0)
    agather.forward()
    stage(1)
    agather.finish()

    w_all = w_ref[...].reshape(width, w_ref.shape[2])
    out_weight = w_all[:, 3 * cols :]
    for i in range(MP):
        xs[i, :, :, WIDE : WIDE + cols] = (
            dotf(rows2_ref[i], out_weight).astype(bf16).reshape(MP, QUARTER, cols)
        )
    grads_ref[:, 3 * cols :] = dotf(rows2_ref[...].reshape(everyone, width), mixed_ref[...], TN).astype(bf16)

    combine = Scatter(mp_me, core_out, ncore_in, chip_out, nchip_in, bsend, brecv)

    def out_block(q):
        at = pl.ds(pl.multiple_of(q * rows, rows), rows)
        weighted = (ret_ref[...].astype(f32) * gate_ref[:, :, 0:1]).astype(bf16)
        return dotf(
            pick_ref[:, :, at].reshape(NFFN * QUARTER, rows),
            weighted.reshape(NFFN * QUARTER, width), TN,
        )

    def head_back(h):
        lanes = slice(h * HD, (h + 1) * HD)
        for b in range(MP):
            at = slice(b * rows, (b + 1) * rows)
            seen = (b + 1) * rows
            query = q_ref[h, at]
            keys = k_ref[h, :seen]
            out_grad = xs[b, :, :, WIDE + h * HD : WIDE + (h + 1) * HD].reshape(rows, HD)
            scores = dotf(query, keys, NT) * HD**-0.5
            allowed = b * rows + lax.broadcasted_iota(
                jnp.int32, (rows, seen), 0
            ) >= lax.broadcasted_iota(jnp.int32, (rows, seen), 1)
            probs = jnp.where(allowed, jnp.exp(scores - lse_ref[at, h : h + 1]), 0.0)
            probs_grad = dotf(out_grad, v_ref[h, :seen], NT)
            inner = jnp.sum(probs * probs_grad, axis=1, keepdims=True)
            score_grad = (probs * (probs_grad - inner)).astype(bf16)
            query_grad = dotf(score_grad, keys) * HD**-0.5
            xs[b, :, :, lanes] = (
                (query_grad * cos_ref[at] - swap_halves(query_grad) * sin_ref[at])
                .astype(bf16)
                .reshape(MP, QUARTER, HD)
            )
            key_grad = dotf(score_grad, query, TN) * HD**-0.5
            value_grad = dotf(probs.astype(bf16), out_grad, TN)
            if b == 0:
                key_acc[...] = jnp.zeros_like(key_acc)
                value_acc[...] = jnp.zeros_like(value_acc)
            key_acc[:seen] += key_grad
            value_acc[:seen] += value_grad
        key_grad = key_acc[...]
        key_grad = key_grad * cos_ref[...] - swap_halves(key_grad) * sin_ref[...]
        xs[0:MP, :, :, cols + h * HD : cols + (h + 1) * HD] = key_grad.astype(bf16).reshape(
            MP, MP, QUARTER, HD
        )
        xs[0:MP, :, :, 2 * cols + h * HD : 2 * cols + (h + 1) * HD] = (
            value_acc[...].astype(bf16).reshape(MP, MP, QUARTER, HD)
        )

    last = heads - 1
    for h in range(heads):
        head_back(h)
        if h == 0:
            stage(2)
        if h == last:
            stage(3)

    depth = width // NFFN
    grads_ref[:, : 3 * cols] = dotf(
        rows1_ref[...].reshape(everyone, width),
        xs[0:MP, :, :, 0 : 3 * cols].reshape(everyone, 3 * cols), TN,
    ).astype(bf16)
    if inside:
        lean = lax.rem(near, 2)
        tall = grads_ref[...].reshape(NFFN // 2, 2, depth, grads_ref.shape[1])
        across_out[...] = jnp.where(lean == 0, tall[:, 1], tall[:, 0])
        kept_half = jnp.where(lean == 0, tall[:, 0], tall[:, 1])
        over = remote(across_out, across_in, vsend.at[0], vrecv.at[0], dp=base + flip(near, 1))
        over.start()
    else:
        wgrad_ref[...] = grads_ref[...].astype(f32)
    stage(4)

    home = Scatter(mp_me, core_out, core_in, chip_out, chip_in, tsend, trecv)

    def x_block(q):
        joint = xs[q, :, :, 0 : 3 * cols].reshape(rows, 3 * cols)
        return dotf(joint, w_all[:, : 3 * cols], NT)

    normed_grad = home.run(x_block)
    home.drain()
    if inside:
        over.wait_recv()
        over.wait_send()
        across_out[...] = (kept_half.astype(f32) + across_in[...].astype(f32)).astype(bf16)
        up = near // 2
        alongs = [
            remote(across_out.at[flip(near, k) // 2], along_in.at[k // 2], vsend.at[k], vrecv.at[k],
                   dp=base + flip(near, k))
            for k in (4, 6, 2)
        ]
        for copy in alongs:
            copy.start()
    tokens = x_ref[...].astype(f32)
    scale = lax.rsqrt(jnp.mean(tokens * tokens, axis=-1, keepdims=True) + epsilon)
    scaled = tokens * scale
    first_out[0] = jnp.sum(normed_grad * scaled, axis=0, keepdims=True)
    firsts = [
        remote(first_out.at[0], first_mp.at[k], fsend.at[k], frecv.at[k], mp=flip(mp_me, k))
        for k in range(1, MP)
    ]
    for copy in firsts:
        copy.start()
    weighted = normed_grad * params_ref[23:24]
    xgrad_ref[...] = hgrad_ref[...] + scale * (
        weighted - scaled * jnp.mean(weighted * scaled, axis=-1, keepdims=True)
    )
    for copy in firsts:
        copy.wait_recv()
    first_out[1] = first_out[0] + first_mp[1] + first_mp[2] + first_mp[3]
    seconds = [
        remote(first_out.at[1], first_dp.at[k], fsend.at[MP + k], frecv.at[MP + k],
               dp=base + flip(near, k))
        for k in range(1, NFFN)
    ]
    for copy in seconds:
        copy.start()
    stage(5)
    for copy in returns.values():
        copy.wait_recv()
    routed = combine.run(out_block)
    output_ref[...] = (residual_ref[...] + routed).astype(bf16)
    if inside:
        for copy in alongs:
            copy.wait_recv()
        wgrad_ref[...] = across_out[up].astype(f32) + (
            along_in[1].astype(f32) + along_in[2].astype(f32) + along_in[3].astype(f32)
        )
    for copy in seconds:
        copy.wait_recv()
    total = first_out[1]
    for k in range(1, NFFN):
        total = total + first_dp[k]
    first_ref[...] = total

    for copy in moved:
        copy.wait_recv()
    for copy in kept:
        copy.wait()
    if inside:
        for copy in alongs:
            copy.wait_send()
    for copy in moved + p_core + p_chip + list(returns.values()) + stages + firsts + seconds:
        copy.wait_send()
    combine.drain()


def layer(x, cot, params, routing, wshard, win, wout, groups):
    rows, width = x.shape
    cos, sin = rope_constants()
    inside = groups == 1
    cols = wshard.shape[-1]
    depth = width // NFFN
    hidden_cols = win.shape[-1]
    heads = cols // 4 // HD
    everyone = MP * rows
    slots = NFFN * CAP
    wide = width + 128
    sd = jax.ShapeDtypeStruct
    vm = pltpu.VMEM
    dma = pltpu.SemaphoreType.DMA
    outs = [
        sd((rows, width), bf16),
        sd((rows, width), f32),
        sd((16, rows), f32),
        sd((depth if inside else width, cols), f32),
        sd((40, width), f32),
        sd((1, width), f32),
        sd((NFFN, 3, depth, hidden_cols), bf16),
    ]
    if not inside:
        wshard = wshard.reshape(NFFN, depth, cols)
    return pl.pallas_call(
        functools.partial(layer_kernel, inside),
        out_shape=outs,
        in_specs=[VM] * 7 + [HB, HB],
        out_specs=[VM] * 6 + [HB],
        scratch_shapes=[
            vm((MP, rows, width), bf16),
            vm((NFFN, depth, cols), bf16),
            vm((heads, SEQ, HD), bf16),
            vm((heads, SEQ, HD), bf16),
            vm((heads, SEQ, HD), bf16),
            vm((SEQ, heads * HD), bf16),
            vm((SEQ, 128), f32),
            vm((NFFN, QUARTER, everyone), bf16),
            vm((NFFN, QUARTER, 128), f32),
            vm((NFFN, MP, QUARTER, width), bf16),
            vm((3, width, hidden_cols), bf16),
            vm((MP, rows, width), bf16),
            vm((rows, width), f32),
            vm((rows, width), f32),
            vm((2, rows, width), bf16),
            vm((rows, width), bf16),
            vm((rows, width), bf16),
            vm((2, rows, width), bf16),
            vm((16, everyone), f32),
            vm((16, everyone), f32),
            vm((16, everyone), f32),
            vm((NFFN, QUARTER, wide), bf16),
            vm((NFFN, QUARTER, width), bf16),
            vm((NFFN, MP, QUARTER, wide), bf16),
            vm((NFFN, MP, QUARTER, width), bf16),
            vm((slots, hidden_cols), bf16),
            vm((2, slots, hidden_cols), bf16),
            vm((MP, QUARTER, wide), f32),
            vm((4, 2, QUARTER, wide), f32),
            vm((4, 2, QUARTER, wide), bf16),
            vm((NFFN, 2, QUARTER, wide), bf16),
            vm((4, QUARTER, wide), bf16),
            vm((NFFN, QUARTER, wide), bf16),
            vm((NFFN, QUARTER, wide), bf16),
            vm((MP, 8, rows), f32),
            vm((MP, 8, rows), f32),
            vm((2, rows, width), bf16),
            vm((rows, width), bf16),
            vm((everyone, HD), f32),
            vm((everyone, HD), f32),
            vm((width, cols), bf16),
            vm((NFFN // 2, depth, cols), bf16),
            vm((NFFN // 2, depth, cols), bf16),
            vm((NFFN // 2, depth, cols), bf16),
            vm((NFFN, QUARTER, width), bf16),
            vm((2, NFFN, QUARTER, width), bf16),
            vm((NFFN, QUARTER, width), bf16),
            vm((5, 40, width), f32),
            vm((5, 40, width), f32),
            vm((MP, 1, width), f32),
            vm((NFFN, 1, width), f32),
            vm((2, 1, width), f32),
            dma((9,)), dma((9,)),
            dma((8,)), dma((8,)),
            dma((2, 8)), dma((2, 8)),
            dma((2,)),
            dma((3,)), dma((3,)),
            dma((8,)), dma((8,)),
            dma((8,)), dma((8,)),
            dma((8, 3)), dma((8, 3)),
            dma((8, 3)), dma((8, 3)),
            dma((8, 3)), dma((8, 3)),
            dma((8,)), dma((8,)),
            dma((4,)), dma((4,)),
            dma((3,)), dma((3,)),
            dma((3,)), dma((3,)),
            dma((8,)), dma((8,)),
            dma((8,)), dma((8,)),
            dma((4,)), dma((4,)), dma((8,)),
            dma((3,)), dma((3,)),
            dma((3,)), dma((3,)),
            dma((8,)), dma((8,)),
            dma((5,)), dma((5,)),
            dma((MP + NFFN,)), dma((MP + NFFN,)),
        ],
        compiler_params=pltpu.CompilerParams(
            collective_id=0, has_side_effects=True, vmem_limit_bytes=VMEM_LIMIT
        ),
        name="layer",
    )(x, cot, params, routing, jnp.asarray(cos), jnp.asarray(sin), wshard, win, wout)


def clusters():
    groups = lax.axis_size("dp") // NFFN
    near = [[group * NFFN + expert for expert in range(NFFN)] for group in range(groups)]
    far = [[group * NFFN + expert for group in range(groups)] for expert in range(NFFN)]
    return groups, near, far


def exchange(shard, dim):
    _, near, far = clusters()
    own = lax.all_to_all(shard, "dp", 0, dim, axis_index_groups=near, tiled=True)
    return lax.all_gather(own, "dp", axis=dim, axis_index_groups=far, tiled=True)


def exchange_back(grads, dim):
    _, near, far = clusters()
    grads = lax.psum_scatter(
        grads.astype(f32), "dp", scatter_dimension=dim, axis_index_groups=far, tiled=True
    )
    return lax.all_to_all(grads.astype(bf16), "dp", dim, 0, axis_index_groups=near, tiled=True)


def per_device(
    inputs,
    query_key_value,
    output_weight,
    expert_input,
    expert_output,
    first_gain,
    second_gain,
    router_weight,
    logit_carry,
    constant_mix,
    constant_values,
    previous_logits,
    routes,
    cotangent,
):
    rows, width = inputs.shape
    groups, _, far = clusters()

    def padded(array, high, wide, value=0.0):
        return jnp.pad(
            array.astype(f32), ((0, high - array.shape[0]), (0, wide - array.shape[1])),
            constant_values=value,
        )

    params = jnp.concatenate(
        [
            padded(router_weight.T, 16, width),
            constant_mix.T.astype(f32),
            constant_values.astype(f32),
            second_gain.astype(f32)[None],
            first_gain.astype(f32)[None],
            padded(logit_carry, 16, width),
        ],
        axis=0,
    )
    everyone = rows * MP
    routing = jnp.concatenate(
        [padded(previous_logits.T, 16, everyone), padded(routes.T, 8, everyone, -1.0)], axis=0
    )
    shard_depth = query_key_value.shape[0]
    shard = jnp.concatenate(
        [query_key_value.reshape(shard_depth, -1), output_weight.T], axis=1
    )
    cols = output_weight.shape[0]
    expert_output_t = expert_output.transpose(0, 2, 1)
    if groups > 1:
        shard = lax.all_gather(shard, "dp", axis=0, tiled=True)
        win = exchange(expert_input, 2)[0]
        wout = exchange(expert_output_t, 1)[0]
    if groups == 1:
        win, wout = expert_input, expert_output_t
    output, input_grad, logits_grad, weight_grad, sums, first_grad, expert_grad = layer(
        inputs, cotangent, params, routing, shard, win, wout, groups
    )
    if groups > 1:
        weight_grad = lax.psum_scatter(weight_grad, "dp", scatter_dimension=0, tiled=True)
        whole = expert_grad.transpose(1, 0, 2, 3).reshape(1, 3, width, -1)
        expert_grad = exchange_back(whole, 2)
        sums, first_grad = lax.psum((sums, first_grad), "dp", axis_index_groups=far)
    expert_in_grad = expert_grad[:, :2].astype(f32)
    expert_out_grad = expert_grad[:, 2].transpose(0, 2, 1).astype(f32)
    return (
        output,
        input_grad,
        logits_grad[:NEXP].T,
        weight_grad[:, : 3 * cols].reshape(shard_depth, 3, cols),
        weight_grad[:, 3 * cols :].T,
        expert_in_grad,
        expert_out_grad,
        first_grad[0],
        sums[22],
        sums[:NEXP].T,
        sums[24 : 24 + NEXP, :NEXP],
        sums[16:20].T,
        sums[20:22],
    )


def solution(mesh):
    in_specs = (
        P(("dp", "mp"), None),
        P("dp", None, "mp"),
        P("mp", "dp"),
        P(None, None, "dp", "mp"),
        P(None, "mp", "dp"),
        P(),
        P(),
        P(),
        P(),
        P(),
        P(),
        P("dp", None),
        P("dp", None),
        P(("dp", "mp"), None),
    )
    out_specs = (
        P(("dp", "mp"), None),
        P(("dp", "mp"), None),
        P(("dp", "mp"), None),
        P("dp", None, "mp"),
        P("mp", "dp"),
        P(None, None, "dp", "mp"),
        P(None, "mp", "dp"),
        P(),
        P(),
        P(),
        P(),
        P(),
        P(),
    )
    return jax.shard_map(
        per_device, mesh=mesh, in_specs=in_specs, out_specs=out_specs, check_vma=False
    )
```

```python
import functools
import numpy as np
import jax
import jax.numpy as jnp
from jax import lax
from jax.sharding import PartitionSpec as P
from jax.experimental import pallas as pl
from jax.experimental.pallas import tpu as pltpu

HD = 64
NFFN = 8
NEXP = 12
SEQ = 1024
CAP = 256
MP = 4
QUARTER = CAP // MP
WIDE = 640
VMEM_LIMIT = 63 * 2**20

epsilon = 1e-06
rope_base = 10000.0
highest = lax.Precision.HIGHEST
f32 = jnp.float32
bf16 = jnp.bfloat16
MESH = pl.DeviceIdType.MESH
VM = pl.BlockSpec(memory_space=pltpu.VMEM)
HB = pl.BlockSpec(memory_space=pl.ANY)
NT = (((1,), (1,)), ((), ()))
TN = (((0,), (0,)), ((), ()))


def flip(index, distance):
    out = index
    bit = 1
    while bit <= distance:
        if distance & bit:
            out = out + bit - 2 * bit * ((index // bit) % 2)
        bit *= 2
    return out


def dotf(a, b, dims=None):
    if dims is None:
        return jnp.dot(a, b, preferred_element_type=f32)
    return lax.dot_general(a, b, dims, preferred_element_type=f32)


def remote(src, dst, send, recv, **where):
    return pltpu.make_async_remote_copy(
        src_ref=src, dst_ref=dst, send_sem=send, recv_sem=recv, device_id=where, device_id_type=MESH
    )


def greet(mp_me, near, base):
    barrier = pltpu.get_barrier_semaphore()
    for k in range(1, MP):
        pl.semaphore_signal(barrier, inc=1, device_id={"mp": flip(mp_me, k)}, device_id_type=MESH)
    for k in range(1, NFFN):
        pl.semaphore_signal(
            barrier, inc=1, device_id={"dp": base + flip(near, k)}, device_id_type=MESH
        )
    pl.semaphore_wait(barrier, MP - 1 + NFFN - 1)


def rope_constants():
    half = HD // 2
    positions = np.arange(SEQ, dtype=np.float32)
    frequency = (rope_base ** (-np.arange(half, dtype=np.float32) / half)).astype(np.float32)
    angles = (positions[:, None] * frequency[None, :]).astype(np.float32)
    cosine, sine = np.cos(angles), np.sin(angles)
    return (
        np.concatenate([cosine, cosine], axis=1),
        np.concatenate([-sine, sine], axis=1),
    )


def swap_halves(x):
    half = HD // 2
    return jnp.concatenate([x[:, half:], x[:, :half]], axis=1)


class Gather:
    def __init__(self, ref, mp_me, send, recv):
        self.me, self.core, self.chip = mp_me, flip(mp_me, 1), flip(mp_me, 2)
        own = ref.at[mp_me]
        far = ref.at[self.chip]
        self.to_chip = remote(own, own, send.at[0], recv.at[0], mp=self.chip)
        self.to_core = remote(own, own, send.at[1], recv.at[1], mp=self.core)
        self.relay = remote(far, far, send.at[2], recv.at[2], mp=self.core)

    def start(self):
        self.to_chip.start()
        self.to_core.start()

    def forward(self):
        self.to_chip.wait_recv()
        self.relay.start()

    def finish(self):
        self.to_core.wait_recv()
        self.relay.wait_recv()
        self.to_chip.wait_send()
        self.to_core.wait_send()
        self.relay.wait_send()


def pack3(value):
    high = value.astype(bf16).astype(f32)
    rest = value - high
    mid = rest.astype(bf16).astype(f32)
    low = (rest - mid).astype(bf16).astype(f32)
    lane = lax.broadcasted_iota(jnp.int32, (value.shape[0], 128), 1)
    return jnp.where(
        lane == 0, high, jnp.where(lane == 1, mid, jnp.where(lane == 2, low, 0.0))
    ).astype(bf16)


def unpack3(parts):
    return jnp.sum(parts.astype(f32), axis=-1, keepdims=True)


def exact(left, right, dims=None):
    high = left.astype(bf16)
    rest = left - high.astype(f32)
    mid = rest.astype(bf16)
    low = (rest - mid.astype(f32)).astype(bf16)
    return dotf(high, right, dims) + (dotf(mid, right, dims) + dotf(low, right, dims))


class Scatter:
    def __init__(self, mp_me, core_out, core_in, chip_out, chip_in, send, recv):
        self.me, self.core, self.chip = mp_me, flip(mp_me, 1), flip(mp_me, 2)
        self.core_out, self.core_in = core_out, core_in
        self.chip_out, self.chip_in = chip_out, chip_in
        self.to_core = [
            remote(core_out.at[j], core_in.at[j], send.at[j], recv.at[j], mp=self.core)
            for j in range(2)
        ]
        self.to_chip = remote(chip_out, chip_in, send.at[2], recv.at[2], mp=self.chip)

    def run(self, blocks):
        for j, block in enumerate((flip(self.me, 3), self.core)):
            self.core_out[j] = blocks(block).astype(bf16)
            self.to_core[j].start()
        term = blocks(self.chip)
        self.to_core[0].wait_recv()
        self.chip_out[...] = (term + self.core_in[0].astype(f32)).astype(bf16)
        self.to_chip.start()
        term = blocks(self.me)
        self.to_core[1].wait_recv()
        term = term + self.core_in[1].astype(f32)
        self.to_chip.wait_recv()
        return term + self.chip_in[...].astype(f32)

    def drain(self):
        for copy in self.to_core + [self.to_chip]:
            copy.wait_send()


def layer_kernel(
    inside,
    x_ref, cot_ref, router_ref, mix_ref, values_ref, gain2_ref, gain1_ref, carry_ref, previous_ref,
    routes_ref, cos_ref, sin_ref, wshard_ref, win_shard, wout_shard,
    output_ref, xgrad_ref, lgrad_ref, wgrad_ref, sums_ref, first_ref, dw_own,
    rows1_ref, w_ref, q_ref, k_ref, v_ref, mixed_ref, lse_ref, pick_ref, gate_ref, outp_ref, dw_ref,
    rows2_ref, hidden_ref, sum_ref, core_in, chip_out, chip_in, core_out,
    place_ref, gates_ref, prior_ref, msgx, msgc, xs, cs, units_ref, pgrad_ref,
    part_ref, keep_ref, gcore_out, gcore_in, gchip_out, gchip_in, gret, score_out, score_in,
    ncore_in, nchip_in,
    key_acc, value_acc, grads_ref, across_out, across_in, along_in, ret_ref,
    pcore_in, pchip_in, params_ref, routing_ref,
    sum_out, sum_in, first_mp, first_dp, first_out,
    sends, recvs, wsend, wrecv, esend, erecv, local,
    csend, crecv, xsend, xrecv, dsend, drecv, xgs, xgr, cgs, cgr, gsend, grecv,
    rsend, rrecv, ssend, srecv, nsend, nrecv,
    asend, arecv, osend, orecv, msend, mrecv, psend, precv, mlocal, bsend, brecv, tsend, trecv,
    vsend, vrecv, zsend, zrecv, fsend, frecv,
):
    cot_all = rows2_ref
    residual_ref = sum_ref
    hgrad_ref = xgrad_ref
    small_ref = sum_out.at[0]
    mp_me = lax.axis_index("mp")
    dp_me = lax.axis_index("dp")
    near = lax.rem(dp_me, NFFN)
    base = dp_me - near
    core, chip, far = flip(mp_me, 1), flip(mp_me, 2), flip(mp_me, 3)
    rows, width = x_ref.shape
    everyone = MP * rows
    greet(mp_me, near, base)

    params_ref[...] = jnp.zeros_like(params_ref)
    params_ref[0:NEXP] = router_ref[...].astype(f32)
    params_ref[16:20] = mix_ref[...].astype(f32)
    params_ref[20:22] = values_ref[...].astype(f32)
    params_ref[22:23] = gain2_ref[...].astype(f32)
    params_ref[23:24] = gain1_ref[...].astype(f32)
    params_ref[24 : 24 + NEXP, 0:NEXP] = carry_ref[...]
    routing_ref[...] = jnp.zeros_like(routing_ref)
    routing_ref[0:NEXP] = previous_ref[...]
    routing_ref[16:18] = routes_ref[...].astype(f32)

    tokens = x_ref[...].astype(f32)
    scale = lax.rsqrt(jnp.mean(tokens * tokens, axis=-1, keepdims=True) + epsilon)
    rows1_ref[mp_me] = (tokens * scale * params_ref[23:24]).astype(bf16)
    gather1 = Gather(rows1_ref, mp_me, sends.at[pl.ds(0, 3)], recvs.at[pl.ds(0, 3)])
    gather1.start()
    if inside:
        w_ref[near] = wshard_ref[...]
        own = w_ref.at[near]
        along = [
            remote(own, own, wsend.at[k], wrecv.at[k], dp=base + flip(near, k)) for k in (2, 4, 6)
        ]
        for copy in along:
            copy.start()
        mate = base + flip(near, 1)
        across = [remote(own, own, wsend.at[0], wrecv.at[0], dp=mate)]
        across[0].start()
    cot_all[mp_me] = cot_ref[...]
    cot_gather = Gather(cot_all, mp_me, csend, crecv)
    cot_gather.start()

    ids = lax.broadcasted_iota(jnp.int32, (16, everyone), 0).astype(f32)
    chosen = (ids == routing_ref[16:17]) | (ids == routing_ref[17:18])
    earlier = lax.broadcasted_iota(jnp.int32, (everyone, everyone), 0) < lax.broadcasted_iota(
        jnp.int32, (everyone, everyone), 1
    )
    counts = dotf(
        jnp.where(chosen, 1.0, 0.0).astype(bf16), jnp.where(earlier, 1.0, 0.0).astype(bf16)
    )
    place_ref[...] = jnp.where(chosen, counts, -1.0)
    wanted = (lax.broadcasted_iota(jnp.int32, (QUARTER, everyone), 0) + QUARTER * mp_me).astype(f32)

    def target(k):
        return lax.rem(near + k, NFFN)

    def choose(k, carried):
        pick = wanted == place_ref[pl.ds(target(k), 1)]
        pick_ref[k] = jnp.where(pick, 1.0, 0.0).astype(bf16)
        return carried

    lax.fori_loop(0, NFFN, choose, 0)
    carry = params_ref[24:40, 0:16]
    prior_ref[...] = lax.dot_general(
        carry, routing_ref[0:16], TN, preferred_element_type=f32, precision=highest
    )

    if inside:
        for k, copy in zip((2, 4, 6), along):
            copy.wait_recv()
            block = w_ref.at[flip(near, k)]
            onward = remote(block, block, wsend.at[k + 1], wrecv.at[k + 1], dp=mate)
            onward.start()
            across.append(onward)
        gather1.forward()
        for copy in across:
            copy.wait_recv()
        for copy in along + across:
            copy.wait_send()
        weights = []
        din = win_shard.shape[2]
        place = pl.ds(pl.multiple_of(near * din, din), din)
        for k in (4, 2, 6, 5, 7, 3, 1):
            peer = flip(near, k)
            for i, (src, dst) in enumerate([
                (win_shard.at[peer], dw_ref.at[0:2, place]),
                (wout_shard.at[peer], dw_ref.at[2, place]),
            ]):
                weights.append(
                    remote(src, dst, esend.at[i, k], erecv.at[i, k], dp=base + peer)
                )
        first = 4
        for copy in weights[:first]:
            copy.start()
        mine = [
            pltpu.make_async_copy(win_shard.at[near], dw_ref.at[0:2, place], local.at[0]),
            pltpu.make_async_copy(wout_shard.at[near], dw_ref.at[2, place], local.at[1]),
        ]
        for copy in mine:
            copy.start()
    else:
        w_ref[...] = wshard_ref[...]
        mine = [
            pltpu.make_async_copy(win_shard, dw_ref.at[0:2], local.at[0]),
            pltpu.make_async_copy(wout_shard, dw_ref.at[2], local.at[1]),
        ]
        for copy in mine:
            copy.start()
        gather1.forward()
    gather1.finish()

    cot_gather.forward()
    cot_gather.finish()

    def c_copy(k):
        return remote(
            msgc.at[k], cs.at[k, mp_me], dsend.at[k], drecv.at[k], dp=base + target(k)
        )

    def send(picked, ref, copy, lanes):
        def half(i, carried):
            start = 4 - 4 * i
            blocks = dotf(pick_ref[pl.ds(start, 4)].reshape(4 * QUARTER, everyone), picked())
            ref[(pl.ds(start, 4),) + lanes] = blocks.astype(bf16).reshape(4, QUARTER, width)

            def go(k, inner):
                @pl.when(k > 0)
                def _():
                    copy(k).start()

                return inner

            return lax.fori_loop(start, start + 4, go, carried)

        lax.fori_loop(0, 2, half, 0)

    send(lambda: cot_all[...].reshape(everyone, width), msgc, c_copy, ())
    cs[0, mp_me] = msgc[0]
    if inside:
        for copy in weights[first:]:
            copy.start()

    w_all = w_ref[...].reshape(width, w_ref.shape[2])
    heads = q_ref.shape[0]
    cols = heads * HD

    def project(i, carry):
        at = pl.ds(pl.multiple_of(i * rows, rows), rows)
        joint = dotf(rows1_ref[i], w_all[:, : 3 * cols])
        cosine, sine = cos_ref[at], sin_ref[at]
        for h in range(heads):
            query = joint[:, h * HD : (h + 1) * HD]
            key = joint[:, cols + h * HD : cols + (h + 1) * HD]
            q_ref[h, at] = (query * cosine + swap_halves(query) * sine).astype(bf16)
            k_ref[h, at] = (key * cosine + swap_halves(key) * sine).astype(bf16)
            v_ref[h, at] = joint[:, 2 * cols + h * HD : 2 * cols + (h + 1) * HD].astype(bf16)
        return carry

    lax.fori_loop(0, MP, project, 0)
    out_weight = w_all[:, 3 * cols :]

    to_core = [
        remote(core_out.at[j], core_in.at[j], sends.at[3 + j], recvs.at[3 + j], mp=core)
        for j in range(2)
    ]
    to_chip = remote(chip_out, chip_in, sends.at[5], recvs.at[5], mp=chip)

    def attend(step, carry):
        block = flip(mp_me, 3)
        block = jnp.where(step == 1, core, jnp.where(step == 2, chip, jnp.where(step == 3, mp_me, block)))
        at = pl.ds(pl.multiple_of(block * rows, rows), rows)
        row_ids = block * rows + lax.broadcasted_iota(jnp.int32, (rows, SEQ), 0)
        seen = row_ids >= lax.broadcasted_iota(jnp.int32, (rows, SEQ), 1)
        for h in range(heads):
            scores = dotf(q_ref[h, at], k_ref[h], NT) * HD**-0.5
            scores = jnp.where(seen, scores, -jnp.inf)
            peak = jnp.max(scores, axis=-1, keepdims=True)
            exponent = jnp.exp(scores - peak)
            total = jnp.sum(exponent, axis=-1, keepdims=True)
            probs = (exponent * (1.0 / total)).astype(bf16)
            mixed_ref[at, h * HD : (h + 1) * HD] = dotf(probs, v_ref[h]).astype(bf16)
            lse_ref[at, h : h + 1] = peak + jnp.log(total)
        part = dotf(mixed_ref[at], out_weight, NT)

        @pl.when(step == 0)
        def _():
            core_out[0] = part.astype(bf16)
            to_core[0].start()

        @pl.when(step == 1)
        def _():
            core_out[1] = part.astype(bf16)
            to_core[1].start()

        @pl.when(step == 2)
        def _():
            to_core[0].wait_recv()
            chip_out[...] = (part + core_in[0].astype(f32)).astype(bf16)
            to_chip.start()

        @pl.when(step == 3)
        def _():
            sum_ref[...] = part

        return carry

    lax.fori_loop(0, MP, attend, 0)
    to_core[1].wait_recv()
    partial = sum_ref[...] + core_in[1].astype(f32)
    to_chip.wait_recv()
    hidden = x_ref[...].astype(f32) + (partial + chip_in[...].astype(f32))
    hidden_ref[...] = hidden
    scale2 = lax.rsqrt(jnp.mean(hidden * hidden, axis=-1, keepdims=True) + epsilon)
    rows2_ref[mp_me] = (hidden * scale2 * params_ref[22:23]).astype(bf16)
    gather2 = Gather(rows2_ref, mp_me, sends.at[pl.ds(6, 3)], recvs.at[pl.ds(6, 3)])
    gather2.start()
    for copy in to_core + [to_chip]:
        copy.wait_send()
    gather2.forward()

    def turn(i):
        return lax.rem(i + 4, NFFN)

    def c_gather(k):
        return Gather(cs.at[k], mp_me, cgs.at[k], cgr.at[k])

    def at_step(i, first, body):
        @pl.when((i >= first) & (i < NFFN + first))
        def _():
            body(turn(i - first))

    def cot_step(i, carried):
        def arrived(k):
            @pl.when(k > 0)
            def _():
                c_copy(k).wait_recv()

            c_gather(k).start()

        at_step(i, 0, arrived)
        at_step(i, 1, lambda k: c_gather(k).forward())
        return carried

    lax.fori_loop(0, NFFN + 1, cot_step, 0)
    gather2.finish()

    router = params_ref[0:16].astype(bf16)
    mix = params_ref[16:20].astype(bf16)
    tokens = rows2_ref[...].reshape(everyone, width)
    logits = dotf(router, tokens, NT) + prior_ref[...]
    masked = jnp.where(place_ref[...] >= 0.0, logits, -jnp.inf)
    exponent = jnp.exp(masked - jnp.max(masked, axis=0, keepdims=True))
    gates_ref[...] = exponent / jnp.sum(exponent, axis=0, keepdims=True)

    def weigh(k, carried):
        gate = jnp.sum(
            pick_ref[k].astype(f32) * gates_ref[pl.ds(target(k), 1)], axis=1, keepdims=True
        )
        gate_ref[k] = jnp.broadcast_to(gate, (QUARTER, 128))
        msgx[k, :, width:] = pack3(gate)
        return carried

    lax.fori_loop(0, NFFN, weigh, 0)

    def x_copy(k):
        return remote(
            msgx.at[k], xs.at[k, mp_me], xsend.at[k], xrecv.at[k], dp=base + target(k)
        )

    send(
        lambda: rows2_ref[...].reshape(everyone, width), msgx, x_copy,
        (slice(None), slice(0, width)),
    )
    xs[0, mp_me] = msgx[0]

    def x_gather(k):
        return Gather(xs.at[k], mp_me, xgs.at[k], xgr.at[k])

    def slots_of(k):
        return pl.ds(pl.multiple_of(k * CAP, CAP), CAP)

    def x_step(i, carried):
        def arrived(k):
            @pl.when(k > 0)
            def _():
                x_copy(k).wait_recv()

            x_gather(k).start()

        def passed(k):
            x_gather(k).forward()

        at_step(i, 0, arrived)
        at_step(i, 1, passed)
        return carried

    lax.fori_loop(0, NFFN + 1, x_step, 0)
    if inside:
        for copy in weights:
            copy.wait_recv()
    for copy in mine:
        copy.wait()

    def r_trip(k):
        slot = lax.rem(k, 4)
        return Scatter(
            mp_me, gcore_out.at[slot], gcore_in.at[k], gchip_out.at[slot], gchip_in.at[k],
            gsend.at[k], grecv.at[k],
        )

    def g_copy(k):
        return remote(
            msgx.at[k], gret.at[k], rsend.at[k], rrecv.at[k],
            dp=base + lax.rem(near - k + NFFN, NFFN),
        )

    def seal(ref, index, total):
        ref[index + (slice(None), slice(0, width))] = total[:, :width].astype(bf16)
        ref[index + (slice(None), slice(width, None))] = pack3(unpack3(total[:, width:]))

    def expert_step(i, carried):
        def compute(k):
            c_gather(k).finish()
            x_gather(k).finish()
            x = xs[k].reshape(CAP, width + 128)[:, :width]
            gate = unpack3(xs[k].reshape(CAP, width + 128)[:, width:])
            c = cs[k].reshape(CAP, width)
            gate_pre = dotf(x, dw_ref[0])
            up_pre = dotf(x, dw_ref[1])
            sig = jax.nn.sigmoid(gate_pre)
            units = (gate_pre * sig * up_pre).astype(bf16)
            units_ref[slots_of(k)] = units
            outp_ref[k] = dotf(units, dw_ref[2], NT).astype(bf16).reshape(MP, QUARTER, width)
            raw = dotf(c, dw_ref[2])
            score = jnp.sum(units.astype(f32) * raw, axis=1, keepdims=True)
            units_grad = raw * gate
            gate_grad = (units_grad * up_pre * sig * (1.0 + gate_pre * (1.0 - sig))).astype(bf16)
            up_grad = (units_grad * (gate_pre * sig)).astype(bf16)
            pgrad_ref[0, slots_of(k)] = gate_grad
            pgrad_ref[1, slots_of(k)] = up_grad
            back = dotf(gate_grad, dw_ref[0], NT) + dotf(up_grad, dw_ref[1], NT)
            cs[k] = (c.astype(f32) * gate).astype(bf16).reshape(MP, QUARTER, width)
            part_ref[:, :, :width] = back.reshape(MP, QUARTER, width)
            part_ref[:, :, width:] = pack3(score).astype(f32).reshape(MP, QUARTER, 128)
            slot = lax.rem(k, 4)
            gcore_out[slot, 0] = part_ref[far].astype(bf16)
            gcore_out[slot, 1] = part_ref[core].astype(bf16)
            keep_ref[slot, 0] = part_ref[chip]
            keep_ref[slot, 1] = part_ref[mp_me]
            for copy in r_trip(k).to_core:
                copy.start()

        def across(k):
            trip = r_trip(k)
            trip.to_core[0].wait_recv()
            seal(gchip_out, (lax.rem(k, 4),), keep_ref[lax.rem(k, 4), 0] + gcore_in[k, 0].astype(f32))
            trip.to_chip.start()

        def away(k):
            trip = r_trip(k)
            trip.to_core[1].wait_recv()
            trip.to_chip.wait_recv()
            total = (
                keep_ref[lax.rem(k, 4), 1]
                + gcore_in[k, 1].astype(f32)
                + gchip_in[k].astype(f32)
            )
            trip.drain()

            @pl.when(k > 0)
            def _():
                x_copy(k).wait_send()

            seal(msgx, (k,), total)

            @pl.when(k > 0)
            def _():
                g_copy(k).start()

            @pl.when(k == 0)
            def _():
                gret[0] = msgx[0]

        at_step(i, 4, away)
        at_step(i, 0, compute)
        at_step(i, 2, across)
        return carried

    lax.fori_loop(0, NFFN + 4, expert_step, 0)

    p_core = [
        remote(outp_ref.at[:, far], pcore_in.at[0], psend.at[0], precv.at[0], mp=core),
        remote(outp_ref.at[:, core], pcore_in.at[1], psend.at[1], precv.at[1], mp=core),
    ]
    for copy in p_core:
        copy.start()
    parts = (slice(4, 8), slice(0, 4))
    p_chip = [
        remote(cs.at[part, 3], pchip_in.at[part], psend.at[2 + j], precv.at[2 + j], mp=chip)
        for j, part in enumerate(parts)
    ]
    returns = {
        k: remote(msgc.at[k], ret_ref.at[k], osend.at[k], orecv.at[k],
                  dp=base + lax.rem(near - k + NFFN, NFFN))
        for k in range(1, NFFN)
    }

    def results_across():
        p_core[0].wait_recv()
        for j, part in enumerate(parts):
            cs[part, 3] = (
                outp_ref[part, chip].astype(f32) + pcore_in[0, part].astype(f32)
            ).astype(bf16)
            p_chip[j].start()

    def results_away(j):
        part = parts[j]
        if j == 0:
            p_core[1].wait_recv()
        p_chip[j].wait_recv()
        msgc[part] = (
            outp_ref[part, mp_me].astype(f32)
            + (pcore_in[1, part].astype(f32) + pchip_in[part].astype(f32))
        ).astype(bf16)
        for k in range(part.start, part.stop):
            if k > 0:
                returns[k].start()
            else:
                ret_ref[0] = msgc[0]

    def weights_step(j, carried):
        at = pl.ds(pl.multiple_of(j * 128, 128), 128)
        x = xs[:, :, :, at].reshape(NFFN * CAP, 128)
        c = cs[:, :, :, at].reshape(NFFN * CAP, 128)
        dw_ref[0, at] = dotf(x, pgrad_ref[0], TN).astype(bf16)
        dw_ref[1, at] = dotf(x, pgrad_ref[1], TN).astype(bf16)
        dw_ref[2, at] = dotf(c, units_ref[...], TN).astype(bf16)
        return carried

    lax.fori_loop(0, width // 128, weights_step, 0)

    din = dw_own.shape[2]

    def rows_of(index):
        return pl.ds(pl.multiple_of(index * din, din), din)

    if inside:
        moved = [
            remote(dw_ref.at[:, rows_of(flip(near, k))], dw_own.at[near], msend.at[k],
                   mrecv.at[k], dp=base + flip(near, k))
            for k in (4, 6, 5, 7, 2, 3, 1)
        ]
        kept = [pltpu.make_async_copy(dw_ref.at[:, rows_of(near)], dw_own.at[near], mlocal.at[0])]
    else:
        moved = []
        kept = [
            pltpu.make_async_copy(dw_ref.at[:, rows_of(p)], dw_own.at[p], mlocal.at[p])
            for p in range(NFFN)
        ]
    early = 7
    for copy in moved[:early] + kept:
        copy.start()
    results_across()

    n_bf = rows2_ref[mp_me]
    n = n_bf.astype(f32)
    cot = cot_ref[...].astype(f32)
    hidden = hidden_ref[...]
    lane = lax.broadcasted_iota(jnp.int32, (rows, 128), 1)
    own_at = pl.ds(pl.multiple_of(mp_me * rows, rows), rows)
    gates_t = gates_ref[:, own_at]
    own_gates = jnp.concatenate([gates_t, jnp.zeros((112, rows), f32)], axis=0).T
    copy_gate = own_gates[:, NFFN + 1 : NFFN + 2]
    const_gates = [own_gates[:, NFFN + 2 : NFFN + 3], own_gates[:, NFFN + 3 : NFFN + 4]]
    mix_logits = dotf(n_bf, mix, NT)
    with_normed = jnp.sum(cot * n, axis=1, keepdims=True)
    residual = hidden + copy_gate * n
    local_grad = copy_gate * cot
    local_scores = jnp.where(lane == NFFN + 1, with_normed, 0.0)
    mix_grads = jnp.zeros((rows, 128), f32)
    for c in range(2):
        first, second = mix_logits[:, 2 * c : 2 * c + 1], mix_logits[:, 2 * c + 1 : 2 * c + 2]
        top = jnp.maximum(first, second)
        first, second = jnp.exp(first - top), jnp.exp(second - top)
        share = 1.0 / (first + second)
        first, second = first * share, second * share
        constant = params_ref[20 + c : 21 + c]
        with_constant = jnp.sum(cot * constant, axis=1, keepdims=True)
        gate = const_gates[c]
        residual = residual + gate * (first * n + second * constant)
        local_scores = jnp.where(
            lane == NFFN + 2 + c, first * with_normed + second * with_constant, local_scores
        )
        local_grad = local_grad + (first * gate) * cot
        small_ref[20 + c : 21 + c] = jnp.sum((second * gate) * cot, axis=0, keepdims=True)
        grad_first, grad_second = gate * with_normed, gate * with_constant
        mean = first * grad_first + second * grad_second
        mix_grads = jnp.where(lane == 2 * c, first * (grad_first - mean), mix_grads)
        mix_grads = jnp.where(lane == 2 * c + 1, second * (grad_second - mean), mix_grads)
    residual_ref[...] = residual

    def returned(k, carried):
        g_copy(k).wait_recv()
        return carried

    lax.fori_loop(1, NFFN, returned, 0)
    ret = gret[...].reshape(NFFN * QUARTER, width + 128)
    score_out[...] = jnp.zeros_like(score_out)

    def give_scores(k, carried):
        slots = unpack3(gret[k, :, width:])
        row = jnp.sum(pick_ref[k].astype(f32) * slots, axis=0, keepdims=True)
        for q in range(MP):
            score_out[q, pl.ds(target(k), 1)] = row[:, q * rows : (q + 1) * rows]
        return carried

    lax.fori_loop(0, NFFN, give_scores, 0)
    score_copies = [
        remote(score_out.at[flip(mp_me, k)], score_in.at[k], ssend.at[k], srecv.at[k], mp=flip(mp_me, k))
        for k in range(1, MP)
    ]
    for copy in score_copies:
        copy.start()

    def grad_block(q):
        at = pl.ds(pl.multiple_of(q * rows, rows), rows)
        return dotf(
            pick_ref[:, :, at].reshape(NFFN * QUARTER, rows), ret[:, :width], TN
        )

    trip = Scatter(mp_me, core_out, ncore_in, chip_out, nchip_in, nsend, nrecv)
    normed_grad = trip.run(grad_block) + local_grad
    lax.fori_loop(1, NFFN, lambda k, carried: (c_copy(k).wait_send(), carried)[1], 0)
    results_away(0)
    results_away(1)
    for copy in moved[early:]:
        copy.start()

    for copy in score_copies:
        copy.wait_recv()
    ffn_scores = (score_out[mp_me] + score_in[1]) + (score_in[2] + score_in[3])
    scores = local_scores.T[:16] + jnp.concatenate([ffn_scores, jnp.zeros((8, rows), f32)], axis=0)
    logit_grad = gates_t * (scores - jnp.sum(gates_t * scores, axis=0, keepdims=True))
    lgrad_ref[...] = lax.dot_general(
        carry, logit_grad, (((1,), (0,)), ((), ())),
        preferred_element_type=f32, precision=highest,
    )
    small_ref[24:40] = jnp.zeros((16, width), f32)
    small_ref[24:40, 0:16] = lax.dot_general(
        routing_ref[0:16, own_at], logit_grad, NT, preferred_element_type=f32, precision=highest
    )
    stacked = jnp.concatenate([logit_grad, mix_grads.T[:16]], axis=0)
    stack = params_ref[0:32]
    sublane = lax.broadcasted_iota(jnp.int32, (32, width), 0)
    stack = jnp.where(sublane < 20, stack, 0.0).astype(bf16)
    feature_grads = exact(stacked, n_bf)
    small_ref[0:20] = feature_grads[0:20]
    normed_grad = normed_grad + exact(stacked, stack, TN)
    scale = lax.rsqrt(jnp.mean(hidden * hidden, axis=-1, keepdims=True) + epsilon)
    scaled = hidden * scale
    small_ref[22:23] = jnp.sum(normed_grad * scaled, axis=0, keepdims=True)
    small_ref[23:24] = jnp.zeros((1, width), f32)
    weighted = normed_grad * params_ref[22:23]
    hidden_grad = cot + scale * (
        weighted - scaled * jnp.mean(weighted * scaled, axis=-1, keepdims=True)
    )
    hgrad_ref[...] = hidden_grad
    rows2_ref[mp_me] = hidden_grad.astype(bf16)
    agather = Gather(rows2_ref, mp_me, asend, arecv)
    agather.start()

    trip.drain()
    for copy in score_copies:
        copy.wait_send()

    def drain(k, carried):
        g_copy(k).wait_send()
        return carried

    lax.fori_loop(1, NFFN, drain, 0)
    if inside:
        for copy in weights:
            copy.wait_send()

    places = [{"mp": flip(mp_me, 1)}, {"mp": flip(mp_me, 2)}] + [
        {"dp": base + flip(near, k)} for k in (1, 2, 4)
    ]
    stages = [
        remote(sum_out.at[j], sum_in.at[j], zsend.at[j], zrecv.at[j], **where)
        for j, where in enumerate(places)
    ]

    def stage(j):
        if j > 0:
            stages[j - 1].wait_recv()
            total = sum_out[j - 1] + sum_in[j - 1]
            if j == len(stages):
                sums_ref[...] = total
                return
            sum_out[j] = total
        stages[j].start()

    stage(0)
    agather.forward()
    stage(1)
    agather.finish()

    w_all = w_ref[...].reshape(width, w_ref.shape[2])
    out_weight = w_all[:, 3 * cols :]
    for i in range(MP):
        xs[i, :, :, WIDE : WIDE + cols] = (
            dotf(rows2_ref[i], out_weight).astype(bf16).reshape(MP, QUARTER, cols)
        )
    grads_ref[:, 3 * cols :] = dotf(rows2_ref[...].reshape(everyone, width), mixed_ref[...], TN).astype(bf16)

    combine = Scatter(mp_me, core_out, ncore_in, chip_out, nchip_in, bsend, brecv)

    def out_block(q):
        at = pl.ds(pl.multiple_of(q * rows, rows), rows)
        weighted = (ret_ref[...].astype(f32) * gate_ref[:, :, 0:1]).astype(bf16)
        return dotf(
            pick_ref[:, :, at].reshape(NFFN * QUARTER, rows),
            weighted.reshape(NFFN * QUARTER, width), TN,
        )

    def head_back(h):
        lanes = slice(h * HD, (h + 1) * HD)
        for b in range(MP):
            at = slice(b * rows, (b + 1) * rows)
            seen = (b + 1) * rows
            query = q_ref[h, at]
            keys = k_ref[h, :seen]
            out_grad = xs[b, :, :, WIDE + h * HD : WIDE + (h + 1) * HD].reshape(rows, HD)
            scores = dotf(query, keys, NT) * HD**-0.5
            allowed = b * rows + lax.broadcasted_iota(
                jnp.int32, (rows, seen), 0
            ) >= lax.broadcasted_iota(jnp.int32, (rows, seen), 1)
            probs = jnp.where(allowed, jnp.exp(scores - lse_ref[at, h : h + 1]), 0.0)
            probs_grad = dotf(out_grad, v_ref[h, :seen], NT)
            inner = jnp.sum(probs * probs_grad, axis=1, keepdims=True)
            score_grad = (probs * (probs_grad - inner)).astype(bf16)
            query_grad = dotf(score_grad, keys) * HD**-0.5
            xs[b, :, :, lanes] = (
                (query_grad * cos_ref[at] - swap_halves(query_grad) * sin_ref[at])
                .astype(bf16)
                .reshape(MP, QUARTER, HD)
            )
            key_grad = dotf(score_grad, query, TN) * HD**-0.5
            value_grad = dotf(probs.astype(bf16), out_grad, TN)
            if b == 0:
                key_acc[...] = jnp.zeros_like(key_acc)
                value_acc[...] = jnp.zeros_like(value_acc)
            key_acc[:seen] += key_grad
            value_acc[:seen] += value_grad
        key_grad = key_acc[...]
        key_grad = key_grad * cos_ref[...] - swap_halves(key_grad) * sin_ref[...]
        xs[0:MP, :, :, cols + h * HD : cols + (h + 1) * HD] = key_grad.astype(bf16).reshape(
            MP, MP, QUARTER, HD
        )
        xs[0:MP, :, :, 2 * cols + h * HD : 2 * cols + (h + 1) * HD] = (
            value_acc[...].astype(bf16).reshape(MP, MP, QUARTER, HD)
        )

    last = heads - 1
    for h in range(heads):
        head_back(h)
        if h == 0:
            stage(2)
        if h == last:
            stage(3)

    depth = width // NFFN
    grads_ref[:, : 3 * cols] = dotf(
        rows1_ref[...].reshape(everyone, width),
        xs[0:MP, :, :, 0 : 3 * cols].reshape(everyone, 3 * cols), TN,
    ).astype(bf16)
    if inside:
        lean = lax.rem(near, 2)
        tall = grads_ref[...].reshape(NFFN // 2, 2, depth, grads_ref.shape[1])
        across_out[...] = jnp.where(lean == 0, tall[:, 1], tall[:, 0])
        kept_half = jnp.where(lean == 0, tall[:, 0], tall[:, 1])
        over = remote(across_out, across_in, vsend.at[0], vrecv.at[0], dp=base + flip(near, 1))
        over.start()
    else:
        wgrad_ref[...] = grads_ref[...].astype(f32)
    stage(4)

    home = Scatter(mp_me, core_out, core_in, chip_out, chip_in, tsend, trecv)

    def x_block(q):
        joint = xs[q, :, :, 0 : 3 * cols].reshape(rows, 3 * cols)
        return dotf(joint, w_all[:, : 3 * cols], NT)

    normed_grad = home.run(x_block)
    home.drain()
    if inside:
        over.wait_recv()
        over.wait_send()
        across_out[...] = (kept_half.astype(f32) + across_in[...].astype(f32)).astype(bf16)
        up = near // 2
        alongs = [
            remote(across_out.at[flip(near, k) // 2], along_in.at[k // 2], vsend.at[k], vrecv.at[k],
                   dp=base + flip(near, k))
            for k in (4, 6, 2)
        ]
        for copy in alongs:
            copy.start()
    tokens = x_ref[...].astype(f32)
    scale = lax.rsqrt(jnp.mean(tokens * tokens, axis=-1, keepdims=True) + epsilon)
    scaled = tokens * scale
    first_out[0] = jnp.sum(normed_grad * scaled, axis=0, keepdims=True)
    firsts = [
        remote(first_out.at[0], first_mp.at[k], fsend.at[k], frecv.at[k], mp=flip(mp_me, k))
        for k in range(1, MP)
    ]
    for copy in firsts:
        copy.start()
    weighted = normed_grad * params_ref[23:24]
    xgrad_ref[...] = hgrad_ref[...] + scale * (
        weighted - scaled * jnp.mean(weighted * scaled, axis=-1, keepdims=True)
    )
    for copy in firsts:
        copy.wait_recv()
    first_out[1] = first_out[0] + first_mp[1] + first_mp[2] + first_mp[3]
    seconds = [
        remote(first_out.at[1], first_dp.at[k], fsend.at[MP + k], frecv.at[MP + k],
               dp=base + flip(near, k))
        for k in range(1, NFFN)
    ]
    for copy in seconds:
        copy.start()
    stage(5)
    for copy in returns.values():
        copy.wait_recv()
    routed = combine.run(out_block)
    output_ref[...] = (residual_ref[...] + routed).astype(bf16)
    if inside:
        for copy in alongs:
            copy.wait_recv()
        wgrad_ref[...] = across_out[up].astype(f32) + (
            along_in[1].astype(f32) + along_in[2].astype(f32) + along_in[3].astype(f32)
        )
    for copy in seconds:
        copy.wait_recv()
    total = first_out[1]
    for k in range(1, NFFN):
        total = total + first_dp[k]
    first_ref[...] = total

    for copy in moved:
        copy.wait_recv()
    for copy in kept:
        copy.wait()
    if inside:
        for copy in alongs:
            copy.wait_send()
    for copy in moved + p_core + p_chip + list(returns.values()) + stages + firsts + seconds:
        copy.wait_send()
    combine.drain()


def layer(x, cot, small, wshard, win, wout, groups):
    rows, width = x.shape
    cos, sin = rope_constants()
    inside = groups == 1
    cols = wshard.shape[-1]
    depth = width // NFFN
    hidden_cols = win.shape[-1]
    heads = cols // 4 // HD
    everyone = MP * rows
    slots = NFFN * CAP
    wide = width + 128
    sd = jax.ShapeDtypeStruct
    vm = pltpu.VMEM
    dma = pltpu.SemaphoreType.DMA
    outs = [
        sd((rows, width), bf16),
        sd((rows, width), f32),
        sd((16, rows), f32),
        sd((depth if inside else width, cols), f32),
        sd((40, width), f32),
        sd((1, width), f32),
        sd((NFFN, 3, depth, hidden_cols), bf16),
    ]
    if not inside:
        wshard = wshard.reshape(NFFN, depth, cols)
    return pl.pallas_call(
        functools.partial(layer_kernel, inside),
        out_shape=outs,
        in_specs=[VM] * 13 + [HB, HB],
        out_specs=[VM] * 6 + [HB],
        scratch_shapes=[
            vm((MP, rows, width), bf16),
            vm((NFFN, depth, cols), bf16),
            vm((heads, SEQ, HD), bf16),
            vm((heads, SEQ, HD), bf16),
            vm((heads, SEQ, HD), bf16),
            vm((SEQ, heads * HD), bf16),
            vm((SEQ, 128), f32),
            vm((NFFN, QUARTER, everyone), bf16),
            vm((NFFN, QUARTER, 128), f32),
            vm((NFFN, MP, QUARTER, width), bf16),
            vm((3, width, hidden_cols), bf16),
            vm((MP, rows, width), bf16),
            vm((rows, width), f32),
            vm((rows, width), f32),
            vm((2, rows, width), bf16),
            vm((rows, width), bf16),
            vm((rows, width), bf16),
            vm((2, rows, width), bf16),
            vm((16, everyone), f32),
            vm((16, everyone), f32),
            vm((16, everyone), f32),
            vm((NFFN, QUARTER, wide), bf16),
            vm((NFFN, QUARTER, width), bf16),
            vm((NFFN, MP, QUARTER, wide), bf16),
            vm((NFFN, MP, QUARTER, width), bf16),
            vm((slots, hidden_cols), bf16),
            vm((2, slots, hidden_cols), bf16),
            vm((MP, QUARTER, wide), f32),
            vm((4, 2, QUARTER, wide), f32),
            vm((4, 2, QUARTER, wide), bf16),
            vm((NFFN, 2, QUARTER, wide), bf16),
            vm((4, QUARTER, wide), bf16),
            vm((NFFN, QUARTER, wide), bf16),
            vm((NFFN, QUARTER, wide), bf16),
            vm((MP, 8, rows), f32),
            vm((MP, 8, rows), f32),
            vm((2, rows, width), bf16),
            vm((rows, width), bf16),
            vm((everyone, HD), f32),
            vm((everyone, HD), f32),
            vm((width, cols), bf16),
            vm((NFFN // 2, depth, cols), bf16),
            vm((NFFN // 2, depth, cols), bf16),
            vm((NFFN // 2, depth, cols), bf16),
            vm((NFFN, QUARTER, width), bf16),
            vm((2, NFFN, QUARTER, width), bf16),
            vm((NFFN, QUARTER, width), bf16),
            vm((40, width), f32),
            vm((24, everyone), f32),
            vm((5, 40, width), f32),
            vm((5, 40, width), f32),
            vm((MP, 1, width), f32),
            vm((NFFN, 1, width), f32),
            vm((2, 1, width), f32),
            dma((9,)), dma((9,)),
            dma((8,)), dma((8,)),
            dma((2, 8)), dma((2, 8)),
            dma((2,)),
            dma((3,)), dma((3,)),
            dma((8,)), dma((8,)),
            dma((8,)), dma((8,)),
            dma((8, 3)), dma((8, 3)),
            dma((8, 3)), dma((8, 3)),
            dma((8, 3)), dma((8, 3)),
            dma((8,)), dma((8,)),
            dma((4,)), dma((4,)),
            dma((3,)), dma((3,)),
            dma((3,)), dma((3,)),
            dma((8,)), dma((8,)),
            dma((8,)), dma((8,)),
            dma((4,)), dma((4,)), dma((8,)),
            dma((3,)), dma((3,)),
            dma((3,)), dma((3,)),
            dma((8,)), dma((8,)),
            dma((5,)), dma((5,)),
            dma((MP + NFFN,)), dma((MP + NFFN,)),
        ],
        compiler_params=pltpu.CompilerParams(
            collective_id=0, has_side_effects=True, vmem_limit_bytes=VMEM_LIMIT
        ),
        name="layer",
    )(x, cot, *small, jnp.asarray(cos), jnp.asarray(sin), wshard, win, wout)


def clusters():
    groups = lax.axis_size("dp") // NFFN
    near = [[group * NFFN + expert for expert in range(NFFN)] for group in range(groups)]
    far = [[group * NFFN + expert for group in range(groups)] for expert in range(NFFN)]
    return groups, near, far


def exchange(shard, dim):
    _, near, far = clusters()
    own = lax.all_to_all(shard, "dp", 0, dim, axis_index_groups=near, tiled=True)
    return lax.all_gather(own, "dp", axis=dim, axis_index_groups=far, tiled=True)


def exchange_back(grads, dim):
    _, near, far = clusters()
    grads = lax.psum_scatter(
        grads.astype(f32), "dp", scatter_dimension=dim, axis_index_groups=far, tiled=True
    )
    return lax.all_to_all(grads.astype(bf16), "dp", dim, 0, axis_index_groups=near, tiled=True)


def per_device(
    inputs,
    query_key_value,
    output_weight,
    expert_input,
    expert_output,
    first_gain,
    second_gain,
    router_weight,
    logit_carry,
    constant_mix,
    constant_values,
    previous_logits,
    routes,
    cotangent,
):
    rows, width = inputs.shape
    groups, _, far = clusters()

    small = (
        router_weight.T,
        constant_mix.T,
        constant_values,
        second_gain[None],
        first_gain[None],
        logit_carry,
        previous_logits.T,
        routes.T,
    )
    shard_depth = query_key_value.shape[0]
    shard = jnp.concatenate(
        [query_key_value.reshape(shard_depth, -1), output_weight.T], axis=1
    )
    cols = output_weight.shape[0]
    expert_output_t = expert_output.transpose(0, 2, 1)
    if groups > 1:
        shard = lax.all_gather(shard, "dp", axis=0, tiled=True)
        win = exchange(expert_input, 2)[0]
        wout = exchange(expert_output_t, 1)[0]
    if groups == 1:
        win, wout = expert_input, expert_output_t
    output, input_grad, logits_grad, weight_grad, sums, first_grad, expert_grad = layer(
        inputs, cotangent, small, shard, win, wout, groups
    )
    if groups > 1:
        weight_grad = lax.psum_scatter(weight_grad, "dp", scatter_dimension=0, tiled=True)
        whole = expert_grad.transpose(1, 0, 2, 3).reshape(1, 3, width, -1)
        expert_grad = exchange_back(whole, 2)
        sums, first_grad = lax.psum((sums, first_grad), "dp", axis_index_groups=far)
    expert_in_grad = expert_grad[:, :2].astype(f32)
    expert_out_grad = expert_grad[:, 2].transpose(0, 2, 1).astype(f32)
    return (
        output,
        input_grad,
        logits_grad[:NEXP].T,
        weight_grad[:, : 3 * cols].reshape(shard_depth, 3, cols),
        weight_grad[:, 3 * cols :].T,
        expert_in_grad,
        expert_out_grad,
        first_grad[0],
        sums[22],
        sums[:NEXP].T,
        sums[24 : 24 + NEXP, :NEXP],
        sums[16:20].T,
        sums[20:22],
    )


def solution(mesh):
    in_specs = (
        P(("dp", "mp"), None),
        P("dp", None, "mp"),
        P("mp", "dp"),
        P(None, None, "dp", "mp"),
        P(None, "mp", "dp"),
        P(),
        P(),
        P(),
        P(),
        P(),
        P(),
        P("dp", None),
        P("dp", None),
        P(("dp", "mp"), None),
    )
    out_specs = (
        P(("dp", "mp"), None),
        P(("dp", "mp"), None),
        P(("dp", "mp"), None),
        P("dp", None, "mp"),
        P("mp", "dp"),
        P(None, None, "dp", "mp"),
        P(None, "mp", "dp"),
        P(),
        P(),
        P(),
        P(),
        P(),
        P(),
    )
    return jax.shard_map(
        per_device, mesh=mesh, in_specs=in_specs, out_specs=out_specs, check_vma=False
    )
```

```python
import functools
import numpy as np
import jax
import jax.numpy as jnp
from jax import lax
from jax.sharding import PartitionSpec as P
from jax.experimental import pallas as pl
from jax.experimental.pallas import tpu as pltpu

HD = 64
NFFN = 8
NEXP = 12
SEQ = 1024
CAP = 256
MP = 4
QUARTER = CAP // MP
WIDE = 640
VMEM_LIMIT = 63 * 2**20

epsilon = 1e-06
rope_base = 10000.0
highest = lax.Precision.HIGHEST
f32 = jnp.float32
bf16 = jnp.bfloat16
MESH = pl.DeviceIdType.MESH
VM = pl.BlockSpec(memory_space=pltpu.VMEM)
HB = pl.BlockSpec(memory_space=pl.ANY)
NT = (((1,), (1,)), ((), ()))
TN = (((0,), (0,)), ((), ()))


def flip(index, distance):
    out = index
    bit = 1
    while bit <= distance:
        if distance & bit:
            out = out + bit - 2 * bit * ((index // bit) % 2)
        bit *= 2
    return out


def dotf(a, b, dims=None):
    if dims is None:
        return jnp.dot(a, b, preferred_element_type=f32)
    return lax.dot_general(a, b, dims, preferred_element_type=f32)


def remote(src, dst, send, recv, **where):
    return pltpu.make_async_remote_copy(
        src_ref=src, dst_ref=dst, send_sem=send, recv_sem=recv, device_id=where, device_id_type=MESH
    )


def greet(mp_me, near, base):
    barrier = pltpu.get_barrier_semaphore()
    for k in range(1, MP):
        pl.semaphore_signal(barrier, inc=1, device_id={"mp": flip(mp_me, k)}, device_id_type=MESH)
    for k in range(1, NFFN):
        pl.semaphore_signal(
            barrier, inc=1, device_id={"dp": base + flip(near, k)}, device_id_type=MESH
        )
    pl.semaphore_wait(barrier, MP - 1 + NFFN - 1)


def rope_constants():
    half = HD // 2
    positions = np.arange(SEQ, dtype=np.float32)
    frequency = (rope_base ** (-np.arange(half, dtype=np.float32) / half)).astype(np.float32)
    angles = (positions[:, None] * frequency[None, :]).astype(np.float32)
    cosine, sine = np.cos(angles), np.sin(angles)
    return (
        np.concatenate([cosine, cosine], axis=1),
        np.concatenate([-sine, sine], axis=1),
    )


def swap_halves(x):
    half = HD // 2
    return jnp.concatenate([x[:, half:], x[:, :half]], axis=1)


class Gather:
    def __init__(self, ref, mp_me, send, recv):
        self.me, self.core, self.chip = mp_me, flip(mp_me, 1), flip(mp_me, 2)
        own = ref.at[mp_me]
        far = ref.at[self.chip]
        self.to_chip = remote(own, own, send.at[0], recv.at[0], mp=self.chip)
        self.to_core = remote(own, own, send.at[1], recv.at[1], mp=self.core)
        self.relay = remote(far, far, send.at[2], recv.at[2], mp=self.core)

    def start(self):
        self.to_chip.start()
        self.to_core.start()

    def forward(self):
        self.to_chip.wait_recv()
        self.relay.start()

    def finish(self):
        self.to_core.wait_recv()
        self.relay.wait_recv()
        self.to_chip.wait_send()
        self.to_core.wait_send()
        self.relay.wait_send()


def pack3(value):
    high = value.astype(bf16).astype(f32)
    rest = value - high
    mid = rest.astype(bf16).astype(f32)
    low = (rest - mid).astype(bf16).astype(f32)
    lane = lax.broadcasted_iota(jnp.int32, (value.shape[0], 128), 1)
    return jnp.where(
        lane == 0, high, jnp.where(lane == 1, mid, jnp.where(lane == 2, low, 0.0))
    ).astype(bf16)


def unpack3(parts):
    return jnp.sum(parts.astype(f32), axis=-1, keepdims=True)


def exact(left, right, dims=None):
    high = left.astype(bf16)
    rest = left - high.astype(f32)
    mid = rest.astype(bf16)
    low = (rest - mid.astype(f32)).astype(bf16)
    return dotf(high, right, dims) + (dotf(mid, right, dims) + dotf(low, right, dims))


class Scatter:
    def __init__(self, mp_me, core_out, core_in, chip_out, chip_in, send, recv):
        self.me, self.core, self.chip = mp_me, flip(mp_me, 1), flip(mp_me, 2)
        self.core_out, self.core_in = core_out, core_in
        self.chip_out, self.chip_in = chip_out, chip_in
        self.to_core = [
            remote(core_out.at[j], core_in.at[j], send.at[j], recv.at[j], mp=self.core)
            for j in range(2)
        ]
        self.to_chip = remote(chip_out, chip_in, send.at[2], recv.at[2], mp=self.chip)

    def run(self, blocks):
        for j, block in enumerate((flip(self.me, 3), self.core)):
            self.core_out[j] = blocks(block).astype(bf16)
            self.to_core[j].start()
        term = blocks(self.chip)
        self.to_core[0].wait_recv()
        self.chip_out[...] = (term + self.core_in[0].astype(f32)).astype(bf16)
        self.to_chip.start()
        term = blocks(self.me)
        self.to_core[1].wait_recv()
        term = term + self.core_in[1].astype(f32)
        self.to_chip.wait_recv()
        return term + self.chip_in[...].astype(f32)

    def drain(self):
        for copy in self.to_core + [self.to_chip]:
            copy.wait_send()


def layer_kernel(
    inside,
    x_ref, cot_ref, router_ref, mix_ref, values_ref, gains_ref, carry_ref, previous_ref,
    routes_ref, cos_ref, sin_ref, wshard_ref, win_shard, wout_shard,
    output_ref, xgrad_ref, lgrad_ref, wgrad_ref, sums_ref, first_ref, dw_own,
    rows1_ref, w_ref, q_ref, k_ref, v_ref, mixed_ref, lse_ref, pick_ref, gate_ref, outp_ref, dw_ref,
    rows2_ref, hidden_ref, sum_ref, core_in, chip_out, chip_in, core_out,
    place_ref, gates_ref, prior_ref, msgx, msgc, xs, cs, units_ref, pgrad_ref,
    part_ref, keep_ref, gcore_out, gcore_in, gchip_out, gchip_in, gret, score_out, score_in,
    ncore_in, nchip_in,
    key_acc, value_acc, grads_ref, across_out, across_in, along_in, ret_ref,
    pcore_in, pchip_in, params_ref, routing_ref,
    sum_out, sum_in, first_mp, first_dp, first_out,
    sends, recvs, wsend, wrecv, esend, erecv, local,
    csend, crecv, xsend, xrecv, dsend, drecv, xgs, xgr, cgs, cgr, gsend, grecv,
    rsend, rrecv, ssend, srecv, nsend, nrecv,
    asend, arecv, osend, orecv, msend, mrecv, psend, precv, mlocal, bsend, brecv, tsend, trecv,
    vsend, vrecv, zsend, zrecv, fsend, frecv,
):
    cot_all = rows2_ref
    residual_ref = sum_ref
    hgrad_ref = xgrad_ref
    small_ref = sum_out.at[0]
    mp_me = lax.axis_index("mp")
    dp_me = lax.axis_index("dp")
    near = lax.rem(dp_me, NFFN)
    base = dp_me - near
    core, chip, far = flip(mp_me, 1), flip(mp_me, 2), flip(mp_me, 3)
    rows, width = x_ref.shape
    everyone = MP * rows
    greet(mp_me, near, base)

    params_ref[...] = jnp.zeros_like(params_ref)
    params_ref[0:NEXP] = router_ref[...].astype(f32)
    params_ref[16:20] = mix_ref[...].astype(f32)
    params_ref[20:22] = values_ref[...].astype(f32)
    params_ref[22:24] = gains_ref[...].astype(f32)
    params_ref[24 : 24 + NEXP, 0:NEXP] = carry_ref[...]
    routing_ref[...] = jnp.zeros_like(routing_ref)
    routing_ref[0:NEXP] = previous_ref[...]
    routing_ref[16:18] = routes_ref[...].astype(f32)

    tokens = x_ref[...].astype(f32)
    scale = lax.rsqrt(jnp.mean(tokens * tokens, axis=-1, keepdims=True) + epsilon)
    rows1_ref[mp_me] = (tokens * scale * params_ref[23:24]).astype(bf16)
    gather1 = Gather(rows1_ref, mp_me, sends.at[pl.ds(0, 3)], recvs.at[pl.ds(0, 3)])
    gather1.start()
    if inside:
        w_ref[near] = wshard_ref[...]
        own = w_ref.at[near]
        along = [
            remote(own, own, wsend.at[k], wrecv.at[k], dp=base + flip(near, k)) for k in (2, 4, 6)
        ]
        for copy in along:
            copy.start()
        mate = base + flip(near, 1)
        across = [remote(own, own, wsend.at[0], wrecv.at[0], dp=mate)]
        across[0].start()
    cot_all[mp_me] = cot_ref[...]
    cot_gather = Gather(cot_all, mp_me, csend, crecv)
    cot_gather.start()

    ids = lax.broadcasted_iota(jnp.int32, (16, everyone), 0).astype(f32)
    chosen = (ids == routing_ref[16:17]) | (ids == routing_ref[17:18])
    earlier = lax.broadcasted_iota(jnp.int32, (everyone, everyone), 0) < lax.broadcasted_iota(
        jnp.int32, (everyone, everyone), 1
    )
    counts = dotf(
        jnp.where(chosen, 1.0, 0.0).astype(bf16), jnp.where(earlier, 1.0, 0.0).astype(bf16)
    )
    place_ref[...] = jnp.where(chosen, counts, -1.0)
    wanted = (lax.broadcasted_iota(jnp.int32, (QUARTER, everyone), 0) + QUARTER * mp_me).astype(f32)

    def target(k):
        return lax.rem(near + k, NFFN)

    def choose(k, carried):
        pick = wanted == place_ref[pl.ds(target(k), 1)]
        pick_ref[k] = jnp.where(pick, 1.0, 0.0).astype(bf16)
        return carried

    lax.fori_loop(0, NFFN, choose, 0)
    carry = params_ref[24:40, 0:16]
    prior_ref[...] = lax.dot_general(
        carry, routing_ref[0:16], TN, preferred_element_type=f32, precision=highest
    )

    if inside:
        for k, copy in zip((2, 4, 6), along):
            copy.wait_recv()
            block = w_ref.at[flip(near, k)]
            onward = remote(block, block, wsend.at[k + 1], wrecv.at[k + 1], dp=mate)
            onward.start()
            across.append(onward)
        gather1.forward()
        for copy in across:
            copy.wait_recv()
        for copy in along + across:
            copy.wait_send()
        weights = []
        din = win_shard.shape[2]
        place = pl.ds(pl.multiple_of(near * din, din), din)
        for k in (4, 2, 6, 5, 7, 3, 1):
            peer = flip(near, k)
            for i, (src, dst) in enumerate([
                (win_shard.at[peer], dw_ref.at[0:2, place]),
                (wout_shard.at[peer], dw_ref.at[2, place]),
            ]):
                weights.append(
                    remote(src, dst, esend.at[i, k], erecv.at[i, k], dp=base + peer)
                )
        first = 4
        for copy in weights[:first]:
            copy.start()
        mine = [
            pltpu.make_async_copy(win_shard.at[near], dw_ref.at[0:2, place], local.at[0]),
            pltpu.make_async_copy(wout_shard.at[near], dw_ref.at[2, place], local.at[1]),
        ]
        for copy in mine:
            copy.start()
    else:
        w_ref[...] = wshard_ref[...]
        mine = [
            pltpu.make_async_copy(win_shard, dw_ref.at[0:2], local.at[0]),
            pltpu.make_async_copy(wout_shard, dw_ref.at[2], local.at[1]),
        ]
        for copy in mine:
            copy.start()
        gather1.forward()
    gather1.finish()

    cot_gather.forward()
    cot_gather.finish()

    def c_copy(k):
        return remote(
            msgc.at[k], cs.at[k, mp_me], dsend.at[k], drecv.at[k], dp=base + target(k)
        )

    def send(picked, ref, copy, lanes):
        def half(i, carried):
            start = 4 - 4 * i
            blocks = dotf(pick_ref[pl.ds(start, 4)].reshape(4 * QUARTER, everyone), picked())
            ref[(pl.ds(start, 4),) + lanes] = blocks.astype(bf16).reshape(4, QUARTER, width)

            def go(k, inner):
                @pl.when(k > 0)
                def _():
                    copy(k).start()

                return inner

            return lax.fori_loop(start, start + 4, go, carried)

        lax.fori_loop(0, 2, half, 0)

    send(lambda: cot_all[...].reshape(everyone, width), msgc, c_copy, ())
    cs[0, mp_me] = msgc[0]
    if inside:
        for copy in weights[first:]:
            copy.start()

    w_all = w_ref[...].reshape(width, w_ref.shape[2])
    heads = q_ref.shape[0]
    cols = heads * HD

    def project(i, carry):
        at = pl.ds(pl.multiple_of(i * rows, rows), rows)
        joint = dotf(rows1_ref[i], w_all[:, : 3 * cols])
        cosine, sine = cos_ref[at], sin_ref[at]
        for h in range(heads):
            query = joint[:, h * HD : (h + 1) * HD]
            key = joint[:, cols + h * HD : cols + (h + 1) * HD]
            q_ref[h, at] = (query * cosine + swap_halves(query) * sine).astype(bf16)
            k_ref[h, at] = (key * cosine + swap_halves(key) * sine).astype(bf16)
            v_ref[h, at] = joint[:, 2 * cols + h * HD : 2 * cols + (h + 1) * HD].astype(bf16)
        return carry

    lax.fori_loop(0, MP, project, 0)
    out_weight = w_all[:, 3 * cols :]

    to_core = [
        remote(core_out.at[j], core_in.at[j], sends.at[3 + j], recvs.at[3 + j], mp=core)
        for j in range(2)
    ]
    to_chip = remote(chip_out, chip_in, sends.at[5], recvs.at[5], mp=chip)

    def attend(step, carry):
        block = flip(mp_me, 3)
        block = jnp.where(step == 1, core, jnp.where(step == 2, chip, jnp.where(step == 3, mp_me, block)))
        at = pl.ds(pl.multiple_of(block * rows, rows), rows)
        row_ids = block * rows + lax.broadcasted_iota(jnp.int32, (rows, SEQ), 0)
        seen = row_ids >= lax.broadcasted_iota(jnp.int32, (rows, SEQ), 1)
        for h in range(heads):
            scores = dotf(q_ref[h, at], k_ref[h], NT) * HD**-0.5
            scores = jnp.where(seen, scores, -jnp.inf)
            peak = jnp.max(scores, axis=-1, keepdims=True)
            exponent = jnp.exp(scores - peak)
            total = jnp.sum(exponent, axis=-1, keepdims=True)
            probs = (exponent * (1.0 / total)).astype(bf16)
            mixed_ref[at, h * HD : (h + 1) * HD] = dotf(probs, v_ref[h]).astype(bf16)
            lse_ref[at, h : h + 1] = peak + jnp.log(total)
        part = dotf(mixed_ref[at], out_weight, NT)

        @pl.when(step == 0)
        def _():
            core_out[0] = part.astype(bf16)
            to_core[0].start()

        @pl.when(step == 1)
        def _():
            core_out[1] = part.astype(bf16)
            to_core[1].start()

        @pl.when(step == 2)
        def _():
            to_core[0].wait_recv()
            chip_out[...] = (part + core_in[0].astype(f32)).astype(bf16)
            to_chip.start()

        @pl.when(step == 3)
        def _():
            sum_ref[...] = part

        return carry

    lax.fori_loop(0, MP, attend, 0)
    to_core[1].wait_recv()
    partial = sum_ref[...] + core_in[1].astype(f32)
    to_chip.wait_recv()
    hidden = x_ref[...].astype(f32) + (partial + chip_in[...].astype(f32))
    hidden_ref[...] = hidden
    scale2 = lax.rsqrt(jnp.mean(hidden * hidden, axis=-1, keepdims=True) + epsilon)
    rows2_ref[mp_me] = (hidden * scale2 * params_ref[22:23]).astype(bf16)
    gather2 = Gather(rows2_ref, mp_me, sends.at[pl.ds(6, 3)], recvs.at[pl.ds(6, 3)])
    gather2.start()
    for copy in to_core + [to_chip]:
        copy.wait_send()
    gather2.forward()

    def turn(i):
        return lax.rem(i + 4, NFFN)

    def c_gather(k):
        return Gather(cs.at[k], mp_me, cgs.at[k], cgr.at[k])

    def at_step(i, first, body):
        @pl.when((i >= first) & (i < NFFN + first))
        def _():
            body(turn(i - first))

    def cot_step(i, carried):
        def arrived(k):
            @pl.when(k > 0)
            def _():
                c_copy(k).wait_recv()

            c_gather(k).start()

        at_step(i, 0, arrived)
        at_step(i, 1, lambda k: c_gather(k).forward())
        return carried

    lax.fori_loop(0, NFFN + 1, cot_step, 0)
    gather2.finish()

    router = params_ref[0:16].astype(bf16)
    mix = params_ref[16:20].astype(bf16)
    tokens = rows2_ref[...].reshape(everyone, width)
    logits = dotf(router, tokens, NT) + prior_ref[...]
    masked = jnp.where(place_ref[...] >= 0.0, logits, -jnp.inf)
    exponent = jnp.exp(masked - jnp.max(masked, axis=0, keepdims=True))
    gates_ref[...] = exponent / jnp.sum(exponent, axis=0, keepdims=True)

    def weigh(k, carried):
        gate = jnp.sum(
            pick_ref[k].astype(f32) * gates_ref[pl.ds(target(k), 1)], axis=1, keepdims=True
        )
        gate_ref[k] = jnp.broadcast_to(gate, (QUARTER, 128))
        msgx[k, :, width:] = pack3(gate)
        return carried

    lax.fori_loop(0, NFFN, weigh, 0)

    def x_copy(k):
        return remote(
            msgx.at[k], xs.at[k, mp_me], xsend.at[k], xrecv.at[k], dp=base + target(k)
        )

    send(
        lambda: rows2_ref[...].reshape(everyone, width), msgx, x_copy,
        (slice(None), slice(0, width)),
    )
    xs[0, mp_me] = msgx[0]

    def x_gather(k):
        return Gather(xs.at[k], mp_me, xgs.at[k], xgr.at[k])

    def slots_of(k):
        return pl.ds(pl.multiple_of(k * CAP, CAP), CAP)

    def x_step(i, carried):
        def arrived(k):
            @pl.when(k > 0)
            def _():
                x_copy(k).wait_recv()

            x_gather(k).start()

        def passed(k):
            x_gather(k).forward()

        at_step(i, 0, arrived)
        at_step(i, 1, passed)
        return carried

    lax.fori_loop(0, NFFN + 1, x_step, 0)
    if inside:
        for copy in weights:
            copy.wait_recv()
    for copy in mine:
        copy.wait()

    def r_trip(k):
        slot = lax.rem(k, 4)
        return Scatter(
            mp_me, gcore_out.at[slot], gcore_in.at[k], gchip_out.at[slot], gchip_in.at[k],
            gsend.at[k], grecv.at[k],
        )

    def g_copy(k):
        return remote(
            msgx.at[k], gret.at[k], rsend.at[k], rrecv.at[k],
            dp=base + lax.rem(near - k + NFFN, NFFN),
        )

    def seal(ref, index, total):
        ref[index + (slice(None), slice(0, width))] = total[:, :width].astype(bf16)
        ref[index + (slice(None), slice(width, None))] = pack3(unpack3(total[:, width:]))

    def expert_step(i, carried):
        def compute(k):
            c_gather(k).finish()
            x_gather(k).finish()
            x = xs[k].reshape(CAP, width + 128)[:, :width]
            gate = unpack3(xs[k].reshape(CAP, width + 128)[:, width:])
            c = cs[k].reshape(CAP, width)
            gate_pre = dotf(x, dw_ref[0])
            up_pre = dotf(x, dw_ref[1])
            sig = jax.nn.sigmoid(gate_pre)
            units = (gate_pre * sig * up_pre).astype(bf16)
            units_ref[slots_of(k)] = units
            outp_ref[k] = dotf(units, dw_ref[2], NT).astype(bf16).reshape(MP, QUARTER, width)
            raw = dotf(c, dw_ref[2])
            score = jnp.sum(units.astype(f32) * raw, axis=1, keepdims=True)
            units_grad = raw * gate
            gate_grad = (units_grad * up_pre * sig * (1.0 + gate_pre * (1.0 - sig))).astype(bf16)
            up_grad = (units_grad * (gate_pre * sig)).astype(bf16)
            pgrad_ref[0, slots_of(k)] = gate_grad
            pgrad_ref[1, slots_of(k)] = up_grad
            back = dotf(gate_grad, dw_ref[0], NT) + dotf(up_grad, dw_ref[1], NT)
            cs[k] = (c.astype(f32) * gate).astype(bf16).reshape(MP, QUARTER, width)
            part_ref[:, :, :width] = back.reshape(MP, QUARTER, width)
            part_ref[:, :, width:] = pack3(score).astype(f32).reshape(MP, QUARTER, 128)
            slot = lax.rem(k, 4)
            gcore_out[slot, 0] = part_ref[far].astype(bf16)
            gcore_out[slot, 1] = part_ref[core].astype(bf16)
            keep_ref[slot, 0] = part_ref[chip]
            keep_ref[slot, 1] = part_ref[mp_me]
            for copy in r_trip(k).to_core:
                copy.start()

        def across(k):
            trip = r_trip(k)
            trip.to_core[0].wait_recv()
            seal(gchip_out, (lax.rem(k, 4),), keep_ref[lax.rem(k, 4), 0] + gcore_in[k, 0].astype(f32))
            trip.to_chip.start()

        def away(k):
            trip = r_trip(k)
            trip.to_core[1].wait_recv()
            trip.to_chip.wait_recv()
            total = (
                keep_ref[lax.rem(k, 4), 1]
                + gcore_in[k, 1].astype(f32)
                + gchip_in[k].astype(f32)
            )
            trip.drain()

            @pl.when(k > 0)
            def _():
                x_copy(k).wait_send()

            seal(msgx, (k,), total)

            @pl.when(k > 0)
            def _():
                g_copy(k).start()

            @pl.when(k == 0)
            def _():
                gret[0] = msgx[0]

        at_step(i, 4, away)
        at_step(i, 0, compute)
        at_step(i, 2, across)
        return carried

    lax.fori_loop(0, NFFN + 4, expert_step, 0)

    p_core = [
        remote(outp_ref.at[:, far], pcore_in.at[0], psend.at[0], precv.at[0], mp=core),
        remote(outp_ref.at[:, core], pcore_in.at[1], psend.at[1], precv.at[1], mp=core),
    ]
    for copy in p_core:
        copy.start()
    parts = (slice(4, 8), slice(0, 4))
    p_chip = [
        remote(cs.at[part, 3], pchip_in.at[part], psend.at[2 + j], precv.at[2 + j], mp=chip)
        for j, part in enumerate(parts)
    ]
    returns = {
        k: remote(msgc.at[k], ret_ref.at[k], osend.at[k], orecv.at[k],
                  dp=base + lax.rem(near - k + NFFN, NFFN))
        for k in range(1, NFFN)
    }

    def results_across():
        p_core[0].wait_recv()
        for j, part in enumerate(parts):
            cs[part, 3] = (
                outp_ref[part, chip].astype(f32) + pcore_in[0, part].astype(f32)
            ).astype(bf16)
            p_chip[j].start()

    def results_away(j):
        part = parts[j]
        if j == 0:
            p_core[1].wait_recv()
        p_chip[j].wait_recv()
        msgc[part] = (
            outp_ref[part, mp_me].astype(f32)
            + (pcore_in[1, part].astype(f32) + pchip_in[part].astype(f32))
        ).astype(bf16)
        for k in range(part.start, part.stop):
            if k > 0:
                returns[k].start()
            else:
                ret_ref[0] = msgc[0]

    def weights_step(j, carried):
        at = pl.ds(pl.multiple_of(j * 128, 128), 128)
        x = xs[:, :, :, at].reshape(NFFN * CAP, 128)
        c = cs[:, :, :, at].reshape(NFFN * CAP, 128)
        dw_ref[0, at] = dotf(x, pgrad_ref[0], TN).astype(bf16)
        dw_ref[1, at] = dotf(x, pgrad_ref[1], TN).astype(bf16)
        dw_ref[2, at] = dotf(c, units_ref[...], TN).astype(bf16)
        return carried

    lax.fori_loop(0, width // 128, weights_step, 0)

    din = dw_own.shape[2]

    def rows_of(index):
        return pl.ds(pl.multiple_of(index * din, din), din)

    if inside:
        moved = [
            remote(dw_ref.at[:, rows_of(flip(near, k))], dw_own.at[near], msend.at[k],
                   mrecv.at[k], dp=base + flip(near, k))
            for k in (4, 6, 5, 7, 2, 3, 1)
        ]
        kept = [pltpu.make_async_copy(dw_ref.at[:, rows_of(near)], dw_own.at[near], mlocal.at[0])]
    else:
        moved = []
        kept = [
            pltpu.make_async_copy(dw_ref.at[:, rows_of(p)], dw_own.at[p], mlocal.at[p])
            for p in range(NFFN)
        ]
    early = 7
    for copy in moved[:early] + kept:
        copy.start()
    results_across()

    n_bf = rows2_ref[mp_me]
    n = n_bf.astype(f32)
    cot = cot_ref[...].astype(f32)
    hidden = hidden_ref[...]
    lane = lax.broadcasted_iota(jnp.int32, (rows, 128), 1)
    own_at = pl.ds(pl.multiple_of(mp_me * rows, rows), rows)
    gates_t = gates_ref[:, own_at]
    own_gates = jnp.concatenate([gates_t, jnp.zeros((112, rows), f32)], axis=0).T
    copy_gate = own_gates[:, NFFN + 1 : NFFN + 2]
    const_gates = [own_gates[:, NFFN + 2 : NFFN + 3], own_gates[:, NFFN + 3 : NFFN + 4]]
    mix_logits = dotf(n_bf, mix, NT)
    with_normed = jnp.sum(cot * n, axis=1, keepdims=True)
    residual = hidden + copy_gate * n
    local_grad = copy_gate * cot
    local_scores = jnp.where(lane == NFFN + 1, with_normed, 0.0)
    mix_grads = jnp.zeros((rows, 128), f32)
    for c in range(2):
        first, second = mix_logits[:, 2 * c : 2 * c + 1], mix_logits[:, 2 * c + 1 : 2 * c + 2]
        top = jnp.maximum(first, second)
        first, second = jnp.exp(first - top), jnp.exp(second - top)
        share = 1.0 / (first + second)
        first, second = first * share, second * share
        constant = params_ref[20 + c : 21 + c]
        with_constant = jnp.sum(cot * constant, axis=1, keepdims=True)
        gate = const_gates[c]
        residual = residual + gate * (first * n + second * constant)
        local_scores = jnp.where(
            lane == NFFN + 2 + c, first * with_normed + second * with_constant, local_scores
        )
        local_grad = local_grad + (first * gate) * cot
        small_ref[20 + c : 21 + c] = jnp.sum((second * gate) * cot, axis=0, keepdims=True)
        grad_first, grad_second = gate * with_normed, gate * with_constant
        mean = first * grad_first + second * grad_second
        mix_grads = jnp.where(lane == 2 * c, first * (grad_first - mean), mix_grads)
        mix_grads = jnp.where(lane == 2 * c + 1, second * (grad_second - mean), mix_grads)
    residual_ref[...] = residual

    def returned(k, carried):
        g_copy(k).wait_recv()
        return carried

    lax.fori_loop(1, NFFN, returned, 0)
    ret = gret[...].reshape(NFFN * QUARTER, width + 128)
    score_out[...] = jnp.zeros_like(score_out)

    def give_scores(k, carried):
        slots = unpack3(gret[k, :, width:])
        row = jnp.sum(pick_ref[k].astype(f32) * slots, axis=0, keepdims=True)
        for q in range(MP):
            score_out[q, pl.ds(target(k), 1)] = row[:, q * rows : (q + 1) * rows]
        return carried

    lax.fori_loop(0, NFFN, give_scores, 0)
    score_copies = [
        remote(score_out.at[flip(mp_me, k)], score_in.at[k], ssend.at[k], srecv.at[k], mp=flip(mp_me, k))
        for k in range(1, MP)
    ]
    for copy in score_copies:
        copy.start()

    def grad_block(q):
        at = pl.ds(pl.multiple_of(q * rows, rows), rows)
        return dotf(
            pick_ref[:, :, at].reshape(NFFN * QUARTER, rows), ret[:, :width], TN
        )

    trip = Scatter(mp_me, core_out, ncore_in, chip_out, nchip_in, nsend, nrecv)
    normed_grad = trip.run(grad_block) + local_grad
    lax.fori_loop(1, NFFN, lambda k, carried: (c_copy(k).wait_send(), carried)[1], 0)
    results_away(0)
    results_away(1)
    for copy in moved[early:]:
        copy.start()

    for copy in score_copies:
        copy.wait_recv()
    ffn_scores = (score_out[mp_me] + score_in[1]) + (score_in[2] + score_in[3])
    scores = local_scores.T[:16] + jnp.concatenate([ffn_scores, jnp.zeros((8, rows), f32)], axis=0)
    logit_grad = gates_t * (scores - jnp.sum(gates_t * scores, axis=0, keepdims=True))
    lgrad_ref[...] = lax.dot_general(
        carry, logit_grad, (((1,), (0,)), ((), ())),
        preferred_element_type=f32, precision=highest,
    )
    small_ref[24:40] = jnp.zeros((16, width), f32)
    small_ref[24:40, 0:16] = lax.dot_general(
        routing_ref[0:16, own_at], logit_grad, NT, preferred_element_type=f32, precision=highest
    )
    stacked = jnp.concatenate([logit_grad, mix_grads.T[:16]], axis=0)
    stack = params_ref[0:32]
    sublane = lax.broadcasted_iota(jnp.int32, (32, width), 0)
    stack = jnp.where(sublane < 20, stack, 0.0).astype(bf16)
    feature_grads = exact(stacked, n_bf)
    small_ref[0:20] = feature_grads[0:20]
    normed_grad = normed_grad + exact(stacked, stack, TN)
    scale = lax.rsqrt(jnp.mean(hidden * hidden, axis=-1, keepdims=True) + epsilon)
    scaled = hidden * scale
    small_ref[22:23] = jnp.sum(normed_grad * scaled, axis=0, keepdims=True)
    small_ref[23:24] = jnp.zeros((1, width), f32)
    weighted = normed_grad * params_ref[22:23]
    hidden_grad = cot + scale * (
        weighted - scaled * jnp.mean(weighted * scaled, axis=-1, keepdims=True)
    )
    hgrad_ref[...] = hidden_grad
    rows2_ref[mp_me] = hidden_grad.astype(bf16)
    agather = Gather(rows2_ref, mp_me, asend, arecv)
    agather.start()

    trip.drain()
    for copy in score_copies:
        copy.wait_send()

    def drain(k, carried):
        g_copy(k).wait_send()
        return carried

    lax.fori_loop(1, NFFN, drain, 0)
    if inside:
        for copy in weights:
            copy.wait_send()

    places = [{"mp": flip(mp_me, 1)}, {"mp": flip(mp_me, 2)}] + [
        {"dp": base + flip(near, k)} for k in (1, 2, 4)
    ]
    stages = [
        remote(sum_out.at[j], sum_in.at[j], zsend.at[j], zrecv.at[j], **where)
        for j, where in enumerate(places)
    ]

    def stage(j):
        if j > 0:
            stages[j - 1].wait_recv()
            total = sum_out[j - 1] + sum_in[j - 1]
            if j == len(stages):
                sums_ref[...] = total
                return
            sum_out[j] = total
        stages[j].start()

    stage(0)
    agather.forward()
    stage(1)
    agather.finish()

    w_all = w_ref[...].reshape(width, w_ref.shape[2])
    out_weight = w_all[:, 3 * cols :]
    for i in range(MP):
        xs[i, :, :, WIDE : WIDE + cols] = (
            dotf(rows2_ref[i], out_weight).astype(bf16).reshape(MP, QUARTER, cols)
        )
    grads_ref[:, 3 * cols :] = dotf(rows2_ref[...].reshape(everyone, width), mixed_ref[...], TN).astype(bf16)

    combine = Scatter(mp_me, core_out, ncore_in, chip_out, nchip_in, bsend, brecv)

    def out_block(q):
        at = pl.ds(pl.multiple_of(q * rows, rows), rows)
        weighted = (ret_ref[...].astype(f32) * gate_ref[:, :, 0:1]).astype(bf16)
        return dotf(
            pick_ref[:, :, at].reshape(NFFN * QUARTER, rows),
            weighted.reshape(NFFN * QUARTER, width), TN,
        )

    def head_back(h):
        lanes = slice(h * HD, (h + 1) * HD)
        for b in range(MP):
            at = slice(b * rows, (b + 1) * rows)
            seen = (b + 1) * rows
            query = q_ref[h, at]
            keys = k_ref[h, :seen]
            out_grad = xs[b, :, :, WIDE + h * HD : WIDE + (h + 1) * HD].reshape(rows, HD)
            scores = dotf(query, keys, NT) * HD**-0.5
            allowed = b * rows + lax.broadcasted_iota(
                jnp.int32, (rows, seen), 0
            ) >= lax.broadcasted_iota(jnp.int32, (rows, seen), 1)
            probs = jnp.where(allowed, jnp.exp(scores - lse_ref[at, h : h + 1]), 0.0)
            probs_grad = dotf(out_grad, v_ref[h, :seen], NT)
            inner = jnp.sum(probs * probs_grad, axis=1, keepdims=True)
            score_grad = (probs * (probs_grad - inner)).astype(bf16)
            query_grad = dotf(score_grad, keys) * HD**-0.5
            xs[b, :, :, lanes] = (
                (query_grad * cos_ref[at] - swap_halves(query_grad) * sin_ref[at])
                .astype(bf16)
                .reshape(MP, QUARTER, HD)
            )
            key_grad = dotf(score_grad, query, TN) * HD**-0.5
            value_grad = dotf(probs.astype(bf16), out_grad, TN)
            if b == 0:
                key_acc[...] = jnp.zeros_like(key_acc)
                value_acc[...] = jnp.zeros_like(value_acc)
            key_acc[:seen] += key_grad
            value_acc[:seen] += value_grad
        key_grad = key_acc[...]
        key_grad = key_grad * cos_ref[...] - swap_halves(key_grad) * sin_ref[...]
        xs[0:MP, :, :, cols + h * HD : cols + (h + 1) * HD] = key_grad.astype(bf16).reshape(
            MP, MP, QUARTER, HD
        )
        xs[0:MP, :, :, 2 * cols + h * HD : 2 * cols + (h + 1) * HD] = (
            value_acc[...].astype(bf16).reshape(MP, MP, QUARTER, HD)
        )

    last = heads - 1
    for h in range(heads):
        head_back(h)
        if h == 0:
            stage(2)
        if h == last:
            stage(3)

    depth = width // NFFN
    grads_ref[:, : 3 * cols] = dotf(
        rows1_ref[...].reshape(everyone, width),
        xs[0:MP, :, :, 0 : 3 * cols].reshape(everyone, 3 * cols), TN,
    ).astype(bf16)
    if inside:
        lean = lax.rem(near, 2)
        tall = grads_ref[...].reshape(NFFN // 2, 2, depth, grads_ref.shape[1])
        across_out[...] = jnp.where(lean == 0, tall[:, 1], tall[:, 0])
        kept_half = jnp.where(lean == 0, tall[:, 0], tall[:, 1])
        over = remote(across_out, across_in, vsend.at[0], vrecv.at[0], dp=base + flip(near, 1))
        over.start()
    else:
        wgrad_ref[...] = grads_ref[...].astype(f32)
    stage(4)

    home = Scatter(mp_me, core_out, core_in, chip_out, chip_in, tsend, trecv)

    def x_block(q):
        joint = xs[q, :, :, 0 : 3 * cols].reshape(rows, 3 * cols)
        return dotf(joint, w_all[:, : 3 * cols], NT)

    normed_grad = home.run(x_block)
    home.drain()
    if inside:
        over.wait_recv()
        over.wait_send()
        across_out[...] = (kept_half.astype(f32) + across_in[...].astype(f32)).astype(bf16)
        up = near // 2
        alongs = [
            remote(across_out.at[flip(near, k) // 2], along_in.at[k // 2], vsend.at[k], vrecv.at[k],
                   dp=base + flip(near, k))
            for k in (4, 6, 2)
        ]
        for copy in alongs:
            copy.start()
    tokens = x_ref[...].astype(f32)
    scale = lax.rsqrt(jnp.mean(tokens * tokens, axis=-1, keepdims=True) + epsilon)
    scaled = tokens * scale
    first_out[0] = jnp.sum(normed_grad * scaled, axis=0, keepdims=True)
    firsts = [
        remote(first_out.at[0], first_mp.at[k], fsend.at[k], frecv.at[k], mp=flip(mp_me, k))
        for k in range(1, MP)
    ]
    for copy in firsts:
        copy.start()
    weighted = normed_grad * params_ref[23:24]
    xgrad_ref[...] = hgrad_ref[...] + scale * (
        weighted - scaled * jnp.mean(weighted * scaled, axis=-1, keepdims=True)
    )
    for copy in firsts:
        copy.wait_recv()
    first_out[1] = first_out[0] + first_mp[1] + first_mp[2] + first_mp[3]
    seconds = [
        remote(first_out.at[1], first_dp.at[k], fsend.at[MP + k], frecv.at[MP + k],
               dp=base + flip(near, k))
        for k in range(1, NFFN)
    ]
    for copy in seconds:
        copy.start()
    stage(5)
    for copy in returns.values():
        copy.wait_recv()
    routed = combine.run(out_block)
    output_ref[...] = (residual_ref[...] + routed).astype(bf16)
    if inside:
        for copy in alongs:
            copy.wait_recv()
        wgrad_ref[...] = across_out[up].astype(f32) + (
            along_in[1].astype(f32) + along_in[2].astype(f32) + along_in[3].astype(f32)
        )
    for copy in seconds:
        copy.wait_recv()
    total = first_out[1]
    for k in range(1, NFFN):
        total = total + first_dp[k]
    first_ref[...] = total

    for copy in moved:
        copy.wait_recv()
    for copy in kept:
        copy.wait()
    if inside:
        for copy in alongs:
            copy.wait_send()
    for copy in moved + p_core + p_chip + list(returns.values()) + stages + firsts + seconds:
        copy.wait_send()
    combine.drain()


def layer(x, cot, small, wshard, win, wout, groups):
    rows, width = x.shape
    cos, sin = rope_constants()
    inside = groups == 1
    cols = wshard.shape[-1]
    depth = width // NFFN
    hidden_cols = win.shape[-1]
    heads = cols // 4 // HD
    everyone = MP * rows
    slots = NFFN * CAP
    wide = width + 128
    sd = jax.ShapeDtypeStruct
    vm = pltpu.VMEM
    dma = pltpu.SemaphoreType.DMA
    outs = [
        sd((rows, width), bf16),
        sd((rows, width), f32),
        sd((16, rows), f32),
        sd((depth if inside else width, cols), f32),
        sd((40, width), f32),
        sd((1, width), f32),
        sd((NFFN, 3, depth, hidden_cols), bf16),
    ]
    if not inside:
        wshard = wshard.reshape(NFFN, depth, cols)
    return pl.pallas_call(
        functools.partial(layer_kernel, inside),
        out_shape=outs,
        in_specs=[VM] * 12 + [HB, HB],
        out_specs=[VM] * 6 + [HB],
        scratch_shapes=[
            vm((MP, rows, width), bf16),
            vm((NFFN, depth, cols), bf16),
            vm((heads, SEQ, HD), bf16),
            vm((heads, SEQ, HD), bf16),
            vm((heads, SEQ, HD), bf16),
            vm((SEQ, heads * HD), bf16),
            vm((SEQ, 128), f32),
            vm((NFFN, QUARTER, everyone), bf16),
            vm((NFFN, QUARTER, 128), f32),
            vm((NFFN, MP, QUARTER, width), bf16),
            vm((3, width, hidden_cols), bf16),
            vm((MP, rows, width), bf16),
            vm((rows, width), f32),
            vm((rows, width), f32),
            vm((2, rows, width), bf16),
            vm((rows, width), bf16),
            vm((rows, width), bf16),
            vm((2, rows, width), bf16),
            vm((16, everyone), f32),
            vm((16, everyone), f32),
            vm((16, everyone), f32),
            vm((NFFN, QUARTER, wide), bf16),
            vm((NFFN, QUARTER, width), bf16),
            vm((NFFN, MP, QUARTER, wide), bf16),
            vm((NFFN, MP, QUARTER, width), bf16),
            vm((slots, hidden_cols), bf16),
            vm((2, slots, hidden_cols), bf16),
            vm((MP, QUARTER, wide), f32),
            vm((4, 2, QUARTER, wide), f32),
            vm((4, 2, QUARTER, wide), bf16),
            vm((NFFN, 2, QUARTER, wide), bf16),
            vm((4, QUARTER, wide), bf16),
            vm((NFFN, QUARTER, wide), bf16),
            vm((NFFN, QUARTER, wide), bf16),
            vm((MP, 8, rows), f32),
            vm((MP, 8, rows), f32),
            vm((2, rows, width), bf16),
            vm((rows, width), bf16),
            vm((everyone, HD), f32),
            vm((everyone, HD), f32),
            vm((width, cols), bf16),
            vm((NFFN // 2, depth, cols), bf16),
            vm((NFFN // 2, depth, cols), bf16),
            vm((NFFN // 2, depth, cols), bf16),
            vm((NFFN, QUARTER, width), bf16),
            vm((2, NFFN, QUARTER, width), bf16),
            vm((NFFN, QUARTER, width), bf16),
            vm((40, width), f32),
            vm((24, everyone), f32),
            vm((5, 40, width), f32),
            vm((5, 40, width), f32),
            vm((MP, 1, width), f32),
            vm((NFFN, 1, width), f32),
            vm((2, 1, width), f32),
            dma((9,)), dma((9,)),
            dma((8,)), dma((8,)),
            dma((2, 8)), dma((2, 8)),
            dma((2,)),
            dma((3,)), dma((3,)),
            dma((8,)), dma((8,)),
            dma((8,)), dma((8,)),
            dma((8, 3)), dma((8, 3)),
            dma((8, 3)), dma((8, 3)),
            dma((8, 3)), dma((8, 3)),
            dma((8,)), dma((8,)),
            dma((4,)), dma((4,)),
            dma((3,)), dma((3,)),
            dma((3,)), dma((3,)),
            dma((8,)), dma((8,)),
            dma((8,)), dma((8,)),
            dma((4,)), dma((4,)), dma((8,)),
            dma((3,)), dma((3,)),
            dma((3,)), dma((3,)),
            dma((8,)), dma((8,)),
            dma((5,)), dma((5,)),
            dma((MP + NFFN,)), dma((MP + NFFN,)),
        ],
        compiler_params=pltpu.CompilerParams(
            collective_id=0, has_side_effects=True, vmem_limit_bytes=VMEM_LIMIT
        ),
        name="layer",
    )(x, cot, *small, jnp.asarray(cos), jnp.asarray(sin), wshard, win, wout)


def clusters():
    groups = lax.axis_size("dp") // NFFN
    near = [[group * NFFN + expert for expert in range(NFFN)] for group in range(groups)]
    far = [[group * NFFN + expert for group in range(groups)] for expert in range(NFFN)]
    return groups, near, far


def exchange(shard, dim):
    _, near, far = clusters()
    own = lax.all_to_all(shard, "dp", 0, dim, axis_index_groups=near, tiled=True)
    return lax.all_gather(own, "dp", axis=dim, axis_index_groups=far, tiled=True)


def exchange_back(grads, dim):
    _, near, far = clusters()
    grads = lax.psum_scatter(
        grads.astype(f32), "dp", scatter_dimension=dim, axis_index_groups=far, tiled=True
    )
    return lax.all_to_all(grads.astype(bf16), "dp", dim, 0, axis_index_groups=near, tiled=True)


def per_device(
    inputs,
    query_key_value,
    output_weight,
    expert_input,
    expert_output,
    first_gain,
    second_gain,
    router_weight,
    logit_carry,
    constant_mix,
    constant_values,
    previous_logits,
    routes,
    cotangent,
):
    rows, width = inputs.shape
    groups, _, far = clusters()

    small = (
        router_weight.T,
        constant_mix.T,
        constant_values,
        jnp.stack([second_gain, first_gain]),
        logit_carry,
        previous_logits.T,
        routes.T,
    )
    shard_depth = query_key_value.shape[0]
    shard = jnp.concatenate(
        [query_key_value.reshape(shard_depth, -1), output_weight.T], axis=1
    )
    cols = output_weight.shape[0]
    expert_output_t = expert_output.transpose(0, 2, 1)
    if groups > 1:
        shard = lax.all_gather(shard, "dp", axis=0, tiled=True)
        win = exchange(expert_input, 2)[0]
        wout = exchange(expert_output_t, 1)[0]
    if groups == 1:
        win, wout = expert_input, expert_output_t
    output, input_grad, logits_grad, weight_grad, sums, first_grad, expert_grad = layer(
        inputs, cotangent, small, shard, win, wout, groups
    )
    if groups > 1:
        weight_grad = lax.psum_scatter(weight_grad, "dp", scatter_dimension=0, tiled=True)
        whole = expert_grad.transpose(1, 0, 2, 3).reshape(1, 3, width, -1)
        expert_grad = exchange_back(whole, 2)
        sums, first_grad = lax.psum((sums, first_grad), "dp", axis_index_groups=far)
    expert_in_grad = expert_grad[:, :2].astype(f32)
    expert_out_grad = expert_grad[:, 2].transpose(0, 2, 1).astype(f32)
    return (
        output,
        input_grad,
        logits_grad[:NEXP].T,
        weight_grad[:, : 3 * cols].reshape(shard_depth, 3, cols),
        weight_grad[:, 3 * cols :].T,
        expert_in_grad,
        expert_out_grad,
        first_grad[0],
        sums[22],
        sums[:NEXP].T,
        sums[24 : 24 + NEXP, :NEXP],
        sums[16:20].T,
        sums[20:22],
    )


def solution(mesh):
    in_specs = (
        P(("dp", "mp"), None),
        P("dp", None, "mp"),
        P("mp", "dp"),
        P(None, None, "dp", "mp"),
        P(None, "mp", "dp"),
        P(),
        P(),
        P(),
        P(),
        P(),
        P(),
        P("dp", None),
        P("dp", None),
        P(("dp", "mp"), None),
    )
    out_specs = (
        P(("dp", "mp"), None),
        P(("dp", "mp"), None),
        P(("dp", "mp"), None),
        P("dp", None, "mp"),
        P("mp", "dp"),
        P(None, None, "dp", "mp"),
        P(None, "mp", "dp"),
        P(),
        P(),
        P(),
        P(),
        P(),
        P(),
    )
    return jax.shard_map(
        per_device, mesh=mesh, in_specs=in_specs, out_specs=out_specs, check_vma=False
    )
```
